256 devices in a mesh: gs: 128 (over z, x, y), px: 2 (over core).
Axes of the slice: x: 4, y: 4, z: 8, core: 2. Of those that a mesh axis runs over, the one named last changes fastest.
Arguments:
- features: float32 [262144, 128], P('gs'), may hold values from -6 to 6
- gauss_params: float32 [6, 262144], P(None, 'gs'), as said below
- send_index: int32 [131072], P('gs'), may hold values from 0 to 2047, as said below
- tile_ids: int32 [1024], P('gs'), may hold values from 0 to 1023, as said below
- tile_lists: int32 [1024, 512], P('gs'), may hold values from -1 to 1023, as said below
- teacher: float32 [1024, 256, 512], P('gs', 'px'), may hold values from -6 to 6
- decoder_weight: float32 [128, 512], replicated, may hold values from -0.5 to 0.5
- decoder_bias: float32 [512], replicated, may hold values from -3 to 3
Outputs:
- grad_features: float32 [262144, 128], P('gs')
- grad_params: float32 [6, 262144], P(None, 'gs')
- grad_decoder: float32 [128, 512], replicated
- grad_bias: float32 [512], replicated
- loss: float32 [], replicated
The draws below stay inside these ranges and needn't reach their ends.
Inputs may be any that keep to these rules, and one draw needn't show every extreme that they name: `send_index`: each holder's 1024 entries are distinct local Gaussian numbers; entry o * 8 + s is what that holder puts in slot s for tile owner o, so every holder sends exactly 8 Gaussians to every owner. `tile_ids`: A permutation of all tile numbers. `tile_lists`: each row holds distinct live pool entries followed only by -1; within one owner's 8 rows no pool entry appears twice, and one row of each owner is live in all 512 entries. `gauss_params`: rows 2 to 4 form a positive definite conic (a > 0, c > 0, a c > b^2); opacity lies in (0, 0.95].
All inputs are finite; a program needn't handle non-finite values.
Results may differ from the reference program's by a relative error of at most 0.0003.
Values sent between devices are 32-bit elements; how exact they have to be, the bound alone decides.
No kernel may reach another device: no remote copies, remote signals or barrier semaphores. Data moves between devices by JAX's collectives and lax.ppermute only.
A program may use at most 128 MiB of HBM per device.

```python
import math
from functools import partial
import jax
import jax.numpy as jnp
from jax import lax

C = 128
CH = 512
PIX = 256
LIST = 512
TILE_DEV = 8
POOL = 1024
CAP = 8
G_DEV = 2048
GAUSS = 262144
TILES = 1024
TILE_COLS = 128
N_GS = 128


def layout(key):
    subkeys = jax.random.split(key, 5)
    tile_order = jax.random.permutation(subkeys[0], TILES).astype(jnp.int32)
    holder_keys = jax.random.split(subkeys[1], N_GS)
    holder_perms = jax.vmap(lambda subkey: jax.random.permutation(subkey, G_DEV))(holder_keys).astype(jnp.int32)
    owner_keys = jax.random.split(subkeys[2], N_GS)
    orders = jax.vmap(lambda subkey: jax.random.permutation(subkey, POOL))(owner_keys).astype(jnp.int32)
    upper_len = (POOL - LIST) // (TILE_DEV - 1) + 1
    lengths = jax.random.randint(subkeys[3], (N_GS, TILE_DEV), LIST // 16, upper_len, dtype=jnp.int32)
    full_tile = jax.random.randint(subkeys[4], (N_GS, 1), 0, TILE_DEV, dtype=jnp.int32)
    lengths = jnp.where(jnp.arange(TILE_DEV, dtype=jnp.int32)[None, :] == full_tile, LIST, lengths)
    list_ends = jnp.cumsum(lengths, axis=1).astype(jnp.int32)
    starts = list_ends - lengths
    positions = starts[:, :, None] + jnp.arange(LIST, dtype=jnp.int32)[None, None, :]
    positions = jnp.minimum(positions, POOL - 1).reshape(N_GS, TILE_DEV * LIST)
    picked = jnp.take_along_axis(orders, positions, axis=1).reshape(N_GS, TILE_DEV, LIST)
    listed = jnp.where(jnp.arange(LIST, dtype=jnp.int32)[None, None, :] < lengths[:, :, None], picked, -1)
    return (tile_order, holder_perms, listed.reshape(TILES, LIST).astype(jnp.int32), orders, list_ends)


def draw_tile_ids(key, part):
    shared = layout(key)
    return shared[0]


def draw_send_index(key, part):
    shared = layout(key)
    return shared[1][:, :POOL].reshape(-1)


def draw_tile_lists(key, part):
    shared = layout(key)
    return shared[2]


def draw_gauss_params(key, part):
    tile_order, holder_perms, listed, orders, list_ends = layout(key)
    key = jax.random.fold_in(key, 11)
    inverse = jnp.argsort(holder_perms, axis=1).astype(jnp.int32).reshape(-1)
    holder = jnp.arange(GAUSS, dtype=jnp.int32) // G_DEV
    target = jnp.minimum(inverse // CAP, N_GS - 1)
    slot_index = inverse % CAP
    pool_entry = holder * CAP + slot_index
    order_inv = jnp.argsort(orders, axis=1).astype(jnp.int32)
    list_rank = order_inv[target, pool_entry]
    home_tile = jnp.minimum(jnp.sum((list_ends[target] <= list_rank[:, None]).astype(jnp.int32), axis=1), TILE_DEV - 1)
    list_lengths = list_ends - jnp.concatenate([jnp.zeros((N_GS, 1), jnp.int32), list_ends[:, :-1]], axis=1)
    in_full = list_lengths[target, home_tile] == LIST
    global_tile = tile_order[target * TILE_DEV + home_tile]
    anchor_x = (global_tile % TILE_COLS * 16).astype(jnp.float32)
    anchor_y = (global_tile // TILE_COLS * 16).astype(jnp.float32)
    subkeys = jax.random.split(key, 7)
    offset_x = jax.random.uniform(subkeys[0], (GAUSS,), jnp.float32, -2.0, 18.0)
    offset_y = jax.random.uniform(subkeys[1], (GAUSS,), jnp.float32, -2.0, 18.0)
    sigma_x = jnp.exp(jax.random.uniform(subkeys[2], (GAUSS,), jnp.float32, math.log(1.2), math.log(5.0)))
    sigma_y = jnp.exp(jax.random.uniform(subkeys[3], (GAUSS,), jnp.float32, math.log(1.2), math.log(5.0)))
    opacity = jax.random.uniform(subkeys[5], (GAUSS,), jnp.float32, 0.05, 0.9)
    faint = jax.random.uniform(subkeys[6], (GAUSS,), jnp.float32, 0.005, 0.05)
    opacity = jnp.where(in_full, faint, opacity)
    correlation = jax.random.uniform(subkeys[4], (GAUSS,), jnp.float32, -0.6, 0.6)
    conic_a = 1.0 / (sigma_x * sigma_x)
    conic_c = 1.0 / (sigma_y * sigma_y)
    conic_b = correlation / (sigma_x * sigma_y)
    return jnp.stack([anchor_x + offset_x, anchor_y + offset_y, conic_a, conic_b, conic_c, opacity]).astype(jnp.float32)


def shard_levels(key, shape, pieces, least, largest):
    def one(axis_at, shards_of):
        draws = jax.random.uniform(jax.random.fold_in(jax.random.fold_in(key, 6), axis_at), (shards_of,), jnp.float32, least / len(pieces), largest / len(pieces))
        return jnp.repeat(jnp.exp(draws), shape[axis_at] // shards_of).reshape((-1,) + (1,) * (len(shape) - axis_at - 1))

    gain = one(*pieces[0])
    for cut in pieces[1:]:
        gain = gain * one(*cut)
    return gain


def centred(key, shape, width, limit, cuts=(), kind=jnp.bfloat16):
    result = width * jax.random.normal(key, shape, jnp.float32)
    if cuts:
        result = result * shard_levels(key, shape, cuts, -0.22, 0.18)
    return jnp.clip(result, -limit, limit).astype(kind)


def setup_inputs(seed: int = 0) -> dict:
    arg_keys = jax.random.split(jax.random.key(seed), 9)
    features = centred(arg_keys[0], (GAUSS, C), 1.0, 6.0, ((0, 128),), jnp.float32)
    gauss_params = draw_gauss_params(jax.random.fold_in(arg_keys[8], 71), 0)
    send_index = draw_send_index(jax.random.fold_in(arg_keys[8], 71), 0)
    tile_ids = draw_tile_ids(jax.random.fold_in(arg_keys[8], 71), 0)
    tile_lists = draw_tile_lists(jax.random.fold_in(arg_keys[8], 71), 0)
    teacher = centred(arg_keys[5], (TILES, PIX, CH), 1.0, 6.0, ((0, 128), (1, 2)), jnp.float32)
    decoder_weight = centred(arg_keys[6], (C, CH), C ** -0.5, 0.5, (), jnp.float32)
    decoder_bias = centred(arg_keys[7], (CH,), 0.5, 3.0, (), jnp.float32)
    return dict(features=features, gauss_params=gauss_params, send_index=send_index, tile_ids=tile_ids, tile_lists=tile_lists, teacher=teacher, decoder_weight=decoder_weight, decoder_bias=decoder_bias)


HIGH = lax.Precision.HIGHEST

def tile_objective(gathered, prm_rows, decoder_weight, decoder_bias, live, pixel_x, pixel_y, target):
    delta_x = pixel_x[:, None] - prm_rows[None, :, 0]
    delta_y = pixel_y[:, None] - prm_rows[None, :, 1]
    exponent = -0.5 * (prm_rows[None, :, 2] * delta_x * delta_x + prm_rows[None, :, 4] * delta_y * delta_y) - prm_rows[None, :, 3] * delta_x * delta_y
    alphas = prm_rows[None, :, 5] * live[None, :] * jnp.exp(exponent)
    log_keep = jnp.log1p(-alphas)
    running = jnp.cumsum(log_keep, axis=1)
    log_trans = jnp.concatenate([jnp.zeros((running.shape[0], 1), jnp.float32), running[:, :-1]], axis=1)
    rendered = jnp.dot(jnp.exp(log_trans) * alphas, gathered, precision=HIGH)
    decoded = jnp.dot(rendered, decoder_weight, precision=HIGH) + decoder_bias
    resid = decoded - target
    squares = jnp.sum(resid * resid)
    return (0.5 * squares, squares)

def reference(features, gauss_params, send_index, tile_ids, tile_lists, teacher, decoder_weight, decoder_bias):
    owners = jnp.arange(TILES, dtype=jnp.int32) // TILE_DEV
    live_mask = (tile_lists >= 0).astype(jnp.float32)
    pool_entry = jnp.maximum(tile_lists, 0)
    holder = pool_entry // CAP
    slot_index = pool_entry % CAP
    sent_table = send_index.reshape(N_GS, POOL)
    local_index = sent_table[holder, owners[:, None] * CAP + slot_index]
    gauss_ids = (holder * G_DEV + local_index).astype(jnp.int32)
    pixel_index = jnp.arange(PIX, dtype=jnp.int32)
    pixel_x = ((tile_ids % TILE_COLS * 16)[:, None] + pixel_index[None, :] % 16).astype(jnp.float32) + 0.5
    pixel_y = ((tile_ids // TILE_COLS * 16)[:, None] + pixel_index[None, :] // 16).astype(jnp.float32) + 0.5
    gathered = features[gauss_ids]
    prm_rows = gauss_params.T[gauss_ids]

    def advance(totals, pack):
        tile_rows, tile_prms, tile_live, row_x, row_y, target = pack
        bound = partial(tile_objective, live=tile_live, pixel_x=row_x, pixel_y=row_y, target=target)
        half_sq, pullback, squares = jax.vjp(bound, tile_rows, tile_prms, decoder_weight, decoder_bias, has_aux=True)
        grad_rows, grad_prms, grad_weight, grad_bias = pullback(jnp.ones((), jnp.float32))
        new_totals = (totals[0] + grad_weight, totals[1] + grad_bias, totals[2] + squares)
        return (new_totals, (grad_rows * tile_live[:, None], grad_prms * tile_live[:, None]))
    start_state = (jnp.zeros_like(decoder_weight), jnp.zeros_like(decoder_bias), jnp.zeros((), jnp.float32))
    totals, (grad_rows, grad_prms) = lax.scan(advance, start_state, (gathered, prm_rows, live_mask, pixel_x, pixel_y, teacher))
    flat_ids = gauss_ids.reshape(-1)
    grad_features = jnp.zeros((GAUSS, C), jnp.float32).at[flat_ids].add(grad_rows.reshape(-1, C))
    grad_params = jnp.zeros((GAUSS, 6), jnp.float32).at[flat_ids].add(grad_prms.reshape(-1, 6)).T
    pixels = TILES * PIX
    return (grad_features, grad_params, totals[0] / pixels, totals[1] / pixels, totals[2] / (pixels * CH))
```

```python
import functools

import jax
import jax.numpy as jnp
from jax import lax
from jax.experimental import pallas as pl
from jax.experimental.pallas import tpu as pltpu
from jax.sharding import PartitionSpec as P

F32 = jnp.float32
BF16 = jnp.bfloat16
L = 128
SWAP = [(0, 1), (1, 0)]
FWD = 5
RET = 7
GAT = 3
VMEM = pl.BlockSpec(memory_space=pltpu.VMEM)
SMEM = pl.BlockSpec(memory_space=pltpu.SMEM)
PARAMS = pltpu.CompilerParams(vmem_limit_bytes=48 * 1024 * 1024)


def nn(lhs, rhs):
    return lax.dot_general(lhs, rhs, (((1,), (0,)), ((), ())), preferred_element_type=F32)


def nt(lhs, rhs):
    return lax.dot_general(lhs, rhs, (((1,), (1,)), ((), ())), preferred_element_type=F32)


def split2(value):
    high = value.astype(BF16)
    return high, (value - high.astype(F32)).astype(BF16)


def split3(value):
    high = value.astype(BF16)
    rest = value - high.astype(F32)
    mid = rest.astype(BF16)
    return high, mid, (rest - mid.astype(F32)).astype(BF16)


def ones_where(mask):
    return jnp.where(mask, 1.0, 0.0).astype(F32)


def column_of(rows):
    pad = jnp.zeros((L - rows.shape[0], L), F32)
    return jnp.concatenate([rows, pad], axis=0).T


def pack_kernel(par_ref, idx_ref, feat_ref, prm_ref, out_ref):
    gauss = feat_ref.shape[0]
    first = par_ref[0] == 0
    rows = jnp.where(first, idx_ref[0:4, :], idx_ref[4:8, :])
    cols = column_of(rows.astype(F32))
    high, mid = split2(feat_ref[...])
    table = jnp.concatenate([high, mid], axis=1)
    lane = lax.broadcasted_iota(jnp.int32, (L, gauss), 1).astype(F32)
    groups = gauss // L
    pieces = [prm_ref[:, g * L : (g + 1) * L] for g in range(groups)]
    pad = jnp.zeros((2, L), F32)
    stacked = jnp.concatenate([x for piece in pieces for x in (piece, pad)], axis=0)
    stack3 = jnp.concatenate(split3(stacked), axis=0)
    low_iota = lax.broadcasted_iota(jnp.int32, (L, L), 0)
    packed = []
    for c in range(4):
        onehot = ones_where(cols[:, c : c + 1] == lane).astype(BF16)
        got = nn(onehot, table)
        out_ref[pl.ds(c, L, stride=FWD), :] = got[:, :L] + got[:, L:]
        row = rows[c : c + 1, :]
        low = ones_where((row & (L - 1)) == low_iota).astype(BF16)
        part = nn(stack3, low)
        span = groups * 8
        part = part[:span] + part[span : 2 * span] + part[2 * span :]
        total = jnp.zeros((8, L), F32)
        for g in range(groups):
            total = total + jnp.where((row >> 7) == g, part[g * 8 : g * 8 + 8], 0.0)
        packed.append(total)
    out_ref[pl.ds(4, L, stride=FWD), :] = column_of(jnp.concatenate(packed, axis=0))


def key_kernel(par_ref, lists_ref, row_ref, col_ref):
    shift = par_ref[0] * 4
    tiles, length = lists_ref.shape
    slot_iota = lax.broadcasted_iota(jnp.int32, (8, length), 0)
    holder_iota = lax.broadcasted_iota(jnp.int32, (L, length), 0)
    place = lax.broadcasted_iota(jnp.int32, (8, length), 1)
    place_high = (place >> 4).astype(F32)
    place_low = (place & 15).astype(F32)
    total = jnp.zeros((32, L), F32)
    for t in range(tiles):
        entry = lists_ref[t : t + 1, :]
        holder = ones_where((entry >> 3) == holder_iota).astype(BF16)
        slot = ones_where(((entry + shift) & 7) == slot_iota)
        left = jnp.concatenate(
            [slot * (t + 1.0), slot * place_high, slot * place_low, jnp.zeros((8, length), F32)],
            axis=0,
        ).astype(BF16)
        total = total + nt(left, holder)
    tile = total[0:8]
    key = jnp.where(tile > 0.5, (tile - 1.0) * length + total[8:16] * 16.0 + total[16:24], -1.0)
    row_ref[...] = key
    col_ref[...] = column_of(key)


def main_kernel(
    length,
    par_ref,
    own_ref,
    peer_ref,
    keyrow_ref,
    keycol_ref,
    teacher_hbm,
    weight_ref,
    bias_ref,
    keep_ref,
    give_ref,
    teacher_ref,
    teacher_sem,
    mask_ref,
    prm_ref,
    feat_ref,
    feat2_ref,
    ex_ref,
    alpha_ref,
    trans_ref,
    lk_ref,
    wm_hi,
    wm_lo,
    rt_ref,
    resid_hi,
    resid_lo,
    drt_ref,
    dw_ref,
):
    stripe = par_ref[0]
    fetch = pltpu.make_async_copy(teacher_hbm, teacher_ref, teacher_sem)
    fetch.start()
    tiles = 8
    keyrow = keyrow_ref[...]
    live_all = keyrow >= 0.0
    tile_all = jnp.floor(keyrow * (1.0 / length))
    base_all = jnp.where(live_all, tile_all * length, 1.0e9)
    ox_all = jnp.zeros((8, L), F32)
    oy_all = jnp.zeros((8, L), F32)
    for t in range(tiles):
        ident = par_ref[1 + t]
        here = tile_all == float(t)
        ox_all = jnp.where(here, ((ident & 127) * 16).astype(F32) + 0.5, ox_all)
        oy_all = jnp.where(here, ((ident >> 7) * 16 + stripe * 8).astype(F32) + 0.5, oy_all)
    live_all = ones_where(live_all)

    for side, ref in ((0, own_ref), (1, peer_ref)):
        for c in range(4):
            at = (side * 4 + c) * L
            high, low = split2(ref[pl.ds(c, L, stride=FWD), :])
            feat_ref[at : at + L, 0:L] = high
            feat_ref[at : at + L, L : 2 * L] = low
            feat2_ref[at : at + L, 0:L] = high
            feat2_ref[at : at + L, L : 2 * L] = high
        prm_ref[side * 32 : side * 32 + 32, :] = ref[pl.ds(4, L, stride=FWD), :].T[0:32]

    for a in range(8):
        front = jnp.broadcast_to(keycol_ref[:, a : a + 1], (L, L))
        for b in range(8):
            hit = (front < keyrow[b : b + 1, :]) & (front >= base_all[b : b + 1, :])
            mask_ref[a * L : a * L + L, b * L : b * L + L] = ones_where(hit).astype(BF16)

    kx = lax.broadcasted_iota(jnp.int32, (16, L), 0).astype(F32)
    ky = lax.broadcasted_iota(jnp.int32, (8, L), 0).astype(F32)

    def geometry(b):
        prm = prm_ref[b * 8 : b * 8 + 8, :]
        dx = (kx + ox_all[b : b + 1, :]) - prm[0:1]
        dy = (ky + oy_all[b : b + 1, :]) - prm[1:2]
        return prm, dx, dy

    for b in range(8):
        prm, dx, dy = geometry(b)
        live = live_all[b : b + 1, :]
        ax = prm[2:3] * dx * dx
        cy = prm[4:5] * dy * dy
        bx = prm[3:4] * dx
        cols = slice(b * L, b * L + L)
        for j in range(8):
            power = -0.5 * (ax + cy[j : j + 1]) - bx * dy[j : j + 1]
            ex = live * jnp.exp(power)
            alpha = prm[5:6] * ex
            high, low = split2(jnp.log1p(-alpha))
            spot = slice(j * 16, j * 16 + 16)
            ex_ref[spot, cols] = ex
            alpha_ref[spot, cols] = alpha
            lk_ref[spot, cols] = high
            lk_ref[L + j * 16 : L + j * 16 + 16, cols] = low

    for b in range(8):
        cols = slice(b * L, b * L + L)
        both = nn(lk_ref[...], mask_ref[:, cols])
        trans = jnp.exp(both[:L] + both[L:])
        trans_ref[:, cols] = trans
        high, low = split2(trans * alpha_ref[:, cols])
        for t in range(tiles):
            here = ones_where(tile_all[b : b + 1, :] == float(t))
            here = jnp.broadcast_to(here, (L, L)).astype(BF16)
            wm_hi[t * L : t * L + L, cols] = high * here
            wm_lo[t * L : t * L + L, cols] = low * here

    w_hi, w_lo = split2(weight_ref[...])
    w_pair = jnp.concatenate([w_hi, w_hi], axis=0)
    w_both = jnp.concatenate([w_hi, w_lo], axis=0)
    width = weight_ref.shape[1]
    squares = jnp.zeros((1, width), F32)
    bias_sum = jnp.zeros((1, width), F32)
    dw_ref[...] = jnp.zeros(dw_ref.shape, F32)
    fetch.wait()
    step = 2 * L
    for r in range(tiles // 2):
        rows = slice(r * step, r * step + step)
        both = nn(wm_hi[rows, :], feat_ref[...])
        rendered = both[:, :L] + both[:, L:] + nn(wm_lo[rows, :], feat_ref[:, 0:L])
        high, low = split2(rendered)
        rt_hi, rt_lo = split2(rendered.T)
        rt_ref[0:L, rows] = rt_hi
        rt_ref[L : 2 * L, rows] = rt_lo
        decoded = nn(jnp.concatenate([high, low], axis=1), w_pair) + nn(high, w_lo)
        resid = decoded + bias_ref[...] - teacher_ref[rows, :]
        squares = squares + jnp.sum(resid * resid, axis=0, keepdims=True)
        bias_sum = bias_sum + jnp.sum(resid, axis=0, keepdims=True)
        high, low = split2(resid)
        resid_hi[rows, :] = high
        resid_lo[rows, :] = low
        both = nt(high, w_both)
        grad = both[:, :L] + both[:, L:] + nt(low, w_hi)
        high, low = split2(grad)
        pair = jnp.concatenate([high, low], axis=1)
        dt_hi, dt_lo = split2(grad.T)
        drt_ref[0:L, rows] = dt_hi
        drt_ref[L : 2 * L, rows] = dt_lo
        for b in range(0, 8, 2):
            entries = slice(b * L, b * L + step)
            part = nt(pair, feat2_ref[entries, :]) + nt(high, feat_ref[entries, L : 2 * L])
            for q in range(2):
                cols = slice((b + q) * L, (b + q) * L + L)
                tile = tile_all[b + q : b + q + 1, :]
                got = part[:, q * L : q * L + L]
                kept = jnp.where(tile == float(2 * r), got[:L], dw_ref[:, cols])
                dw_ref[:, cols] = jnp.where(tile == float(2 * r + 1), got[L:], kept)

    both = nn(rt_ref[...], resid_hi[...])
    grad_w = both[:L] + both[L:] + nn(rt_ref[0:L, :], resid_lo[...])

    for b in range(8):
        cols = slice(b * L, b * L + L)
        high, low = split2(dw_ref[:, cols] * (trans_ref[:, cols] * alpha_ref[:, cols]))
        lk_ref[0:L, cols] = high
        lk_ref[L : 2 * L, cols] = low

    blocks = []
    for b in range(8):
        cols = slice(b * L, b * L + L)
        both = nt(lk_ref[...], mask_ref[cols, :])
        alpha = alpha_ref[:, cols]
        dalpha = dw_ref[:, cols] * trans_ref[:, cols] - (both[:L] + both[L:]) / (1.0 - alpha)
        prm, dx, dy = geometry(b)
        dpower = dalpha * alpha
        dopac = jnp.sum(dalpha * ex_ref[:, cols], axis=0, keepdims=True)
        flat = jnp.zeros((16, L), F32)
        by_y = jnp.zeros((16, L), F32)
        by_yy = jnp.zeros((16, L), F32)
        for j in range(8):
            part = dpower[j * 16 : j * 16 + 16]
            scaled = part * dy[j : j + 1]
            flat = flat + part
            by_y = by_y + scaled
            by_yy = by_yy + scaled * dy[j : j + 1]

        def total(value):
            return jnp.sum(value, axis=0, keepdims=True)

        sx = total(flat * dx)
        sxx = total(flat * dx * dx)
        sy = total(by_y)
        sxy = total(by_y * dx)
        syy = total(by_yy)
        blocks += [
            prm[2:3] * sx + prm[3:4] * sy,
            prm[4:5] * sy + prm[3:4] * sx,
            -0.5 * sxx,
            -sxy,
            -0.5 * syy,
            dopac,
            jnp.zeros((2, L), F32),
        ]

    sq_row = jnp.broadcast_to(jnp.sum(squares, axis=1, keepdims=True), (1, L))
    first = stripe == 0
    half = width // 2
    for side, ref in ((0, keep_ref), (1, give_ref)):
        for c in range(4):
            b = side * 4 + c
            cols = slice(b * L, b * L + L)
            both = nn(drt_ref[...], wm_hi[:, cols])
            grad = both[:L] + both[L:] + nn(drt_ref[0:L, :], wm_lo[:, cols])
            ref[pl.ds(c, L, stride=RET), :] = grad.T
        left = first if side == 0 else jnp.logical_not(first)
        piece = jnp.where(left, bias_sum[:, :half], bias_sum[:, half:])
        extra = blocks[side * 28 : side * 28 + 28] + [piece[:, :L], piece[:, L:], sq_row]
        ref[pl.ds(4, L, stride=RET), :] = column_of(jnp.concatenate(extra, axis=0))
        piece = jnp.where(left, grad_w[:, :half], grad_w[:, half:])
        ref[pl.ds(5, L, stride=RET), :] = piece[:, :L]
        ref[pl.ds(6, L, stride=RET), :] = piece[:, L:]


def share_kernel(got_ref, out_ref):
    for at, row in enumerate((5, 6, 4)):
        total = jnp.sum(got_ref[pl.ds(row, L, stride=RET), :], axis=0, keepdims=True)
        out_ref[pl.ds(at, L, stride=GAT), :] = jnp.broadcast_to(total, (L, L))


def scatter_kernel(par_ref, idx_ref, own_ref, peer_ref, feat_ref, prm_ref):
    gauss = feat_ref.shape[0]
    groups = gauss // L
    first = par_ref[0] == 0
    idx = idx_ref[...]
    top, bottom = idx[0:4], idx[4:8]
    idx = jnp.concatenate(
        [jnp.where(first, top, bottom), jnp.where(first, bottom, top)], axis=0
    )
    grads = []
    hots = []
    sub = lax.broadcasted_iota(jnp.int32, (gauss, L), 0)
    low_iota = lax.broadcasted_iota(jnp.int32, (L, L), 0)
    params = jnp.zeros((2 * groups * 8, L), F32)
    for side, ref in ((0, own_ref), (1, peer_ref)):
        prm = ref[pl.ds(4, L, stride=RET), :].T
        for c in range(4):
            b = side * 4 + c
            row = idx[b : b + 1]
            high, low = split2(ref[pl.ds(c, L, stride=RET), :])
            grads.append(jnp.concatenate([high, low], axis=1))
            hots.append(ones_where(row == sub).astype(BF16))
            block = prm[c * 8 : c * 8 + 8]
            spread = jnp.concatenate(
                [jnp.where((row >> 7) == g, block, 0.0) for g in range(groups)], axis=0
            )
            both = jnp.concatenate(split2(spread), axis=0)
            hot = ones_where((row & (L - 1)) == low_iota).astype(BF16)
            params = params + nt(both, hot)
    params = params[: groups * 8] + params[groups * 8 :]
    for g in range(groups):
        prm_ref[:, g * L : g * L + L] = params[g * 8 : g * 8 + 6]
    onehot = jnp.concatenate(hots, axis=1)
    both = nn(onehot, jnp.concatenate(grads, axis=0))
    feat_ref[...] = both[:, :L] + both[:, L:]


def finish_kernel(pixels, par_ref, own_ref, peer_ref, weight_ref, bias_ref, loss_ref):
    first = par_ref[0] == 0
    width = weight_ref.shape[1]
    scale = 1.0 / pixels

    def halves(ref):
        wide = jnp.concatenate(
            [ref[pl.ds(0, L, stride=GAT), :], ref[pl.ds(1, L, stride=GAT), :]], axis=1
        )
        small = ref[pl.ds(2, L, stride=GAT), :].T
        return wide * scale, jnp.concatenate([small[32:33], small[33:34]], axis=1) * scale, small

    own_w, own_b, small = halves(own_ref)
    peer_w, peer_b, unused = halves(peer_ref)
    weight_ref[:, : width // 2] = jnp.where(first, own_w, peer_w)
    weight_ref[:, width // 2 :] = jnp.where(first, peer_w, own_w)
    bias_ref[:, : width // 2] = jnp.where(first, own_b, peer_b)
    bias_ref[:, width // 2 :] = jnp.where(first, peer_b, own_b)
    loss_ref[...] = small[34:35, :] * (scale / width)


def call(kernel, shapes, specs, scratch=()):
    single = not isinstance(shapes, (list, tuple))
    count = 1 if single else len(shapes)
    return pl.pallas_call(
        kernel,
        out_shape=shapes,
        in_specs=specs,
        out_specs=VMEM if single else [VMEM] * count,
        scratch_shapes=list(scratch),
        compiler_params=PARAMS,
    )


def f32(*shape):
    return jax.ShapeDtypeStruct(shape, F32)


def pack(par, idx, features, gauss_params):
    return call(pack_kernel, f32(FWD * L, L), [SMEM, VMEM, VMEM, VMEM])(
        par, idx, features, gauss_params
    )


def keys(par, tile_lists):
    return call(key_kernel, [f32(8, L), f32(L, L)], [SMEM, VMEM])(par, tile_lists)


def main(par, own, peer, keyrow, keycol, teacher, weight, bias, length):
    pixels, width = teacher.shape
    pool = 8 * L
    scratch = [
        pltpu.VMEM((pixels, width), F32),
        pltpu.SemaphoreType.DMA,
        pltpu.VMEM((pool, pool), BF16),
        pltpu.VMEM((64, L), F32),
        pltpu.VMEM((pool, 2 * L), BF16),
        pltpu.VMEM((pool, 2 * L), BF16),
        pltpu.VMEM((L, pool), F32),
        pltpu.VMEM((L, pool), F32),
        pltpu.VMEM((L, pool), F32),
        pltpu.VMEM((2 * L, pool), BF16),
        pltpu.VMEM((pixels, pool), BF16),
        pltpu.VMEM((pixels, pool), BF16),
        pltpu.VMEM((2 * L, pixels), BF16),
        pltpu.VMEM((pixels, width), BF16),
        pltpu.VMEM((pixels, width), BF16),
        pltpu.VMEM((2 * L, pixels), BF16),
        pltpu.VMEM((L, pool), F32),
    ]
    return call(
        functools.partial(main_kernel, float(length)),
        [f32(RET * L, L), f32(RET * L, L)],
        [SMEM, VMEM, VMEM, VMEM, VMEM, pl.BlockSpec(memory_space=pl.ANY), VMEM, VMEM],
        scratch,
    )(par, own, peer, keyrow, keycol, teacher, weight, bias)


def share(got):
    return call(share_kernel, f32(GAT * L, L), [VMEM])(got)


def scatter(par, idx, own, peer, gauss):
    return call(scatter_kernel, [f32(gauss, L), f32(6, gauss)], [SMEM, VMEM, VMEM, VMEM])(
        par, idx, own, peer
    )


def finish(par, own, peer, width, pixels):
    return call(
        functools.partial(finish_kernel, float(pixels)),
        [f32(L, width), f32(1, width), f32(1, L)],
        [SMEM, VMEM, VMEM],
    )(par, own, peer)


def swap(value):
    return lax.ppermute(value, "px", SWAP)


def exchange(value, rows):
    sent = value.reshape(L, 1, rows * L)
    return lax.all_to_all(sent, "gs", split_axis=0, concat_axis=0, tiled=True).reshape(rows * L, L)


def per_device(
    features, gauss_params, send_index, tile_ids, tile_lists, teacher, decoder_weight, decoder_bias
):
    holders = lax.axis_size("gs")
    stripe = lax.axis_index("px").astype(jnp.int32)
    par = jnp.concatenate([stripe[None], tile_ids])
    idx = send_index.reshape(holders, -1).T
    width = teacher.shape[2]
    got = exchange(pack(par, idx, features, gauss_params), FWD)
    keyrow, keycol = keys(par, tile_lists)
    keep, give = main(
        par,
        got,
        swap(got),
        keyrow,
        keycol,
        teacher.reshape(-1, width),
        decoder_weight,
        decoder_bias.reshape(1, -1),
        tile_lists.shape[1],
    )
    back = exchange(keep + swap(give), RET)
    shares = exchange(share(back), GAT)
    grad_features, grad_params = scatter(par, idx, back, swap(back), features.shape[0])
    pixels = holders * tile_ids.shape[0] * 256
    grad_weight, grad_bias, loss = finish(par, shares, swap(shares), width, pixels)
    return grad_features, grad_params, grad_weight, grad_bias.reshape(-1), loss[0, 0]


def solution(mesh):
    return jax.shard_map(
        per_device,
        mesh=mesh,
        in_specs=(
            P("gs", None),
            P(None, "gs"),
            P("gs"),
            P("gs"),
            P("gs", None),
            P("gs", "px", None),
            P(),
            P(),
        ),
        out_specs=(P("gs", None), P(None, "gs"), P(), P(), P()),
        check_vma=False,
    )
```

```python
import functools

import jax
import jax.numpy as jnp
from jax import lax
from jax.experimental import pallas as pl
from jax.experimental.pallas import tpu as pltpu
from jax.sharding import PartitionSpec as P

F32 = jnp.float32
BF16 = jnp.bfloat16
L = 128
SWAP = [(0, 1), (1, 0)]
FWD = 5
RET = 7
GAT = 3
VMEM = pl.BlockSpec(memory_space=pltpu.VMEM)
SMEM = pl.BlockSpec(memory_space=pltpu.SMEM)
PARAMS = pltpu.CompilerParams(vmem_limit_bytes=48 * 1024 * 1024)


def nn(lhs, rhs):
    return lax.dot_general(lhs, rhs, (((1,), (0,)), ((), ())), preferred_element_type=F32)


def nt(lhs, rhs):
    return lax.dot_general(lhs, rhs, (((1,), (1,)), ((), ())), preferred_element_type=F32)


def split2(value):
    high = value.astype(BF16)
    return high, (value - high.astype(F32)).astype(BF16)


def split3(value):
    high = value.astype(BF16)
    rest = value - high.astype(F32)
    mid = rest.astype(BF16)
    return high, mid, (rest - mid.astype(F32)).astype(BF16)


def ones_where(mask):
    return jnp.where(mask, 1.0, 0.0).astype(F32)


def column_of(rows):
    pad = jnp.zeros((L - rows.shape[0], L), F32)
    return jnp.concatenate([rows, pad], axis=0).T


def slot_rows(raw):
    slot = lax.broadcasted_iota(jnp.int32, (8, L), 1) & 7
    mine = slot == lax.broadcasted_iota(jnp.int32, (8, L), 0)
    spread = []
    for r in range(8):
        row = raw[r : r + 1, :]
        high = jnp.where(mine, row >> 4, 0).astype(F32)
        low = jnp.where(mine, row & 15, 0).astype(F32)
        spread.append(jnp.concatenate([high, low], axis=0).astype(BF16))
    source = lax.broadcasted_iota(jnp.int32, (8 * L, L), 0) >> 3
    owner = lax.broadcasted_iota(jnp.int32, (8 * L, L), 1)
    got = nn(jnp.concatenate(spread, axis=1), ones_where(source == owner).astype(BF16))
    return (got[:8] * 16.0 + got[8:]).astype(jnp.int32)


def pack_kernel(par_ref, send_ref, feat_ref, prm_ref, out_ref, idx_ref):
    gauss = feat_ref.shape[0]
    first = par_ref[0] == 0
    idx = slot_rows(send_ref[...])
    idx_ref[...] = idx
    rows = jnp.where(first, idx[0:4, :], idx[4:8, :])
    cols = column_of(rows.astype(F32))
    high, mid = split2(feat_ref[...])
    table = jnp.concatenate([high, mid], axis=1)
    lane = lax.broadcasted_iota(jnp.int32, (L, gauss), 1).astype(F32)
    groups = gauss // L
    pieces = [prm_ref[:, g * L : (g + 1) * L] for g in range(groups)]
    pad = jnp.zeros((2, L), F32)
    stacked = jnp.concatenate([x for piece in pieces for x in (piece, pad)], axis=0)
    stack3 = jnp.concatenate(split3(stacked), axis=0)
    low_iota = lax.broadcasted_iota(jnp.int32, (L, L), 0)
    packed = []
    for c in range(4):
        onehot = ones_where(cols[:, c : c + 1] == lane).astype(BF16)
        got = nn(onehot, table)
        out_ref[pl.ds(c, L, stride=FWD), :] = got[:, :L] + got[:, L:]
        row = rows[c : c + 1, :]
        low = ones_where((row & (L - 1)) == low_iota).astype(BF16)
        part = nn(stack3, low)
        span = groups * 8
        part = part[:span] + part[span : 2 * span] + part[2 * span :]
        total = jnp.zeros((8, L), F32)
        for g in range(groups):
            total = total + jnp.where((row >> 7) == g, part[g * 8 : g * 8 + 8], 0.0)
        packed.append(total)
    out_ref[pl.ds(4, L, stride=FWD), :] = column_of(jnp.concatenate(packed, axis=0))


def key_kernel(par_ref, lists_ref, weight_ref, row_ref, mask_ref, high_ref, low_ref):
    high_ref[...], low_ref[...] = split2(weight_ref[...])
    shift = par_ref[0] * 4
    tiles, length = lists_ref.shape
    slot_iota = lax.broadcasted_iota(jnp.int32, (8, length), 0)
    holder_iota = lax.broadcasted_iota(jnp.int32, (L, length), 0)
    place = lax.broadcasted_iota(jnp.int32, (8, length), 1)
    place_high = (place >> 4).astype(F32)
    place_low = (place & 15).astype(F32)
    total = jnp.zeros((32, L), F32)
    for t in range(tiles):
        entry = lists_ref[t : t + 1, :]
        holder = ones_where((entry >> 3) == holder_iota).astype(BF16)
        slot = ones_where(((entry + shift) & 7) == slot_iota)
        left = jnp.concatenate(
            [slot * (t + 1.0), slot * place_high, slot * place_low, jnp.zeros((8, length), F32)],
            axis=0,
        ).astype(BF16)
        total = total + nt(left, holder)
    tile = total[0:8]
    key = jnp.where(tile > 0.5, (tile - 1.0) * length + total[8:16] * 16.0 + total[16:24], -1.0)
    row_ref[...] = key
    cols = column_of(key)
    base = jnp.where(key >= 0.0, (tile - 1.0) * length, 1.0e9)
    for a in range(8):
        front = jnp.broadcast_to(cols[:, a : a + 1], (L, L))
        for b in range(8):
            hit = (front < key[b : b + 1, :]) & (front >= base[b : b + 1, :])
            mask_ref[a * L : a * L + L, b * L : b * L + L] = ones_where(hit).astype(BF16)


def main_kernel(
    length,
    par_ref,
    ids_ref,
    own_ref,
    peer_ref,
    keyrow_ref,
    mask_ref,
    teacher_hbm,
    whigh_ref,
    wlow_ref,
    bias_ref,
    keep_ref,
    give_ref,
    teacher_ref,
    teacher_sem,
    prm_ref,
    feat_ref,
    feat2_ref,
    ex_ref,
    alpha_ref,
    trans_ref,
    lk_ref,
    wm_hi,
    wm_lo,
    rt_ref,
    resid_hi,
    resid_lo,
    drt_ref,
    dw_ref,
):
    stripe = par_ref[0]
    fetch = pltpu.make_async_copy(teacher_hbm, teacher_ref, teacher_sem)
    fetch.start()
    tiles = 8
    keyrow = keyrow_ref[...]
    live_all = keyrow >= 0.0
    tile_all = jnp.floor(keyrow * (1.0 / length))
    ox_all = jnp.zeros((8, L), F32)
    oy_all = jnp.zeros((8, L), F32)
    for t in range(tiles):
        ident = ids_ref[t]
        here = tile_all == float(t)
        ox_all = jnp.where(here, ((ident & 127) * 16).astype(F32) + 0.5, ox_all)
        oy_all = jnp.where(here, ((ident >> 7) * 16 + stripe * 8).astype(F32) + 0.5, oy_all)
    live_all = ones_where(live_all)

    for side, ref in ((0, own_ref), (1, peer_ref)):
        for c in range(4):
            at = (side * 4 + c) * L
            high, low = split2(ref[pl.ds(c, L, stride=FWD), :])
            feat_ref[at : at + L, 0:L] = high
            feat_ref[at : at + L, L : 2 * L] = low
            feat2_ref[at : at + L, 0:L] = high
            feat2_ref[at : at + L, L : 2 * L] = high
        prm_ref[side * 32 : side * 32 + 32, :] = ref[pl.ds(4, L, stride=FWD), :].T[0:32]

    kx = lax.broadcasted_iota(jnp.int32, (16, L), 0).astype(F32)
    ky = lax.broadcasted_iota(jnp.int32, (8, L), 0).astype(F32)

    def geometry(b):
        prm = prm_ref[b * 8 : b * 8 + 8, :]
        dx = (kx + ox_all[b : b + 1, :]) - prm[0:1]
        dy = (ky + oy_all[b : b + 1, :]) - prm[1:2]
        return prm, dx, dy

    for b in range(8):
        prm, dx, dy = geometry(b)
        live = live_all[b : b + 1, :]
        ax = prm[2:3] * dx * dx
        cy = prm[4:5] * dy * dy
        bx = prm[3:4] * dx
        cols = slice(b * L, b * L + L)
        for j in range(8):
            power = -0.5 * (ax + cy[j : j + 1]) - bx * dy[j : j + 1]
            ex = live * jnp.exp(power)
            alpha = prm[5:6] * ex
            high, low = split2(jnp.log1p(-alpha))
            spot = slice(j * 16, j * 16 + 16)
            ex_ref[spot, cols] = ex
            alpha_ref[spot, cols] = alpha
            lk_ref[spot, cols] = high
            lk_ref[L + j * 16 : L + j * 16 + 16, cols] = low

    for b in range(8):
        cols = slice(b * L, b * L + L)
        both = nn(lk_ref[...], mask_ref[:, cols])
        trans = jnp.exp(both[:L] + both[L:])
        trans_ref[:, cols] = trans
        high, low = split2(trans * alpha_ref[:, cols])
        for t in range(tiles):
            here = ones_where(tile_all[b : b + 1, :] == float(t))
            here = jnp.broadcast_to(here, (L, L)).astype(BF16)
            wm_hi[t * L : t * L + L, cols] = high * here
            wm_lo[t * L : t * L + L, cols] = low * here

    w_hi, w_lo = whigh_ref[...], wlow_ref[...]
    w_pair = jnp.concatenate([w_hi, w_hi], axis=0)
    w_both = jnp.concatenate([w_hi, w_lo], axis=0)
    width = whigh_ref.shape[1]
    squares = jnp.zeros((1, width), F32)
    bias_sum = jnp.zeros((1, width), F32)
    dw_ref[...] = jnp.zeros(dw_ref.shape, F32)
    fetch.wait()
    step = 2 * L
    for r in range(tiles // 2):
        rows = slice(r * step, r * step + step)
        both = nn(wm_hi[rows, :], feat_ref[...])
        rendered = both[:, :L] + both[:, L:] + nn(wm_lo[rows, :], feat_ref[:, 0:L])
        high, low = split2(rendered)
        rt_hi, rt_lo = split2(rendered.T)
        rt_ref[0:L, rows] = rt_hi
        rt_ref[L : 2 * L, rows] = rt_lo
        decoded = nn(jnp.concatenate([high, low], axis=1), w_pair) + nn(high, w_lo)
        resid = decoded + bias_ref[...] - teacher_ref[rows, :]
        squares = squares + jnp.sum(resid * resid, axis=0, keepdims=True)
        bias_sum = bias_sum + jnp.sum(resid, axis=0, keepdims=True)
        high, low = split2(resid)
        resid_hi[rows, :] = high
        resid_lo[rows, :] = low
        both = nt(high, w_both)
        grad = both[:, :L] + both[:, L:] + nt(low, w_hi)
        high, low = split2(grad)
        pair = jnp.concatenate([high, low], axis=1)
        dt_hi, dt_lo = split2(grad.T)
        drt_ref[0:L, rows] = dt_hi
        drt_ref[L : 2 * L, rows] = dt_lo
        for b in range(0, 8, 2):
            entries = slice(b * L, b * L + step)
            part = nt(pair, feat2_ref[entries, :]) + nt(high, feat_ref[entries, L : 2 * L])
            for q in range(2):
                cols = slice((b + q) * L, (b + q) * L + L)
                tile = tile_all[b + q : b + q + 1, :]
                got = part[:, q * L : q * L + L]
                kept = jnp.where(tile == float(2 * r), got[:L], dw_ref[:, cols])
                dw_ref[:, cols] = jnp.where(tile == float(2 * r + 1), got[L:], kept)

    both = nn(rt_ref[...], resid_hi[...])
    grad_w = both[:L] + both[L:] + nn(rt_ref[0:L, :], resid_lo[...])

    for b in range(8):
        cols = slice(b * L, b * L + L)
        high, low = split2(dw_ref[:, cols] * (trans_ref[:, cols] * alpha_ref[:, cols]))
        lk_ref[0:L, cols] = high
        lk_ref[L : 2 * L, cols] = low

    blocks = []
    for b in range(8):
        cols = slice(b * L, b * L + L)
        both = nt(lk_ref[...], mask_ref[cols, :])
        alpha = alpha_ref[:, cols]
        dalpha = dw_ref[:, cols] * trans_ref[:, cols] - (both[:L] + both[L:]) / (1.0 - alpha)
        prm, dx, dy = geometry(b)
        dpower = dalpha * alpha
        dopac = jnp.sum(dalpha * ex_ref[:, cols], axis=0, keepdims=True)
        flat = jnp.zeros((16, L), F32)
        by_y = jnp.zeros((16, L), F32)
        by_yy = jnp.zeros((16, L), F32)
        for j in range(8):
            part = dpower[j * 16 : j * 16 + 16]
            scaled = part * dy[j : j + 1]
            flat = flat + part
            by_y = by_y + scaled
            by_yy = by_yy + scaled * dy[j : j + 1]

        def total(value):
            return jnp.sum(value, axis=0, keepdims=True)

        sx = total(flat * dx)
        sxx = total(flat * dx * dx)
        sy = total(by_y)
        sxy = total(by_y * dx)
        syy = total(by_yy)
        blocks += [
            prm[2:3] * sx + prm[3:4] * sy,
            prm[4:5] * sy + prm[3:4] * sx,
            -0.5 * sxx,
            -sxy,
            -0.5 * syy,
            dopac,
            jnp.zeros((2, L), F32),
        ]

    sq_row = jnp.broadcast_to(jnp.sum(squares, axis=1, keepdims=True), (1, L))
    first = stripe == 0
    half = width // 2
    for side, ref in ((0, keep_ref), (1, give_ref)):
        for c in range(4):
            b = side * 4 + c
            cols = slice(b * L, b * L + L)
            both = nn(drt_ref[...], wm_hi[:, cols])
            grad = both[:L] + both[L:] + nn(drt_ref[0:L, :], wm_lo[:, cols])
            ref[pl.ds(c, L, stride=RET), :] = grad.T
        left = first if side == 0 else jnp.logical_not(first)
        piece = jnp.where(left, bias_sum[:, :half], bias_sum[:, half:])
        extra = blocks[side * 28 : side * 28 + 28] + [piece[:, :L], piece[:, L:], sq_row]
        ref[pl.ds(4, L, stride=RET), :] = column_of(jnp.concatenate(extra, axis=0))
        piece = jnp.where(left, grad_w[:, :half], grad_w[:, half:])
        ref[pl.ds(5, L, stride=RET), :] = piece[:, :L]
        ref[pl.ds(6, L, stride=RET), :] = piece[:, L:]


def share_kernel(got_ref, out_ref):
    for at, row in enumerate((5, 6, 4)):
        total = jnp.sum(got_ref[pl.ds(row, L, stride=RET), :], axis=0, keepdims=True)
        out_ref[pl.ds(at, L, stride=GAT), :] = jnp.broadcast_to(total, (L, L))


def scatter_kernel(par_ref, idx_ref, own_ref, peer_ref, feat_ref, prm_ref):
    gauss = feat_ref.shape[0]
    groups = gauss // L
    first = par_ref[0] == 0
    idx = idx_ref[...]
    top, bottom = idx[0:4], idx[4:8]
    idx = jnp.concatenate(
        [jnp.where(first, top, bottom), jnp.where(first, bottom, top)], axis=0
    )
    grads = []
    hots = []
    sub = lax.broadcasted_iota(jnp.int32, (gauss, L), 0)
    low_iota = lax.broadcasted_iota(jnp.int32, (L, L), 0)
    params = jnp.zeros((2 * groups * 8, L), F32)
    for side, ref in ((0, own_ref), (1, peer_ref)):
        prm = ref[pl.ds(4, L, stride=RET), :].T
        for c in range(4):
            b = side * 4 + c
            row = idx[b : b + 1]
            high, low = split2(ref[pl.ds(c, L, stride=RET), :])
            grads.append(jnp.concatenate([high, low], axis=1))
            hots.append(ones_where(row == sub).astype(BF16))
            block = prm[c * 8 : c * 8 + 8]
            spread = jnp.concatenate(
                [jnp.where((row >> 7) == g, block, 0.0) for g in range(groups)], axis=0
            )
            both = jnp.concatenate(split2(spread), axis=0)
            hot = ones_where((row & (L - 1)) == low_iota).astype(BF16)
            params = params + nt(both, hot)
    params = params[: groups * 8] + params[groups * 8 :]
    for g in range(groups):
        prm_ref[:, g * L : g * L + L] = params[g * 8 : g * 8 + 6]
    onehot = jnp.concatenate(hots, axis=1)
    both = nn(onehot, jnp.concatenate(grads, axis=0))
    feat_ref[...] = both[:, :L] + both[:, L:]


def finish_kernel(pixels, par_ref, own_ref, peer_ref, weight_ref, bias_ref, loss_ref):
    first = par_ref[0] == 0
    width = weight_ref.shape[1]
    scale = 1.0 / pixels

    def halves(ref):
        wide = jnp.concatenate(
            [ref[pl.ds(0, L, stride=GAT), :], ref[pl.ds(1, L, stride=GAT), :]], axis=1
        )
        small = ref[pl.ds(2, L, stride=GAT), :].T
        return wide * scale, jnp.concatenate([small[32:33], small[33:34]], axis=1) * scale, small

    own_w, own_b, small = halves(own_ref)
    peer_w, peer_b, unused = halves(peer_ref)
    weight_ref[:, : width // 2] = jnp.where(first, own_w, peer_w)
    weight_ref[:, width // 2 :] = jnp.where(first, peer_w, own_w)
    bias_ref[:, : width // 2] = jnp.where(first, own_b, peer_b)
    bias_ref[:, width // 2 :] = jnp.where(first, peer_b, own_b)
    loss_ref[...] = small[34:35, :] * (scale / width)


def call(kernel, shapes, specs, scratch=(), flops=0):
    single = not isinstance(shapes, (list, tuple))
    count = 1 if single else len(shapes)
    cost = pl.CostEstimate(flops=flops, bytes_accessed=flops // 300, transcendentals=0)
    return pl.pallas_call(
        kernel,
        out_shape=shapes,
        in_specs=specs,
        out_specs=VMEM if single else [VMEM] * count,
        scratch_shapes=list(scratch),
        compiler_params=PARAMS,
        cost_estimate=cost,
    )


def f32(*shape):
    return jax.ShapeDtypeStruct(shape, F32)


def bf16(*shape):
    return jax.ShapeDtypeStruct(shape, BF16)


def pack(par, send, features, gauss_params):
    shapes = [f32(FWD * L, L), jax.ShapeDtypeStruct((8, L), jnp.int32)]
    return call(pack_kernel, shapes, [SMEM, VMEM, VMEM, VMEM], flops=2 * 10**9)(
        par, send, features, gauss_params
    )


def keys(par, tile_lists, weight):
    shapes = [f32(8, L), bf16(8 * L, 8 * L), bf16(*weight.shape), bf16(*weight.shape)]
    return call(key_kernel, shapes, [SMEM, VMEM, VMEM], flops=3 * 10**9)(par, tile_lists, weight)


def main(par, ids, own, peer, keyrow, mask, teacher, whigh, wlow, bias, length):
    pixels, width = teacher.shape
    pool = 8 * L
    scratch = [
        pltpu.VMEM((pixels, width), F32),
        pltpu.SemaphoreType.DMA,
        pltpu.VMEM((64, L), F32),
        pltpu.VMEM((pool, 2 * L), BF16),
        pltpu.VMEM((pool, 2 * L), BF16),
        pltpu.VMEM((L, pool), F32),
        pltpu.VMEM((L, pool), F32),
        pltpu.VMEM((L, pool), F32),
        pltpu.VMEM((2 * L, pool), BF16),
        pltpu.VMEM((pixels, pool), BF16),
        pltpu.VMEM((pixels, pool), BF16),
        pltpu.VMEM((2 * L, pixels), BF16),
        pltpu.VMEM((pixels, width), BF16),
        pltpu.VMEM((pixels, width), BF16),
        pltpu.VMEM((2 * L, pixels), BF16),
        pltpu.VMEM((L, pool), F32),
    ]
    anywhere = pl.BlockSpec(memory_space=pl.ANY)
    return call(
        functools.partial(main_kernel, float(length)),
        [f32(RET * L, L), f32(RET * L, L)],
        [SMEM, SMEM, VMEM, VMEM, VMEM, VMEM, anywhere, VMEM, VMEM, VMEM],
        scratch,
        flops=10**10,
    )(par, ids, own, peer, keyrow, mask, teacher, whigh, wlow, bias)


def share(got):
    return call(share_kernel, f32(GAT * L, L), [VMEM], flops=10**9)(got)


def scatter(par, idx, own, peer, gauss):
    shapes = [f32(gauss, L), f32(6, gauss)]
    return call(scatter_kernel, shapes, [SMEM, VMEM, VMEM, VMEM], flops=4 * 10**9)(
        par, idx, own, peer
    )


def finish(par, own, peer, width, pixels):
    return call(
        functools.partial(finish_kernel, float(pixels)),
        [f32(L, width), f32(1, width), f32(1, L)],
        [SMEM, VMEM, VMEM],
        flops=10**9,
    )(par, own, peer)


def swap(value):
    return lax.ppermute(value, "px", SWAP)


def exchange(value, rows):
    sent = value.reshape(L, 1, rows * L)
    return lax.all_to_all(sent, "gs", split_axis=0, concat_axis=0, tiled=True).reshape(rows * L, L)


def per_device(
    features, gauss_params, send_index, tile_ids, tile_lists, teacher, decoder_weight, decoder_bias
):
    holders = lax.axis_size("gs")
    par = lax.axis_index("px").astype(jnp.int32).reshape(1)
    width = teacher.shape[2]
    sent, idx = pack(par, send_index.reshape(8, -1), features, gauss_params)
    sent, tile_lists, decoder_weight, teacher = lax.optimization_barrier(
        (sent, tile_lists, decoder_weight, teacher)
    )
    got = exchange(sent, FWD)
    prepared = keys(par, tile_lists, decoder_weight)
    got, prepared = lax.optimization_barrier((got, prepared))
    keyrow, mask, whigh, wlow = prepared
    keep, give = main(
        par,
        tile_ids,
        got,
        swap(got),
        keyrow,
        mask,
        teacher.reshape(-1, width),
        whigh,
        wlow,
        decoder_bias.reshape(1, -1),
        tile_lists.shape[1],
    )
    back = exchange(keep + swap(give), RET)
    shares = exchange(share(back), GAT)
    grads = scatter(par, idx, back, swap(back), features.shape[0])
    shares, (grad_features, grad_params) = lax.optimization_barrier((shares, grads))
    pixels = holders * tile_ids.shape[0] * 256
    grad_weight, grad_bias, loss = finish(par, shares, swap(shares), width, pixels)
    return grad_features, grad_params, grad_weight, grad_bias.reshape(-1), loss[0, 0]


def solution(mesh):
    return jax.shard_map(
        per_device,
        mesh=mesh,
        in_specs=(
            P("gs", None),
            P(None, "gs"),
            P("gs"),
            P("gs"),
            P("gs", None),
            P("gs", "px", None),
            P(),
            P(),
        ),
        out_specs=(P("gs", None), P(None, "gs"), P(), P(), P()),
        check_vma=False,
    )
```

```python
import functools

import jax
import jax.numpy as jnp
from jax import lax
from jax.experimental import pallas as pl
from jax.experimental.pallas import tpu as pltpu
from jax.sharding import PartitionSpec as P

F32 = jnp.float32
BF16 = jnp.bfloat16
L = 128
SWAP = [(0, 1), (1, 0)]
FWD = 5
RET = 7
GAT = 3
VMEM = pl.BlockSpec(memory_space=pltpu.VMEM)
SMEM = pl.BlockSpec(memory_space=pltpu.SMEM)
HBM = pl.BlockSpec(memory_space=pltpu.HBM)
PARAMS = pltpu.CompilerParams(vmem_limit_bytes=40 * 1024 * 1024)


def nn(lhs, rhs):
    return lax.dot_general(lhs, rhs, (((1,), (0,)), ((), ())), preferred_element_type=F32)


def nt(lhs, rhs):
    return lax.dot_general(lhs, rhs, (((1,), (1,)), ((), ())), preferred_element_type=F32)


def split2(value):
    high = value.astype(BF16)
    return high, (value - high.astype(F32)).astype(BF16)


def split3(value):
    high = value.astype(BF16)
    rest = value - high.astype(F32)
    mid = rest.astype(BF16)
    return high, mid, (rest - mid.astype(F32)).astype(BF16)


def ones_where(mask):
    return jnp.where(mask, 1.0, 0.0).astype(F32)


def column_of(rows):
    pad = jnp.zeros((L - rows.shape[0], L), F32)
    return jnp.concatenate([rows, pad], axis=0).T


def slot_rows(raw):
    slot = lax.broadcasted_iota(jnp.int32, (8, L), 1) & 7
    mine = slot == lax.broadcasted_iota(jnp.int32, (8, L), 0)
    spread = []
    for r in range(8):
        row = raw[r : r + 1, :]
        high = jnp.where(mine, row >> 4, 0).astype(F32)
        low = jnp.where(mine, row & 15, 0).astype(F32)
        spread.append(jnp.concatenate([high, low], axis=0).astype(BF16))
    source = lax.broadcasted_iota(jnp.int32, (8 * L, L), 0) >> 3
    owner = lax.broadcasted_iota(jnp.int32, (8 * L, L), 1)
    got = nn(jnp.concatenate(spread, axis=1), ones_where(source == owner).astype(BF16))
    return (got[:8] * 16.0 + got[8:]).astype(jnp.int32)


def pack_kernel(par_ref, send_hbm, feat_hbm, prm_hbm, out_ref, idx_ref, send_ref, feat_ref, prm_ref, sems):
    copies = [
        pltpu.make_async_copy(src, dst, sems.at[n])
        for n, (src, dst) in enumerate(
            ((send_hbm, send_ref), (feat_hbm, feat_ref), (prm_hbm, prm_ref))
        )
    ]
    for copy in copies:
        copy.start()
    gauss = feat_ref.shape[0]
    copies[0].wait()
    first = par_ref[0] == 0
    idx = slot_rows(send_ref[...])
    idx_ref[...] = idx
    rows = jnp.where(first, idx[0:4, :], idx[4:8, :])
    cols = column_of(rows.astype(F32))
    lane = lax.broadcasted_iota(jnp.int32, (L, gauss), 1).astype(F32)
    hots = [ones_where(cols[:, c : c + 1] == lane).astype(BF16) for c in range(4)]
    copies[2].wait()
    copies[1].wait()
    got = nn(
        jnp.concatenate(hots, axis=0), jnp.concatenate(split2(feat_ref[...]), axis=1)
    )
    groups = gauss // L
    pieces = [prm_ref[:, g * L : (g + 1) * L] for g in range(groups)]
    pad = jnp.zeros((2, L), F32)
    stacked = jnp.concatenate([x for piece in pieces for x in (piece, pad)], axis=0)
    stack3 = jnp.concatenate(split3(stacked), axis=0)
    low_iota = lax.broadcasted_iota(jnp.int32, (L, L), 0)
    packed = []
    for c in range(4):
        part = got[c * L : c * L + L]
        out_ref[pl.ds(c, L, stride=FWD), :] = part[:, :L] + part[:, L:]
        row = rows[c : c + 1, :]
        low = ones_where((row & (L - 1)) == low_iota).astype(BF16)
        part = nn(stack3, low)
        span = groups * 8
        part = part[:span] + part[span : 2 * span] + part[2 * span :]
        total = jnp.zeros((8, L), F32)
        for g in range(groups):
            total = total + jnp.where((row >> 7) == g, part[g * 8 : g * 8 + 8], 0.0)
        packed.append(total)
    out_ref[pl.ds(4, L, stride=FWD), :] = column_of(jnp.concatenate(packed, axis=0))


def key_kernel(par_ref, lists_ref, weight_ref, row_ref, high_ref, low_ref):
    high_ref[...], low_ref[...] = split2(weight_ref[...])
    shift = par_ref[0] * 4
    tiles, length = lists_ref.shape
    slot_iota = lax.broadcasted_iota(jnp.int32, (8, length), 0)
    holder_iota = lax.broadcasted_iota(jnp.int32, (L, length), 0)
    place = lax.broadcasted_iota(jnp.int32, (8, length), 1)
    place_high = (place >> 4).astype(F32)
    place_low = (place & 15).astype(F32)
    total = jnp.zeros((32, L), F32)
    for t in range(tiles):
        entry = lists_ref[t : t + 1, :]
        holder = ones_where((entry >> 3) == holder_iota).astype(BF16)
        slot = ones_where(((entry + shift) & 7) == slot_iota)
        left = jnp.concatenate(
            [slot * (t + 1.0), slot * place_high, slot * place_low, jnp.zeros((8, length), F32)],
            axis=0,
        ).astype(BF16)
        total = total + nt(left, holder)
    tile = total[0:8]
    key = jnp.where(tile > 0.5, (tile - 1.0) * length + total[8:16] * 16.0 + total[16:24], -1.0)
    row_ref[...] = key


class Pool:
    def __init__(self, length, par_ref, ids_ref, keyrow_ref, prm_ref, own_ref, peer_ref):
        self.length, self.prm_ref = length, prm_ref
        stripe = par_ref[0]
        self.key = keyrow_ref[...]
        live = self.key >= 0.0
        self.tile = jnp.floor(self.key * (1.0 / length))
        self.ox = jnp.zeros((8, L), F32)
        self.oy = jnp.zeros((8, L), F32)
        for t in range(8):
            ident = ids_ref[t]
            here = self.tile == float(t)
            self.ox = jnp.where(here, ((ident & 127) * 16).astype(F32) + 0.5, self.ox)
            self.oy = jnp.where(
                here, ((ident >> 7) * 16 + stripe * 8).astype(F32) + 0.5, self.oy
            )
        self.base = jnp.where(live, self.tile * length, 1.0e9)
        self.live = ones_where(live)
        self.kx = lax.broadcasted_iota(jnp.int32, (16, L), 0).astype(F32)
        self.ky = lax.broadcasted_iota(jnp.int32, (8, L), 0).astype(F32)
        for side, ref in ((0, own_ref), (1, peer_ref)):
            prm_ref[side * 32 : side * 32 + 32, :] = ref[pl.ds(4, L, stride=FWD), :].T[0:32]

    def geometry(self, b):
        prm = self.prm_ref[b * 8 : b * 8 + 8, :]
        dx = (self.kx + self.ox[b : b + 1, :]) - prm[0:1]
        dy = (self.ky + self.oy[b : b + 1, :]) - prm[1:2]
        return prm, dx, dy

    def alphas(self, b):
        prm, dx, dy = self.geometry(b)
        ax = prm[2:3] * dx * dx
        cy = prm[4:5] * dy * dy
        bx = prm[3:4] * dx
        for j in range(8):
            power = -0.5 * (ax + cy[j : j + 1]) - bx * dy[j : j + 1]
            ex = self.live[b : b + 1, :] * jnp.exp(power)
            yield slice(j * 16, j * 16 + 16), ex, prm[5:6] * ex

    def fill_mask(self, mask_ref):
        cols = column_of(self.key)
        for a in range(8):
            front = jnp.broadcast_to(cols[:, a : a + 1], (L, L))
            for b in range(8):
                hit = (front < self.key[b : b + 1, :]) & (front >= self.base[b : b + 1, :])
                mask_ref[a * L : a * L + L, b * L : b * L + L] = ones_where(hit).astype(BF16)

    def spread(self, b, weights, high_ref, low_ref):
        cols = slice(b * L, b * L + L)
        high, low = split2(weights)
        for t in range(8):
            here = ones_where(self.tile[b : b + 1, :] == float(t))
            here = jnp.broadcast_to(here, (L, L)).astype(BF16)
            high_ref[t * L : t * L + L, cols] = high * here
            low_ref[t * L : t * L + L, cols] = low * here


def fill_features(own_ref, peer_ref, feat_ref):
    for side, ref in ((0, own_ref), (1, peer_ref)):
        for c in range(4):
            at = (side * 4 + c) * L
            high, low = split2(ref[pl.ds(c, L, stride=FWD), :])
            feat_ref[at : at + L, 0:L] = high
            feat_ref[at : at + L, L : 2 * L] = low


def front_kernel(
    length,
    par_ref,
    ids_ref,
    own_ref,
    peer_ref,
    keyrow_ref,
    teacher_ref,
    whigh_ref,
    wlow_ref,
    bias_ref,
    keep_ref,
    give_ref,
    trans_ref,
    grad_ref,
    mask_ref,
    prm_ref,
    feat_ref,
    alpha_ref,
    lk_ref,
    wm_hi,
    wm_lo,
    rt_ref,
    resid_hi,
    resid_lo,
):
    pool = Pool(length, par_ref, ids_ref, keyrow_ref, prm_ref, own_ref, peer_ref)
    fill_features(own_ref, peer_ref, feat_ref)
    pool.fill_mask(mask_ref)
    for b in range(8):
        cols = slice(b * L, b * L + L)
        for spot, ex, alpha in pool.alphas(b):
            high, low = split2(jnp.log1p(-alpha))
            alpha_ref[spot, cols] = alpha
            lk_ref[spot, cols] = high
            lk_ref[L + spot.start : L + spot.stop, cols] = low

    for b in range(0, 8, 2):
        both = nn(lk_ref[...], mask_ref[:, b * L : b * L + 2 * L])
        trans = jnp.exp(both[:L] + both[L:])
        trans_ref[:, b * L : b * L + 2 * L] = trans
        for q in range(2):
            cols = slice((b + q) * L, (b + q) * L + L)
            weights = trans[:, q * L : q * L + L] * alpha_ref[:, cols]
            pool.spread(b + q, weights, wm_hi, wm_lo)

    w_hi, w_lo = whigh_ref[...], wlow_ref[...]
    w_pair = jnp.concatenate([w_hi, w_hi], axis=0)
    w_both = jnp.concatenate([w_hi, w_lo], axis=0)
    width = whigh_ref.shape[1]
    squares = jnp.zeros((1, width), F32)
    bias_sum = jnp.zeros((1, width), F32)
    step = 2 * L
    for r in range(4):
        rows = slice(r * step, r * step + step)
        both = nn(wm_hi[rows, :], feat_ref[...])
        rendered = both[:, :L] + both[:, L:] + nn(wm_lo[rows, :], feat_ref[:, 0:L])
        high, low = split2(rendered)
        rt_hi, rt_lo = split2(rendered.T)
        rt_ref[0:L, rows] = rt_hi
        rt_ref[L : 2 * L, rows] = rt_lo
        decoded = nn(jnp.concatenate([high, low], axis=1), w_pair) + nn(high, w_lo)
        resid = decoded + bias_ref[...] - teacher_ref[rows, :]
        squares = squares + jnp.sum(resid * resid, axis=0, keepdims=True)
        bias_sum = bias_sum + jnp.sum(resid, axis=0, keepdims=True)
        high, low = split2(resid)
        resid_hi[rows, :] = high
        resid_lo[rows, :] = low
        both = nt(high, w_both)
        grad_ref[rows, :] = both[:, :L] + both[:, L:] + nt(low, w_hi)

    both = nn(rt_ref[...], resid_hi[...])
    grad_w = both[:L] + both[L:] + nn(rt_ref[0:L, :], resid_lo[...])
    sq_row = jnp.broadcast_to(jnp.sum(squares, axis=1, keepdims=True), (1, L))
    first = par_ref[0] == 0
    half = width // 2
    for ref, left in ((keep_ref, first), (give_ref, jnp.logical_not(first))):
        piece = jnp.where(left, grad_w[:, :half], grad_w[:, half:])
        ref[pl.ds(0, L, stride=GAT), :] = piece[:, :L]
        ref[pl.ds(1, L, stride=GAT), :] = piece[:, L:]
        piece = jnp.where(left, bias_sum[:, :half], bias_sum[:, half:])
        rows = jnp.concatenate([piece[:, :L], piece[:, L:], sq_row], axis=0)
        ref[pl.ds(2, L, stride=GAT), :] = column_of(rows)


def back_kernel(
    length,
    par_ref,
    ids_ref,
    own_ref,
    peer_ref,
    keyrow_ref,
    trans_ref,
    grad_ref,
    keep_ref,
    give_ref,
    mask_ref,
    prm_ref,
    feat_ref,
    feat2_ref,
    ex_ref,
    alpha_ref,
    lk_ref,
    wm_hi,
    wm_lo,
    drt_ref,
    dw_ref,
):
    pool = Pool(length, par_ref, ids_ref, keyrow_ref, prm_ref, own_ref, peer_ref)
    fill_features(own_ref, peer_ref, feat_ref)
    feat2_ref[:, 0:L] = feat_ref[:, 0:L]
    feat2_ref[:, L : 2 * L] = feat_ref[:, 0:L]
    pool.fill_mask(mask_ref)
    for b in range(8):
        cols = slice(b * L, b * L + L)
        for spot, ex, alpha in pool.alphas(b):
            ex_ref[spot, cols] = ex
            alpha_ref[spot, cols] = alpha
        pool.spread(b, trans_ref[:, cols] * alpha_ref[:, cols], wm_hi, wm_lo)

    dw_ref[...] = jnp.zeros(dw_ref.shape, F32)
    step = 2 * L
    for r in range(4):
        rows = slice(r * step, r * step + step)
        grad = grad_ref[rows, :]
        high, low = split2(grad)
        pair = jnp.concatenate([high, low], axis=1)
        dt_hi, dt_lo = split2(grad.T)
        drt_ref[0:L, rows] = dt_hi
        drt_ref[L : 2 * L, rows] = dt_lo
        for b in range(0, 8, 2):
            entries = slice(b * L, b * L + step)
            part = nt(pair, feat2_ref[entries, :]) + nt(high, feat_ref[entries, L : 2 * L])
            for q in range(2):
                cols = slice((b + q) * L, (b + q) * L + L)
                tile = pool.tile[b + q : b + q + 1, :]
                got = part[:, q * L : q * L + L]
                kept = jnp.where(tile == float(2 * r), got[:L], dw_ref[:, cols])
                dw_ref[:, cols] = jnp.where(tile == float(2 * r + 1), got[L:], kept)

    for b in range(8):
        cols = slice(b * L, b * L + L)
        high, low = split2(dw_ref[:, cols] * (trans_ref[:, cols] * alpha_ref[:, cols]))
        lk_ref[0:L, cols] = high
        lk_ref[L : 2 * L, cols] = low

    def total(value):
        return jnp.sum(value, axis=0, keepdims=True)

    blocks = []
    for b in range(0, 8, 2):
        wide = slice(b * L, b * L + step)
        both = nt(lk_ref[...], mask_ref[wide, :])
        alpha = alpha_ref[:, wide]
        dalpha = dw_ref[:, wide] * trans_ref[:, wide] - (both[:L] + both[L:]) / (1.0 - alpha)
        dpower = dalpha * alpha
        dopac = total(dalpha * ex_ref[:, wide])
        for q in range(2):
            prm, dx, dy = pool.geometry(b + q)
            flat = jnp.zeros((16, L), F32)
            by_y = jnp.zeros((16, L), F32)
            by_yy = jnp.zeros((16, L), F32)
            for j in range(8):
                part = dpower[j * 16 : j * 16 + 16, q * L : q * L + L]
                scaled = part * dy[j : j + 1]
                flat = flat + part
                by_y = by_y + scaled
                by_yy = by_yy + scaled * dy[j : j + 1]
            sx = total(flat * dx)
            sxx = total(flat * dx * dx)
            sy = total(by_y)
            sxy = total(by_y * dx)
            syy = total(by_yy)
            blocks += [
                prm[2:3] * sx + prm[3:4] * sy,
                prm[4:5] * sy + prm[3:4] * sx,
                -0.5 * sxx,
                -sxy,
                -0.5 * syy,
                dopac[:, q * L : q * L + L],
                jnp.zeros((2, L), F32),
            ]

    for side, ref in ((0, keep_ref), (1, give_ref)):
        for c in range(0, 4, 2):
            wide = slice((side * 4 + c) * L, (side * 4 + c) * L + step)
            both = nn(drt_ref[...], wm_hi[:, wide])
            grad = both[:L] + both[L:] + nn(drt_ref[0:L, :], wm_lo[:, wide])
            ref[pl.ds(c, L, stride=FWD), :] = grad[:, :L].T
            ref[pl.ds(c + 1, L, stride=FWD), :] = grad[:, L:].T
        rows = jnp.concatenate(blocks[side * 28 : side * 28 + 28], axis=0)
        ref[pl.ds(4, L, stride=FWD), :] = column_of(rows)


def compose_kernel(share_ref, keep_ref, give_ref, out_ref):
    for c in range(5):
        spot = pl.ds(c, L, stride=FWD)
        rows = keep_ref[spot, :] + give_ref[spot, :]
        if c == 4:
            small = jnp.sum(share_ref[pl.ds(2, L, stride=GAT), :], axis=0, keepdims=True)
            rows = rows + pltpu.roll(jnp.broadcast_to(small, (L, L)), 32, 1)
        out_ref[pl.ds(c, L, stride=RET), :] = rows
    for c in range(2):
        total = jnp.sum(share_ref[pl.ds(c, L, stride=GAT), :], axis=0, keepdims=True)
        out_ref[pl.ds(5 + c, L, stride=RET), :] = jnp.broadcast_to(total, (L, L))


def final_kernel(
    pixels, par_ref, idx_ref, own_ref, peer_ref, feat_ref, prm_ref, weight_ref, bias_ref, loss_ref
):
    gauss = feat_ref.shape[0]
    groups = gauss // L
    first = par_ref[0] == 0
    idx = idx_ref[...]
    top, bottom = idx[0:4], idx[4:8]
    idx = jnp.concatenate(
        [jnp.where(first, top, bottom), jnp.where(first, bottom, top)], axis=0
    )
    grads = []
    hots = []
    sub = lax.broadcasted_iota(jnp.int32, (gauss, L), 0)
    low_iota = lax.broadcasted_iota(jnp.int32, (L, L), 0)
    params = jnp.zeros((2 * groups * 8, L), F32)
    for side, ref in ((0, own_ref), (1, peer_ref)):
        prm = ref[pl.ds(4, L, stride=RET), :].T
        for c in range(4):
            b = side * 4 + c
            row = idx[b : b + 1]
            high, low = split2(ref[pl.ds(c, L, stride=RET), :])
            grads.append(jnp.concatenate([high, low], axis=1))
            hots.append(ones_where(row == sub).astype(BF16))
            block = prm[c * 8 : c * 8 + 8]
            spread = jnp.concatenate(
                [jnp.where((row >> 7) == g, block, 0.0) for g in range(groups)], axis=0
            )
            both = jnp.concatenate(split2(spread), axis=0)
            hot = ones_where((row & (L - 1)) == low_iota).astype(BF16)
            params = params + nt(both, hot)
    params = params[: groups * 8] + params[groups * 8 :]
    for g in range(groups):
        prm_ref[:, g * L : g * L + L] = params[g * 8 : g * 8 + 6]
    onehot = jnp.concatenate(hots, axis=1)
    both = nn(onehot, jnp.concatenate(grads, axis=0))
    feat_ref[...] = both[:, :L] + both[:, L:]

    width = weight_ref.shape[1]
    half = width // 2
    scale = 1.0 / pixels
    for ref, left in ((own_ref, first), (peer_ref, jnp.logical_not(first))):
        small = ref[pl.ds(4, L, stride=RET), :].T
        wide = [ref[pl.ds(5 + c, L, stride=RET), :] * scale for c in range(2)]
        row = jnp.concatenate([small[32:33], small[33:34]], axis=1) * scale
        wide = jnp.concatenate(wide, axis=1)

        def store(at):
            weight_ref[:, at : at + half] = wide
            bias_ref[:, at : at + half] = row

        pl.when(left)(functools.partial(store, 0))
        pl.when(jnp.logical_not(left))(functools.partial(store, half))
    loss_ref[...] = small[34:35, :] * (scale / width)


def call(kernel, shapes, specs, scratch=(), flops=0):
    single = not isinstance(shapes, (list, tuple))
    count = 1 if single else len(shapes)
    cost = pl.CostEstimate(flops=flops, bytes_accessed=flops // 300, transcendentals=0)
    return pl.pallas_call(
        kernel,
        out_shape=shapes,
        in_specs=specs,
        out_specs=VMEM if single else [VMEM] * count,
        scratch_shapes=list(scratch),
        compiler_params=PARAMS,
        cost_estimate=cost,
    )


def f32(*shape):
    return jax.ShapeDtypeStruct(shape, F32)


def bf16(*shape):
    return jax.ShapeDtypeStruct(shape, BF16)


def pack(par, send, features, gauss_params):
    shapes = [f32(FWD * L, L), jax.ShapeDtypeStruct((8, L), jnp.int32)]
    inputs = (send, features, gauss_params)
    scratch = [pltpu.VMEM(x.shape, x.dtype) for x in inputs]
    scratch.append(pltpu.SemaphoreType.DMA((3,)))
    return call(pack_kernel, shapes, [SMEM, HBM, HBM, HBM], scratch, flops=2 * 10**9)(par, *inputs)


def keys(par, tile_lists, weight):
    shapes = [f32(8, L), bf16(*weight.shape), bf16(*weight.shape)]
    return call(key_kernel, shapes, [SMEM, VMEM, VMEM], flops=2 * 10**9)(par, tile_lists, weight)


def front(par, ids, own, peer, keyrow, teacher, whigh, wlow, bias, length):
    pixels, width = teacher.shape
    pool = 8 * L
    scratch = [
        pltpu.VMEM((pool, pool), BF16),
        pltpu.VMEM((64, L), F32),
        pltpu.VMEM((pool, 2 * L), BF16),
        pltpu.VMEM((L, pool), F32),
        pltpu.VMEM((2 * L, pool), BF16),
        pltpu.VMEM((pixels, pool), BF16),
        pltpu.VMEM((pixels, pool), BF16),
        pltpu.VMEM((2 * L, pixels), BF16),
        pltpu.VMEM((pixels, width), BF16),
        pltpu.VMEM((pixels, width), BF16),
    ]
    return call(
        functools.partial(front_kernel, float(length)),
        [f32(GAT * L, L), f32(GAT * L, L), f32(L, pool), f32(pixels, L)],
        [SMEM, SMEM] + [VMEM] * 7,
        scratch,
        flops=10**10,
    )(par, ids, own, peer, keyrow, teacher, whigh, wlow, bias)


def back(par, ids, own, peer, keyrow, trans, grad, length):
    pool = 8 * L
    pixels = grad.shape[0]
    scratch = [
        pltpu.VMEM((pool, pool), BF16),
        pltpu.VMEM((64, L), F32),
        pltpu.VMEM((pool, 2 * L), BF16),
        pltpu.VMEM((pool, 2 * L), BF16),
        pltpu.VMEM((L, pool), F32),
        pltpu.VMEM((L, pool), F32),
        pltpu.VMEM((2 * L, pool), BF16),
        pltpu.VMEM((pixels, pool), BF16),
        pltpu.VMEM((pixels, pool), BF16),
        pltpu.VMEM((2 * L, pixels), BF16),
        pltpu.VMEM((L, pool), F32),
    ]
    return call(
        functools.partial(back_kernel, float(length)),
        [f32(FWD * L, L), f32(FWD * L, L)],
        [SMEM, SMEM] + [VMEM] * 5,
        scratch,
        flops=8 * 10**9,
    )(par, ids, own, peer, keyrow, trans, grad)


def compose(share, keep, give):
    return call(compose_kernel, f32(RET * L, L), [VMEM] * 3, flops=10**9)(share, keep, give)


def final(par, idx, own, peer, gauss, width, pixels):
    return call(
        functools.partial(final_kernel, float(pixels)),
        [f32(gauss, L), f32(6, gauss), f32(L, width), f32(1, width), f32(1, L)],
        [SMEM, VMEM, VMEM, VMEM],
        flops=4 * 10**9,
    )(par, idx, own, peer)


def swap(value):
    return lax.ppermute(value, "px", SWAP)


def exchange(value, rows):
    sent = value.reshape(L, 1, rows * L)
    return lax.all_to_all(sent, "gs", split_axis=0, concat_axis=0, tiled=True).reshape(rows * L, L)


def per_device(
    features, gauss_params, send_index, tile_ids, tile_lists, teacher, decoder_weight, decoder_bias
):
    holders = lax.axis_size("gs")
    par = lax.axis_index("px").astype(jnp.int32).reshape(1)
    width = teacher.shape[2]
    sent, idx = pack(par, send_index.reshape(8, -1), features, gauss_params)
    sent, tile_lists, decoder_weight, teacher = lax.optimization_barrier(
        (sent, tile_lists, decoder_weight, teacher)
    )
    got = exchange(sent, FWD)
    prepared = keys(par, tile_lists, decoder_weight)
    got, (keyrow, whigh, wlow) = lax.optimization_barrier((got, prepared))
    peer = swap(got)
    length = tile_lists.shape[1]
    flat_teacher = teacher.reshape(-1, width)
    bias = decoder_bias.reshape(1, -1)
    keep, give, trans, grad = front(
        par, tile_ids, got, peer, keyrow, flat_teacher, whigh, wlow, bias, length
    )
    part, trans, grad = lax.optimization_barrier((keep + swap(give), trans, grad))
    share = exchange(part, GAT)
    keep, give = back(par, tile_ids, got, peer, keyrow, trans, grad, length)
    ret = exchange(compose(share, keep, swap(give)), RET)
    pixels = holders * tile_ids.shape[0] * 256
    grad_features, grad_params, grad_weight, grad_bias, loss = final(
        par, idx, ret, swap(ret), features.shape[0], width, pixels
    )
    return grad_features, grad_params, grad_weight, grad_bias.reshape(-1), loss[0, 0]


def solution(mesh):
    return jax.shard_map(
        per_device,
        mesh=mesh,
        in_specs=(
            P("gs", None),
            P(None, "gs"),
            P("gs"),
            P("gs"),
            P("gs", None),
            P("gs", "px", None),
            P(),
            P(),
        ),
        out_specs=(P("gs", None), P(None, "gs"), P(), P(), P()),
        check_vma=False,
    )
```

```python
import functools

import jax
import jax.numpy as jnp
from jax import lax
from jax.experimental import pallas as pl
from jax.experimental.pallas import tpu as pltpu
from jax.sharding import PartitionSpec as P

F32 = jnp.float32
BF16 = jnp.bfloat16
L = 128
SWAP = [(0, 1), (1, 0)]
FWD = 5
RET = 7
GAT = 3
VMEM = pl.BlockSpec(memory_space=pltpu.VMEM)
SMEM = pl.BlockSpec(memory_space=pltpu.SMEM)
HBM = pl.BlockSpec(memory_space=pltpu.HBM)


def nn(lhs, rhs):
    return lax.dot_general(lhs, rhs, (((1,), (0,)), ((), ())), preferred_element_type=F32)


def nt(lhs, rhs):
    return lax.dot_general(lhs, rhs, (((1,), (1,)), ((), ())), preferred_element_type=F32)


def split2(value):
    high = value.astype(BF16)
    return high, (value - high.astype(F32)).astype(BF16)


def split3(value):
    high = value.astype(BF16)
    rest = value - high.astype(F32)
    mid = rest.astype(BF16)
    return high, mid, (rest - mid.astype(F32)).astype(BF16)


def ones_where(mask):
    return jnp.where(mask, 1.0, 0.0).astype(F32)


def column_of(rows):
    pad = jnp.zeros((L - rows.shape[0], L), F32)
    return jnp.concatenate([rows, pad], axis=0).T


def slot_rows(raw):
    slot = lax.broadcasted_iota(jnp.int32, (8, L), 1) & 7
    mine = slot == lax.broadcasted_iota(jnp.int32, (8, L), 0)
    spread = []
    for r in range(8):
        row = raw[r : r + 1, :]
        high = jnp.where(mine, row >> 4, 0).astype(F32)
        low = jnp.where(mine, row & 15, 0).astype(F32)
        spread.append(jnp.concatenate([high, low], axis=0).astype(BF16))
    source = lax.broadcasted_iota(jnp.int32, (8 * L, L), 0) >> 3
    owner = lax.broadcasted_iota(jnp.int32, (8 * L, L), 1)
    got = nn(jnp.concatenate(spread, axis=1), ones_where(source == owner).astype(BF16))
    return (got[:8] * 16.0 + got[8:]).astype(jnp.int32)


def pack_kernel(par_ref, send_hbm, feat_hbm, prm_hbm, out_ref, idx_ref, send_ref, feat_ref, prm_ref, sems):
    copies = [
        pltpu.make_async_copy(src, dst, sems.at[n])
        for n, (src, dst) in enumerate(
            ((send_hbm, send_ref), (feat_hbm, feat_ref), (prm_hbm, prm_ref))
        )
    ]
    for copy in copies:
        copy.start()
    gauss = feat_ref.shape[0]
    copies[0].wait()
    first = par_ref[0] == 0
    idx = slot_rows(send_ref[...])
    idx_ref[...] = idx
    rows = jnp.where(first, idx[0:4, :], idx[4:8, :])
    cols = column_of(rows.astype(F32))
    lane = lax.broadcasted_iota(jnp.int32, (L, gauss), 1).astype(F32)
    hots = [ones_where(cols[:, c : c + 1] == lane).astype(BF16) for c in range(4)]
    copies[2].wait()
    copies[1].wait()
    got = nn(
        jnp.concatenate(hots, axis=0), jnp.concatenate(split2(feat_ref[...]), axis=1)
    )
    groups = gauss // L
    pieces = [prm_ref[:, g * L : (g + 1) * L] for g in range(groups)]
    pad = jnp.zeros((2, L), F32)
    stacked = jnp.concatenate([x for piece in pieces for x in (piece, pad)], axis=0)
    stack3 = jnp.concatenate(split3(stacked), axis=0)
    low_iota = lax.broadcasted_iota(jnp.int32, (L, L), 0)
    packed = []
    for c in range(4):
        part = got[c * L : c * L + L]
        out_ref[pl.ds(c, L, stride=FWD), :] = part[:, :L] + part[:, L:]
        row = rows[c : c + 1, :]
        low = ones_where((row & (L - 1)) == low_iota).astype(BF16)
        part = nn(stack3, low)
        span = groups * 8
        part = part[:span] + part[span : 2 * span] + part[2 * span :]
        total = jnp.zeros((8, L), F32)
        for g in range(groups):
            total = total + jnp.where((row >> 7) == g, part[g * 8 : g * 8 + 8], 0.0)
        packed.append(total)
    out_ref[pl.ds(4, L, stride=FWD), :] = column_of(jnp.concatenate(packed, axis=0))


def key_kernel(par_ref, lists_ref, weight_ref, row_ref, high_ref, low_ref):
    high_ref[...], low_ref[...] = split2(weight_ref[...])
    shift = par_ref[0] * 4
    tiles, length = lists_ref.shape
    slot_iota = lax.broadcasted_iota(jnp.int32, (8, length), 0)
    holder_iota = lax.broadcasted_iota(jnp.int32, (L, length), 0)
    place = lax.broadcasted_iota(jnp.int32, (8, length), 1)
    place_high = (place >> 4).astype(F32)
    place_low = (place & 15).astype(F32)
    total = jnp.zeros((32, L), F32)
    for t in range(tiles):
        entry = lists_ref[t : t + 1, :]
        holder = ones_where((entry >> 3) == holder_iota).astype(BF16)
        slot = ones_where(((entry + shift) & 7) == slot_iota)
        left = jnp.concatenate(
            [slot * (t + 1.0), slot * place_high, slot * place_low, jnp.zeros((8, length), F32)],
            axis=0,
        ).astype(BF16)
        total = total + nt(left, holder)
    tile = total[0:8]
    key = jnp.where(tile > 0.5, (tile - 1.0) * length + total[8:16] * 16.0 + total[16:24], -1.0)
    row_ref[...] = key


class Pool:
    def __init__(self, length, par_ref, ids_ref, keyrow_ref, prm_ref, own_ref, peer_ref):
        self.length, self.prm_ref = length, prm_ref
        stripe = par_ref[0]
        self.key = keyrow_ref[...]
        live = self.key >= 0.0
        self.tile = jnp.floor(self.key * (1.0 / length))
        self.ox = jnp.zeros((8, L), F32)
        self.oy = jnp.zeros((8, L), F32)
        for t in range(8):
            ident = ids_ref[t]
            here = self.tile == float(t)
            self.ox = jnp.where(here, ((ident & 127) * 16).astype(F32) + 0.5, self.ox)
            self.oy = jnp.where(
                here, ((ident >> 7) * 16 + stripe * 8).astype(F32) + 0.5, self.oy
            )
        self.base = jnp.where(live, self.tile * length, 1.0e9)
        self.live = ones_where(live)
        self.kx = lax.broadcasted_iota(jnp.int32, (16, L), 0).astype(F32)
        self.ky = lax.broadcasted_iota(jnp.int32, (8, L), 0).astype(F32)
        for side, ref in ((0, own_ref), (1, peer_ref)):
            prm_ref[side * 32 : side * 32 + 32, :] = ref[pl.ds(4, L, stride=FWD), :].T[0:32]

    def geometry(self, b):
        prm = self.prm_ref[b * 8 : b * 8 + 8, :]
        dx = (self.kx + self.ox[b : b + 1, :]) - prm[0:1]
        dy = (self.ky + self.oy[b : b + 1, :]) - prm[1:2]
        return prm, dx, dy

    def alphas(self, b):
        prm, dx, dy = self.geometry(b)
        ax = prm[2:3] * dx * dx
        cy = prm[4:5] * dy * dy
        bx = prm[3:4] * dx
        for j in range(8):
            power = -0.5 * (ax + cy[j : j + 1]) - bx * dy[j : j + 1]
            ex = self.live[b : b + 1, :] * jnp.exp(power)
            yield slice(j * 16, j * 16 + 16), ex, prm[5:6] * ex

    def fill_mask(self, mask_ref):
        cols = column_of(self.key)
        for a in range(8):
            front = jnp.broadcast_to(cols[:, a : a + 1], (L, L))
            for b in range(8):
                hit = (front < self.key[b : b + 1, :]) & (front >= self.base[b : b + 1, :])
                mask_ref[a * L : a * L + L, b * L : b * L + L] = ones_where(hit).astype(BF16)

    def spread(self, b, weights, high_ref, low_ref):
        cols = slice(b * L, b * L + L)
        high, low = split2(weights)
        for t in range(8):
            here = ones_where(self.tile[b : b + 1, :] == float(t))
            here = jnp.broadcast_to(here, (L, L)).astype(BF16)
            high_ref[t * L : t * L + L, cols] = high * here
            low_ref[t * L : t * L + L, cols] = low * here


def fill_features(own_ref, peer_ref, feat_ref):
    for side, ref in ((0, own_ref), (1, peer_ref)):
        for c in range(4):
            at = (side * 4 + c) * L
            high, low = split2(ref[pl.ds(c, L, stride=FWD), :])
            feat_ref[at : at + L, 0:L] = high
            feat_ref[at : at + L, L : 2 * L] = low


def front_kernel(
    length,
    par_ref,
    ids_ref,
    own_ref,
    peer_ref,
    keyrow_ref,
    teacher_ref,
    whigh_ref,
    wlow_ref,
    bias_ref,
    keep_ref,
    give_ref,
    trans_ref,
    grad_ref,
    mask_ref,
    prm_ref,
    feat_ref,
    alpha_ref,
    lk_ref,
    wm_hi,
    wm_lo,
    rt_ref,
    resid_hi,
    resid_lo,
):
    pool = Pool(length, par_ref, ids_ref, keyrow_ref, prm_ref, own_ref, peer_ref)
    fill_features(own_ref, peer_ref, feat_ref)
    pool.fill_mask(mask_ref)
    for b in range(8):
        cols = slice(b * L, b * L + L)
        for spot, ex, alpha in pool.alphas(b):
            high, low = split2(jnp.log1p(-alpha))
            alpha_ref[spot, cols] = alpha
            lk_ref[spot, cols] = high
            lk_ref[L + spot.start : L + spot.stop, cols] = low

    for b in range(0, 8, 2):
        both = nn(lk_ref[...], mask_ref[:, b * L : b * L + 2 * L])
        trans = jnp.exp(both[:L] + both[L:])
        trans_ref[:, b * L : b * L + 2 * L] = trans
        for q in range(2):
            cols = slice((b + q) * L, (b + q) * L + L)
            weights = trans[:, q * L : q * L + L] * alpha_ref[:, cols]
            pool.spread(b + q, weights, wm_hi, wm_lo)

    w_hi, w_lo = whigh_ref[...], wlow_ref[...]
    w_pair = jnp.concatenate([w_hi, w_hi], axis=0)
    w_both = jnp.concatenate([w_hi, w_lo], axis=0)
    width = whigh_ref.shape[1]
    squares = jnp.zeros((1, width), F32)
    bias_sum = jnp.zeros((1, width), F32)
    step = 2 * L
    for r in range(4):
        rows = slice(r * step, r * step + step)
        both = nn(wm_hi[rows, :], feat_ref[...])
        rendered = both[:, :L] + both[:, L:] + nn(wm_lo[rows, :], feat_ref[:, 0:L])
        high, low = split2(rendered)
        rt_hi, rt_lo = split2(rendered.T)
        rt_ref[0:L, rows] = rt_hi
        rt_ref[L : 2 * L, rows] = rt_lo
        decoded = nn(jnp.concatenate([high, low], axis=1), w_pair) + nn(high, w_lo)
        resid = decoded + bias_ref[...] - teacher_ref[rows, :]
        squares = squares + jnp.sum(resid * resid, axis=0, keepdims=True)
        bias_sum = bias_sum + jnp.sum(resid, axis=0, keepdims=True)
        high, low = split2(resid)
        resid_hi[rows, :] = high
        resid_lo[rows, :] = low
        both = nt(high, w_both)
        grad_ref[rows, :] = both[:, :L] + both[:, L:] + nt(low, w_hi)

    both = nn(rt_ref[...], resid_hi[...])
    grad_w = both[:L] + both[L:] + nn(rt_ref[0:L, :], resid_lo[...])
    sq_row = jnp.broadcast_to(jnp.sum(squares, axis=1, keepdims=True), (1, L))
    first = par_ref[0] == 0
    half = width // 2
    for ref, left in ((keep_ref, first), (give_ref, jnp.logical_not(first))):
        piece = jnp.where(left, grad_w[:, :half], grad_w[:, half:])
        ref[pl.ds(0, L, stride=GAT), :] = piece[:, :L]
        ref[pl.ds(1, L, stride=GAT), :] = piece[:, L:]
        piece = jnp.where(left, bias_sum[:, :half], bias_sum[:, half:])
        rows = jnp.concatenate([piece[:, :L], piece[:, L:], sq_row], axis=0)
        ref[pl.ds(2, L, stride=GAT), :] = column_of(rows)


def back_kernel(
    length,
    par_ref,
    ids_ref,
    own_ref,
    peer_ref,
    keyrow_ref,
    trans_ref,
    grad_ref,
    keep_ref,
    give_ref,
    mask_ref,
    prm_ref,
    feat_ref,
    feat2_ref,
    ex_ref,
    alpha_ref,
    lk_ref,
    wm_hi,
    wm_lo,
    drt_ref,
    dw_ref,
):
    pool = Pool(length, par_ref, ids_ref, keyrow_ref, prm_ref, own_ref, peer_ref)
    fill_features(own_ref, peer_ref, feat_ref)
    feat2_ref[:, 0:L] = feat_ref[:, 0:L]
    feat2_ref[:, L : 2 * L] = feat_ref[:, 0:L]
    pool.fill_mask(mask_ref)
    for b in range(8):
        cols = slice(b * L, b * L + L)
        for spot, ex, alpha in pool.alphas(b):
            ex_ref[spot, cols] = ex
            alpha_ref[spot, cols] = alpha
        pool.spread(b, trans_ref[:, cols] * alpha_ref[:, cols], wm_hi, wm_lo)

    dw_ref[...] = jnp.zeros(dw_ref.shape, F32)
    step = 2 * L
    for r in range(4):
        rows = slice(r * step, r * step + step)
        grad = grad_ref[rows, :]
        high, low = split2(grad)
        pair = jnp.concatenate([high, low], axis=1)
        dt_hi, dt_lo = split2(grad.T)
        drt_ref[0:L, rows] = dt_hi
        drt_ref[L : 2 * L, rows] = dt_lo
        for b in range(0, 8, 2):
            entries = slice(b * L, b * L + step)
            part = nt(pair, feat2_ref[entries, :]) + nt(high, feat_ref[entries, L : 2 * L])
            for q in range(2):
                cols = slice((b + q) * L, (b + q) * L + L)
                tile = pool.tile[b + q : b + q + 1, :]
                got = part[:, q * L : q * L + L]
                kept = jnp.where(tile == float(2 * r), got[:L], dw_ref[:, cols])
                dw_ref[:, cols] = jnp.where(tile == float(2 * r + 1), got[L:], kept)

    for b in range(8):
        cols = slice(b * L, b * L + L)
        high, low = split2(dw_ref[:, cols] * (trans_ref[:, cols] * alpha_ref[:, cols]))
        lk_ref[0:L, cols] = high
        lk_ref[L : 2 * L, cols] = low

    def total(value):
        return jnp.sum(value, axis=0, keepdims=True)

    blocks = []
    for b in range(0, 8, 2):
        wide = slice(b * L, b * L + step)
        both = nt(lk_ref[...], mask_ref[wide, :])
        alpha = alpha_ref[:, wide]
        dalpha = dw_ref[:, wide] * trans_ref[:, wide] - (both[:L] + both[L:]) / (1.0 - alpha)
        dpower = dalpha * alpha
        dopac = total(dalpha * ex_ref[:, wide])
        for q in range(2):
            prm, dx, dy = pool.geometry(b + q)
            flat = jnp.zeros((16, L), F32)
            by_y = jnp.zeros((16, L), F32)
            by_yy = jnp.zeros((16, L), F32)
            for j in range(8):
                part = dpower[j * 16 : j * 16 + 16, q * L : q * L + L]
                scaled = part * dy[j : j + 1]
                flat = flat + part
                by_y = by_y + scaled
                by_yy = by_yy + scaled * dy[j : j + 1]
            sx = total(flat * dx)
            sxx = total(flat * dx * dx)
            sy = total(by_y)
            sxy = total(by_y * dx)
            syy = total(by_yy)
            blocks += [
                prm[2:3] * sx + prm[3:4] * sy,
                prm[4:5] * sy + prm[3:4] * sx,
                -0.5 * sxx,
                -sxy,
                -0.5 * syy,
                dopac[:, q * L : q * L + L],
                jnp.zeros((2, L), F32),
            ]

    for side, ref in ((0, keep_ref), (1, give_ref)):
        for c in range(0, 4, 2):
            wide = slice((side * 4 + c) * L, (side * 4 + c) * L + step)
            both = nn(drt_ref[...], wm_hi[:, wide])
            grad = both[:L] + both[L:] + nn(drt_ref[0:L, :], wm_lo[:, wide])
            ref[pl.ds(c, L, stride=FWD), :] = grad[:, :L].T
            ref[pl.ds(c + 1, L, stride=FWD), :] = grad[:, L:].T
        rows = jnp.concatenate(blocks[side * 28 : side * 28 + 28], axis=0)
        ref[pl.ds(4, L, stride=FWD), :] = column_of(rows)


def compose_kernel(share_ref, keep_ref, give_ref, out_ref):
    for c in range(5):
        spot = pl.ds(c, L, stride=FWD)
        rows = keep_ref[spot, :] + give_ref[spot, :]
        if c == 4:
            small = jnp.sum(share_ref[pl.ds(2, L, stride=GAT), :], axis=0, keepdims=True)
            rows = rows + pltpu.roll(jnp.broadcast_to(small, (L, L)), 32, 1)
        out_ref[pl.ds(c, L, stride=RET), :] = rows
    for c in range(2):
        total = jnp.sum(share_ref[pl.ds(c, L, stride=GAT), :], axis=0, keepdims=True)
        out_ref[pl.ds(5 + c, L, stride=RET), :] = jnp.broadcast_to(total, (L, L))


def final_kernel(
    pixels, par_ref, idx_ref, own_ref, peer_ref, feat_ref, prm_ref, weight_ref, bias_ref, loss_ref
):
    gauss = feat_ref.shape[0]
    groups = gauss // L
    first = par_ref[0] == 0
    idx = idx_ref[...]
    top, bottom = idx[0:4], idx[4:8]
    idx = jnp.concatenate(
        [jnp.where(first, top, bottom), jnp.where(first, bottom, top)], axis=0
    )
    grads = []
    hots = []
    sub = lax.broadcasted_iota(jnp.int32, (gauss, L), 0)
    low_iota = lax.broadcasted_iota(jnp.int32, (L, L), 0)
    params = jnp.zeros((2 * groups * 8, L), F32)
    for side, ref in ((0, own_ref), (1, peer_ref)):
        prm = ref[pl.ds(4, L, stride=RET), :].T
        for c in range(4):
            b = side * 4 + c
            row = idx[b : b + 1]
            high, low = split2(ref[pl.ds(c, L, stride=RET), :])
            grads.append(jnp.concatenate([high, low], axis=1))
            hots.append(ones_where(row == sub).astype(BF16))
            block = prm[c * 8 : c * 8 + 8]
            spread = jnp.concatenate(
                [jnp.where((row >> 7) == g, block, 0.0) for g in range(groups)], axis=0
            )
            both = jnp.concatenate(split2(spread), axis=0)
            hot = ones_where((row & (L - 1)) == low_iota).astype(BF16)
            params = params + nt(both, hot)
    params = params[: groups * 8] + params[groups * 8 :]
    for g in range(groups):
        prm_ref[:, g * L : g * L + L] = params[g * 8 : g * 8 + 6]
    onehot = jnp.concatenate(hots, axis=1)
    both = nn(onehot, jnp.concatenate(grads, axis=0))
    feat_ref[...] = both[:, :L] + both[:, L:]

    width = weight_ref.shape[1]
    half = width // 2
    scale = 1.0 / pixels
    for ref, left in ((own_ref, first), (peer_ref, jnp.logical_not(first))):
        small = ref[pl.ds(4, L, stride=RET), :].T
        wide = [ref[pl.ds(5 + c, L, stride=RET), :] * scale for c in range(2)]
        row = jnp.concatenate([small[32:33], small[33:34]], axis=1) * scale
        wide = jnp.concatenate(wide, axis=1)

        def store(at):
            weight_ref[:, at : at + half] = wide
            bias_ref[:, at : at + half] = row

        pl.when(left)(functools.partial(store, 0))
        pl.when(jnp.logical_not(left))(functools.partial(store, half))
    loss_ref[...] = small[34:35, :] * (scale / width)


def call(kernel, shapes, specs, scratch=(), flops=0, limit=40):
    single = not isinstance(shapes, (list, tuple))
    count = 1 if single else len(shapes)
    cost = pl.CostEstimate(flops=flops, bytes_accessed=flops // 300, transcendentals=0)
    return pl.pallas_call(
        kernel,
        out_shape=shapes,
        in_specs=specs,
        out_specs=VMEM if single else [VMEM] * count,
        scratch_shapes=list(scratch),
        compiler_params=pltpu.CompilerParams(vmem_limit_bytes=limit * 1024 * 1024),
        cost_estimate=cost,
    )


def f32(*shape):
    return jax.ShapeDtypeStruct(shape, F32)


def bf16(*shape):
    return jax.ShapeDtypeStruct(shape, BF16)


def pack(par, send, features, gauss_params):
    shapes = [f32(FWD * L, L), jax.ShapeDtypeStruct((8, L), jnp.int32)]
    inputs = (send, features, gauss_params)
    scratch = [pltpu.VMEM(x.shape, x.dtype) for x in inputs]
    scratch.append(pltpu.SemaphoreType.DMA((3,)))
    return call(pack_kernel, shapes, [SMEM, HBM, HBM, HBM], scratch, flops=2 * 10**9, limit=62)(par, *inputs)


def keys(par, tile_lists, weight):
    shapes = [f32(8, L), bf16(*weight.shape), bf16(*weight.shape)]
    return call(key_kernel, shapes, [SMEM, VMEM, VMEM], flops=2 * 10**9)(par, tile_lists, weight)


def front(par, ids, own, peer, keyrow, teacher, whigh, wlow, bias, length):
    pixels, width = teacher.shape
    pool = 8 * L
    scratch = [
        pltpu.VMEM((pool, pool), BF16),
        pltpu.VMEM((64, L), F32),
        pltpu.VMEM((pool, 2 * L), BF16),
        pltpu.VMEM((L, pool), F32),
        pltpu.VMEM((2 * L, pool), BF16),
        pltpu.VMEM((pixels, pool), BF16),
        pltpu.VMEM((pixels, pool), BF16),
        pltpu.VMEM((2 * L, pixels), BF16),
        pltpu.VMEM((pixels, width), BF16),
        pltpu.VMEM((pixels, width), BF16),
    ]
    return call(
        functools.partial(front_kernel, float(length)),
        [f32(GAT * L, L), f32(GAT * L, L), f32(L, pool), f32(pixels, L)],
        [SMEM, SMEM] + [VMEM] * 7,
        scratch,
        flops=10**10,
    )(par, ids, own, peer, keyrow, teacher, whigh, wlow, bias)


def back(par, ids, own, peer, keyrow, trans, grad, length):
    pool = 8 * L
    pixels = grad.shape[0]
    scratch = [
        pltpu.VMEM((pool, pool), BF16),
        pltpu.VMEM((64, L), F32),
        pltpu.VMEM((pool, 2 * L), BF16),
        pltpu.VMEM((pool, 2 * L), BF16),
        pltpu.VMEM((L, pool), F32),
        pltpu.VMEM((L, pool), F32),
        pltpu.VMEM((2 * L, pool), BF16),
        pltpu.VMEM((pixels, pool), BF16),
        pltpu.VMEM((pixels, pool), BF16),
        pltpu.VMEM((2 * L, pixels), BF16),
        pltpu.VMEM((L, pool), F32),
    ]
    return call(
        functools.partial(back_kernel, float(length)),
        [f32(FWD * L, L), f32(FWD * L, L)],
        [SMEM, SMEM] + [VMEM] * 5,
        scratch,
        flops=8 * 10**9,
    )(par, ids, own, peer, keyrow, trans, grad)


def compose(share, keep, give):
    return call(compose_kernel, f32(RET * L, L), [VMEM] * 3, flops=10**9)(share, keep, give)


def final(par, idx, own, peer, gauss, width, pixels):
    return call(
        functools.partial(final_kernel, float(pixels)),
        [f32(gauss, L), f32(6, gauss), f32(L, width), f32(1, width), f32(1, L)],
        [SMEM, VMEM, VMEM, VMEM],
        flops=4 * 10**9,
    )(par, idx, own, peer)


def swap(value):
    return lax.ppermute(value, "px", SWAP)


def exchange(value, rows):
    sent = value.reshape(L, 1, rows * L)
    return lax.all_to_all(sent, "gs", split_axis=0, concat_axis=0, tiled=True).reshape(rows * L, L)


def per_device(
    features, gauss_params, send_index, tile_ids, tile_lists, teacher, decoder_weight, decoder_bias
):
    holders = lax.axis_size("gs")
    par = lax.axis_index("px").astype(jnp.int32).reshape(1)
    width = teacher.shape[2]
    sent, idx = pack(par, send_index.reshape(8, -1), features, gauss_params)
    sent, tile_lists, decoder_weight, teacher = lax.optimization_barrier(
        (sent, tile_lists, decoder_weight, teacher)
    )
    got = exchange(sent, FWD)
    prepared = keys(par, tile_lists, decoder_weight)
    got, (keyrow, whigh, wlow) = lax.optimization_barrier((got, prepared))
    peer = swap(got)
    length = tile_lists.shape[1]
    flat_teacher = teacher.reshape(-1, width)
    bias = decoder_bias.reshape(1, -1)
    keep, give, trans, grad = front(
        par, tile_ids, got, peer, keyrow, flat_teacher, whigh, wlow, bias, length
    )
    part, trans, grad = lax.optimization_barrier((keep + swap(give), trans, grad))
    share = exchange(part, GAT)
    keep, give = back(par, tile_ids, got, peer, keyrow, trans, grad, length)
    ret = exchange(compose(share, keep, swap(give)), RET)
    pixels = holders * tile_ids.shape[0] * 256
    grad_features, grad_params, grad_weight, grad_bias, loss = final(
        par, idx, ret, swap(ret), features.shape[0], width, pixels
    )
    return grad_features, grad_params, grad_weight, grad_bias.reshape(-1), loss[0, 0]


def solution(mesh):
    return jax.shard_map(
        per_device,
        mesh=mesh,
        in_specs=(
            P("gs", None),
            P(None, "gs"),
            P("gs"),
            P("gs"),
            P("gs", None),
            P("gs", "px", None),
            P(),
            P(),
        ),
        out_specs=(P("gs", None), P(None, "gs"), P(), P(), P()),
        check_vma=False,
    )
```

```python
import functools

import jax
import jax.numpy as jnp
from jax import lax
from jax.experimental import pallas as pl
from jax.experimental.pallas import tpu as pltpu
from jax.sharding import PartitionSpec as P

F32 = jnp.float32
BF16 = jnp.bfloat16
L = 128
SWAP = [(0, 1), (1, 0)]
FWD = 5
RET = 7
GAT = 3
VMEM = pl.BlockSpec(memory_space=pltpu.VMEM)
SMEM = pl.BlockSpec(memory_space=pltpu.SMEM)
HBM = pl.BlockSpec(memory_space=pltpu.HBM)


def nn(lhs, rhs):
    return lax.dot_general(lhs, rhs, (((1,), (0,)), ((), ())), preferred_element_type=F32)


def nt(lhs, rhs):
    return lax.dot_general(lhs, rhs, (((1,), (1,)), ((), ())), preferred_element_type=F32)


def split2(value):
    high = value.astype(BF16)
    return high, (value - high.astype(F32)).astype(BF16)


def split3(value):
    high = value.astype(BF16)
    rest = value - high.astype(F32)
    mid = rest.astype(BF16)
    return high, mid, (rest - mid.astype(F32)).astype(BF16)


def ones_where(mask):
    return jnp.where(mask, 1.0, 0.0).astype(F32)


def column_of(rows):
    pad = jnp.zeros((L - rows.shape[0], L), F32)
    return jnp.concatenate([rows, pad], axis=0).T


def slot_rows(raw):
    slot = lax.broadcasted_iota(jnp.int32, (8, L), 1) & 7
    mine = slot == lax.broadcasted_iota(jnp.int32, (8, L), 0)
    spread = []
    for r in range(8):
        row = raw[r : r + 1, :]
        high = jnp.where(mine, row >> 4, 0).astype(F32)
        low = jnp.where(mine, row & 15, 0).astype(F32)
        spread.append(jnp.concatenate([high, low], axis=0).astype(BF16))
    source = lax.broadcasted_iota(jnp.int32, (8 * L, L), 0) >> 3
    owner = lax.broadcasted_iota(jnp.int32, (8 * L, L), 1)
    got = nn(jnp.concatenate(spread, axis=1), ones_where(source == owner).astype(BF16))
    return (got[:8] * 16.0 + got[8:]).astype(jnp.int32)


def pack_kernel(par_ref, send_hbm, feat_hbm, prm_hbm, out_ref, idx_ref, send_ref, feat_ref, prm_ref, sems):
    copies = [
        pltpu.make_async_copy(src, dst, sems.at[n])
        for n, (src, dst) in enumerate(
            ((send_hbm, send_ref), (feat_hbm, feat_ref), (prm_hbm, prm_ref))
        )
    ]
    for copy in copies:
        copy.start()
    gauss = feat_ref.shape[0]
    copies[0].wait()
    first = par_ref[0] == 0
    idx = slot_rows(send_ref[...])
    idx_ref[...] = idx
    rows = jnp.where(first, idx[0:4, :], idx[4:8, :])
    cols = column_of(rows.astype(F32))
    lane = lax.broadcasted_iota(jnp.int32, (L, gauss), 1).astype(F32)
    hots = [ones_where(cols[:, c : c + 1] == lane).astype(BF16) for c in range(4)]
    copies[2].wait()
    copies[1].wait()
    got = nn(
        jnp.concatenate(hots, axis=0), jnp.concatenate(split2(feat_ref[...]), axis=1)
    )
    groups = gauss // L
    pieces = [prm_ref[:, g * L : (g + 1) * L] for g in range(groups)]
    pad = jnp.zeros((2, L), F32)
    stacked = jnp.concatenate([x for piece in pieces for x in (piece, pad)], axis=0)
    stack3 = jnp.concatenate(split3(stacked), axis=0)
    low_iota = lax.broadcasted_iota(jnp.int32, (L, L), 0)
    packed = []
    for c in range(4):
        part = got[c * L : c * L + L]
        out_ref[pl.ds(c, L, stride=FWD), :] = part[:, :L] + part[:, L:]
        row = rows[c : c + 1, :]
        low = ones_where((row & (L - 1)) == low_iota).astype(BF16)
        part = nn(stack3, low)
        span = groups * 8
        part = part[:span] + part[span : 2 * span] + part[2 * span :]
        total = jnp.zeros((8, L), F32)
        for g in range(groups):
            total = total + jnp.where((row >> 7) == g, part[g * 8 : g * 8 + 8], 0.0)
        packed.append(total)
    out_ref[pl.ds(4, L, stride=FWD), :] = column_of(jnp.concatenate(packed, axis=0))


def key_kernel(par_ref, lists_ref, weight_ref, row_ref, high_ref, low_ref):
    high_ref[...], low_ref[...] = split2(weight_ref[...])
    shift = par_ref[0] * 4
    tiles, length = lists_ref.shape
    slot_iota = lax.broadcasted_iota(jnp.int32, (8, length), 0)
    holder_iota = lax.broadcasted_iota(jnp.int32, (L, length), 0)
    place = lax.broadcasted_iota(jnp.int32, (8, length), 1)
    place_high = (place >> 4).astype(F32)
    place_low = (place & 15).astype(F32)
    total = jnp.zeros((32, L), F32)
    for t in range(tiles):
        entry = lists_ref[t : t + 1, :]
        holder = ones_where((entry >> 3) == holder_iota).astype(BF16)
        slot = ones_where(((entry + shift) & 7) == slot_iota)
        left = jnp.concatenate(
            [slot * (t + 1.0), slot * place_high, slot * place_low, jnp.zeros((8, length), F32)],
            axis=0,
        ).astype(BF16)
        total = total + nt(left, holder)
    tile = total[0:8]
    key = jnp.where(tile > 0.5, (tile - 1.0) * length + total[8:16] * 16.0 + total[16:24], -1.0)
    row_ref[...] = key


class Pool:
    def __init__(self, length, par_ref, ids_ref, keyrow_ref, prm_ref, sides):
        self.length, self.prm_ref = length, prm_ref
        stripe = par_ref[0]
        self.key = keyrow_ref[...]
        live = self.key >= 0.0
        self.tile = jnp.floor(self.key * (1.0 / length))
        self.ox = jnp.zeros((8, L), F32)
        self.oy = jnp.zeros((8, L), F32)
        for t in range(8):
            ident = ids_ref[t]
            here = self.tile == float(t)
            self.ox = jnp.where(here, ((ident & 127) * 16).astype(F32) + 0.5, self.ox)
            self.oy = jnp.where(
                here, ((ident >> 7) * 16 + stripe * 8).astype(F32) + 0.5, self.oy
            )
        self.base = jnp.where(live, self.tile * length, 1.0e9)
        self.live = ones_where(live)
        self.kx = lax.broadcasted_iota(jnp.int32, (16, L), 0).astype(F32)
        self.ky = lax.broadcasted_iota(jnp.int32, (8, L), 0).astype(F32)
        for side, ref in sides:
            prm_ref[side * 32 : side * 32 + 32, :] = ref[pl.ds(4, L, stride=FWD), :].T[0:32]

    def geometry(self, b):
        prm = self.prm_ref[b * 8 : b * 8 + 8, :]
        dx = (self.kx + self.ox[b : b + 1, :]) - prm[0:1]
        dy = (self.ky + self.oy[b : b + 1, :]) - prm[1:2]
        return prm, dx, dy

    def alphas(self, b):
        prm, dx, dy = self.geometry(b)
        ax = prm[2:3] * dx * dx
        cy = prm[4:5] * dy * dy
        bx = prm[3:4] * dx
        for j in range(8):
            power = -0.5 * (ax + cy[j : j + 1]) - bx * dy[j : j + 1]
            ex = self.live[b : b + 1, :] * jnp.exp(power)
            yield slice(j * 16, j * 16 + 16), ex, prm[5:6] * ex

    def fill_mask(self, mask_ref):
        cols = column_of(self.key)
        for a in range(8):
            front = jnp.broadcast_to(cols[:, a : a + 1], (L, L))
            for b in range(8):
                hit = (front < self.key[b : b + 1, :]) & (front >= self.base[b : b + 1, :])
                mask_ref[a * L : a * L + L, b * L : b * L + L] = ones_where(hit).astype(BF16)

    def spread(self, b, weights, high_ref, low_ref):
        cols = slice(b * L, b * L + L)
        high, low = split2(weights)
        for t in range(8):
            here = ones_where(self.tile[b : b + 1, :] == float(t))
            here = jnp.broadcast_to(here, (L, L)).astype(BF16)
            high_ref[t * L : t * L + L, cols] = high * here
            low_ref[t * L : t * L + L, cols] = low * here


def fill_features(own_ref, peer_ref, feat_ref):
    for side, ref in ((0, own_ref), (1, peer_ref)):
        for c in range(4):
            at = (side * 4 + c) * L
            high, low = split2(ref[pl.ds(c, L, stride=FWD), :])
            feat_ref[at : at + L, 0:L] = high
            feat_ref[at : at + L, L : 2 * L] = low


def fill_logs(pool, b, alpha_ref, lk_ref):
    cols = slice(b * L, b * L + L)
    for spot, ex, alpha in pool.alphas(b):
        high, low = split2(jnp.log1p(-alpha))
        alpha_ref[spot, cols] = alpha
        lk_ref[spot, cols] = high
        lk_ref[L + spot.start : L + spot.stop, cols] = low


def ready_kernel(
    length, par_ref, ids_ref, own_ref, keyrow_ref, mask_ref, alpha_ref, lk_ref, prm_ref
):
    pool = Pool(length, par_ref, ids_ref, keyrow_ref, prm_ref, ((0, own_ref),))
    pool.fill_mask(mask_ref)
    for b in range(4):
        fill_logs(pool, b, alpha_ref, lk_ref)


def front_kernel(
    length,
    par_ref,
    ids_ref,
    own_ref,
    peer_ref,
    keyrow_ref,
    mask_ref,
    half_alpha_ref,
    half_lk_ref,
    teacher_ref,
    whigh_ref,
    wlow_ref,
    bias_ref,
    keep_ref,
    give_ref,
    trans_ref,
    grad_ref,
    prm_ref,
    feat_ref,
    alpha_ref,
    lk_ref,
    wm_hi,
    wm_lo,
    rt_ref,
    resid_hi,
    resid_lo,
):
    pool = Pool(
        length, par_ref, ids_ref, keyrow_ref, prm_ref, ((0, own_ref), (1, peer_ref))
    )
    fill_features(own_ref, peer_ref, feat_ref)
    half = 4 * L
    alpha_ref[:, 0:half] = half_alpha_ref[...]
    lk_ref[:, 0:half] = half_lk_ref[...]
    for b in range(4, 8):
        fill_logs(pool, b, alpha_ref, lk_ref)

    for b in range(0, 8, 2):
        both = nn(lk_ref[...], mask_ref[:, b * L : b * L + 2 * L])
        trans = jnp.exp(both[:L] + both[L:])
        trans_ref[:, b * L : b * L + 2 * L] = trans
        for q in range(2):
            cols = slice((b + q) * L, (b + q) * L + L)
            weights = trans[:, q * L : q * L + L] * alpha_ref[:, cols]
            pool.spread(b + q, weights, wm_hi, wm_lo)

    w_hi, w_lo = whigh_ref[...], wlow_ref[...]
    w_pair = jnp.concatenate([w_hi, w_hi], axis=0)
    w_both = jnp.concatenate([w_hi, w_lo], axis=0)
    width = whigh_ref.shape[1]
    squares = jnp.zeros((1, width), F32)
    bias_sum = jnp.zeros((1, width), F32)
    step = 2 * L
    for r in range(4):
        rows = slice(r * step, r * step + step)
        both = nn(wm_hi[rows, :], feat_ref[...])
        rendered = both[:, :L] + both[:, L:] + nn(wm_lo[rows, :], feat_ref[:, 0:L])
        high, low = split2(rendered)
        rt_hi, rt_lo = split2(rendered.T)
        rt_ref[0:L, rows] = rt_hi
        rt_ref[L : 2 * L, rows] = rt_lo
        decoded = nn(jnp.concatenate([high, low], axis=1), w_pair) + nn(high, w_lo)
        resid = decoded + bias_ref[...] - teacher_ref[rows, :]
        squares = squares + jnp.sum(resid * resid, axis=0, keepdims=True)
        bias_sum = bias_sum + jnp.sum(resid, axis=0, keepdims=True)
        high, low = split2(resid)
        resid_hi[rows, :] = high
        resid_lo[rows, :] = low
        both = nt(high, w_both)
        grad_ref[rows, :] = both[:, :L] + both[:, L:] + nt(low, w_hi)

    both = nn(rt_ref[...], resid_hi[...])
    grad_w = both[:L] + both[L:] + nn(rt_ref[0:L, :], resid_lo[...])
    sq_row = jnp.broadcast_to(jnp.sum(squares, axis=1, keepdims=True), (1, L))
    first = par_ref[0] == 0
    half = width // 2
    for ref, left in ((keep_ref, first), (give_ref, jnp.logical_not(first))):
        piece = jnp.where(left, grad_w[:, :half], grad_w[:, half:])
        ref[pl.ds(0, L, stride=GAT), :] = piece[:, :L]
        ref[pl.ds(1, L, stride=GAT), :] = piece[:, L:]
        piece = jnp.where(left, bias_sum[:, :half], bias_sum[:, half:])
        rows = jnp.concatenate([piece[:, :L], piece[:, L:], sq_row], axis=0)
        ref[pl.ds(2, L, stride=GAT), :] = column_of(rows)


def back_kernel(
    length,
    par_ref,
    ids_ref,
    own_ref,
    peer_ref,
    keyrow_ref,
    trans_ref,
    grad_ref,
    keep_ref,
    give_ref,
    mask_ref,
    prm_ref,
    feat_ref,
    feat2_ref,
    ex_ref,
    alpha_ref,
    lk_ref,
    wm_hi,
    wm_lo,
    drt_ref,
    dw_ref,
):
    pool = Pool(
        length, par_ref, ids_ref, keyrow_ref, prm_ref, ((0, own_ref), (1, peer_ref))
    )
    fill_features(own_ref, peer_ref, feat_ref)
    feat2_ref[:, 0:L] = feat_ref[:, 0:L]
    feat2_ref[:, L : 2 * L] = feat_ref[:, 0:L]
    pool.fill_mask(mask_ref)
    for b in range(8):
        cols = slice(b * L, b * L + L)
        for spot, ex, alpha in pool.alphas(b):
            ex_ref[spot, cols] = ex
            alpha_ref[spot, cols] = alpha
        pool.spread(b, trans_ref[:, cols] * alpha_ref[:, cols], wm_hi, wm_lo)

    dw_ref[...] = jnp.zeros(dw_ref.shape, F32)
    step = 2 * L
    for r in range(4):
        rows = slice(r * step, r * step + step)
        grad = grad_ref[rows, :]
        high, low = split2(grad)
        pair = jnp.concatenate([high, low], axis=1)
        dt_hi, dt_lo = split2(grad.T)
        drt_ref[0:L, rows] = dt_hi
        drt_ref[L : 2 * L, rows] = dt_lo
        for b in range(0, 8, 2):
            entries = slice(b * L, b * L + step)
            part = nt(pair, feat2_ref[entries, :]) + nt(high, feat_ref[entries, L : 2 * L])
            for q in range(2):
                cols = slice((b + q) * L, (b + q) * L + L)
                tile = pool.tile[b + q : b + q + 1, :]
                got = part[:, q * L : q * L + L]
                kept = jnp.where(tile == float(2 * r), got[:L], dw_ref[:, cols])
                dw_ref[:, cols] = jnp.where(tile == float(2 * r + 1), got[L:], kept)

    for b in range(8):
        cols = slice(b * L, b * L + L)
        high, low = split2(dw_ref[:, cols] * (trans_ref[:, cols] * alpha_ref[:, cols]))
        lk_ref[0:L, cols] = high
        lk_ref[L : 2 * L, cols] = low

    def total(value):
        return jnp.sum(value, axis=0, keepdims=True)

    blocks = []
    for b in range(0, 8, 2):
        wide = slice(b * L, b * L + step)
        both = nt(lk_ref[...], mask_ref[wide, :])
        alpha = alpha_ref[:, wide]
        dalpha = dw_ref[:, wide] * trans_ref[:, wide] - (both[:L] + both[L:]) / (1.0 - alpha)
        dpower = dalpha * alpha
        dopac = total(dalpha * ex_ref[:, wide])
        for q in range(2):
            prm, dx, dy = pool.geometry(b + q)
            flat = jnp.zeros((16, L), F32)
            by_y = jnp.zeros((16, L), F32)
            by_yy = jnp.zeros((16, L), F32)
            for j in range(8):
                part = dpower[j * 16 : j * 16 + 16, q * L : q * L + L]
                scaled = part * dy[j : j + 1]
                flat = flat + part
                by_y = by_y + scaled
                by_yy = by_yy + scaled * dy[j : j + 1]
            sx = total(flat * dx)
            sxx = total(flat * dx * dx)
            sy = total(by_y)
            sxy = total(by_y * dx)
            syy = total(by_yy)
            blocks += [
                prm[2:3] * sx + prm[3:4] * sy,
                prm[4:5] * sy + prm[3:4] * sx,
                -0.5 * sxx,
                -sxy,
                -0.5 * syy,
                dopac[:, q * L : q * L + L],
                jnp.zeros((2, L), F32),
            ]

    for side, ref in ((0, keep_ref), (1, give_ref)):
        for c in range(0, 4, 2):
            wide = slice((side * 4 + c) * L, (side * 4 + c) * L + step)
            both = nn(drt_ref[...], wm_hi[:, wide])
            grad = both[:L] + both[L:] + nn(drt_ref[0:L, :], wm_lo[:, wide])
            ref[pl.ds(c, L, stride=FWD), :] = grad[:, :L].T
            ref[pl.ds(c + 1, L, stride=FWD), :] = grad[:, L:].T
        rows = jnp.concatenate(blocks[side * 28 : side * 28 + 28], axis=0)
        ref[pl.ds(4, L, stride=FWD), :] = column_of(rows)


def compose_kernel(share_ref, keep_ref, give_ref, out_ref):
    for c in range(5):
        spot = pl.ds(c, L, stride=FWD)
        rows = keep_ref[spot, :] + give_ref[spot, :]
        if c == 4:
            small = jnp.sum(share_ref[pl.ds(2, L, stride=GAT), :], axis=0, keepdims=True)
            rows = rows + pltpu.roll(jnp.broadcast_to(small, (L, L)), 32, 1)
        out_ref[pl.ds(c, L, stride=RET), :] = rows
    for c in range(2):
        total = jnp.sum(share_ref[pl.ds(c, L, stride=GAT), :], axis=0, keepdims=True)
        out_ref[pl.ds(5 + c, L, stride=RET), :] = jnp.broadcast_to(total, (L, L))


def place_kernel(par_ref, idx_ref, own_ref, feat_ref, prm_ref, hot_ref):
    gauss = feat_ref.shape[0]
    first = par_ref[0] == 0
    idx = idx_ref[...]
    top, bottom = idx[0:4], idx[4:8]
    sub = lax.broadcasted_iota(jnp.int32, (gauss, L), 0)
    other = jnp.where(first, bottom, top)
    for c in range(4):
        hot_ref[:, c * L : c * L + L] = ones_where(other[c : c + 1] == sub).astype(BF16)
    mine = jnp.where(first, top, bottom)
    hots = [ones_where(mine[c : c + 1] == sub).astype(BF16) for c in range(4)]
    feat_ref[...] = place_features(own_ref, jnp.concatenate(hots, axis=1))
    prm_ref[...] = place_params(own_ref, mine, gauss // L)


def place_features(ref, onehot):
    grads = [
        jnp.concatenate(split2(ref[pl.ds(c, L, stride=RET), :]), axis=1) for c in range(4)
    ]
    both = nn(onehot, jnp.concatenate(grads, axis=0))
    return both[:, :L] + both[:, L:]


def place_params(ref, idx, groups):
    low_iota = lax.broadcasted_iota(jnp.int32, (L, L), 0)
    prm = ref[pl.ds(4, L, stride=RET), :].T
    params = jnp.zeros((2 * groups * 8, L), F32)
    for c in range(4):
        row = idx[c : c + 1]
        block = prm[c * 8 : c * 8 + 8]
        spread = jnp.concatenate(
            [jnp.where((row >> 7) == g, block, 0.0) for g in range(groups)], axis=0
        )
        both = jnp.concatenate(split2(spread), axis=0)
        hot = ones_where((row & (L - 1)) == low_iota).astype(BF16)
        params = params + nt(both, hot)
    return params[: groups * 8] + params[groups * 8 :]


def final_kernel(
    pixels,
    par_ref,
    idx_ref,
    own_ref,
    peer_ref,
    part_feat_ref,
    part_prm_ref,
    hot_ref,
    feat_ref,
    prm_ref,
    weight_ref,
    bias_ref,
    loss_ref,
):
    first = par_ref[0] == 0
    feat_ref[...] = part_feat_ref[...] + place_features(peer_ref, hot_ref[...])
    groups = feat_ref.shape[0] // L
    idx = idx_ref[...]
    other = jnp.where(first, idx[4:8], idx[0:4])
    params = part_prm_ref[...] + place_params(peer_ref, other, groups)
    for g in range(groups):
        prm_ref[:, g * L : g * L + L] = params[g * 8 : g * 8 + 6]

    width = weight_ref.shape[1]
    half = width // 2
    scale = 1.0 / pixels
    for ref, left in ((own_ref, first), (peer_ref, jnp.logical_not(first))):
        small = ref[pl.ds(4, L, stride=RET), :].T
        wide = [ref[pl.ds(5 + c, L, stride=RET), :] * scale for c in range(2)]
        row = jnp.concatenate([small[32:33], small[33:34]], axis=1) * scale
        wide = jnp.concatenate(wide, axis=1)

        def store(at):
            weight_ref[:, at : at + half] = wide
            bias_ref[:, at : at + half] = row

        pl.when(left)(functools.partial(store, 0))
        pl.when(jnp.logical_not(left))(functools.partial(store, half))
    loss_ref[...] = small[34:35, :] * (scale / width)


def call(kernel, shapes, specs, scratch=(), flops=0, limit=40):
    single = not isinstance(shapes, (list, tuple))
    count = 1 if single else len(shapes)
    cost = pl.CostEstimate(flops=flops, bytes_accessed=flops // 300, transcendentals=0)
    return pl.pallas_call(
        kernel,
        out_shape=shapes,
        in_specs=specs,
        out_specs=VMEM if single else [VMEM] * count,
        scratch_shapes=list(scratch),
        compiler_params=pltpu.CompilerParams(vmem_limit_bytes=limit * 1024 * 1024),
        cost_estimate=cost,
    )


def f32(*shape):
    return jax.ShapeDtypeStruct(shape, F32)


def bf16(*shape):
    return jax.ShapeDtypeStruct(shape, BF16)


def pack(par, send, features, gauss_params):
    shapes = [f32(FWD * L, L), jax.ShapeDtypeStruct((8, L), jnp.int32)]
    inputs = (send, features, gauss_params)
    scratch = [pltpu.VMEM(x.shape, x.dtype) for x in inputs]
    scratch.append(pltpu.SemaphoreType.DMA((3,)))
    return call(pack_kernel, shapes, [SMEM, HBM, HBM, HBM], scratch, flops=2 * 10**9, limit=62)(par, *inputs)


def keys(par, tile_lists, weight):
    shapes = [f32(8, L), bf16(*weight.shape), bf16(*weight.shape)]
    return call(key_kernel, shapes, [SMEM, VMEM, VMEM], flops=2 * 10**9)(par, tile_lists, weight)


def ready(par, ids, own, keyrow, length):
    pool = 8 * L
    return call(
        functools.partial(ready_kernel, float(length)),
        [bf16(pool, pool), f32(L, pool // 2), bf16(2 * L, pool // 2)],
        [SMEM, SMEM, VMEM, VMEM],
        [pltpu.VMEM((64, L), F32)],
        flops=10**9,
    )(par, ids, own, keyrow)


def front(par, ids, own, peer, keyrow, halves, teacher, whigh, wlow, bias, length):
    pixels, width = teacher.shape
    pool = 8 * L
    scratch = [
        pltpu.VMEM((64, L), F32),
        pltpu.VMEM((pool, 2 * L), BF16),
        pltpu.VMEM((L, pool), F32),
        pltpu.VMEM((2 * L, pool), BF16),
        pltpu.VMEM((pixels, pool), BF16),
        pltpu.VMEM((pixels, pool), BF16),
        pltpu.VMEM((2 * L, pixels), BF16),
        pltpu.VMEM((pixels, width), BF16),
        pltpu.VMEM((pixels, width), BF16),
    ]
    return call(
        functools.partial(front_kernel, float(length)),
        [f32(GAT * L, L), f32(GAT * L, L), f32(L, pool), f32(pixels, L)],
        [SMEM, SMEM] + [VMEM] * 10,
        scratch,
        flops=10**10,
    )(par, ids, own, peer, keyrow, *halves, teacher, whigh, wlow, bias)


def back(par, ids, own, peer, keyrow, trans, grad, length):
    pool = 8 * L
    pixels = grad.shape[0]
    scratch = [
        pltpu.VMEM((pool, pool), BF16),
        pltpu.VMEM((64, L), F32),
        pltpu.VMEM((pool, 2 * L), BF16),
        pltpu.VMEM((pool, 2 * L), BF16),
        pltpu.VMEM((L, pool), F32),
        pltpu.VMEM((L, pool), F32),
        pltpu.VMEM((2 * L, pool), BF16),
        pltpu.VMEM((pixels, pool), BF16),
        pltpu.VMEM((pixels, pool), BF16),
        pltpu.VMEM((2 * L, pixels), BF16),
        pltpu.VMEM((L, pool), F32),
    ]
    return call(
        functools.partial(back_kernel, float(length)),
        [f32(FWD * L, L), f32(FWD * L, L)],
        [SMEM, SMEM] + [VMEM] * 5,
        scratch,
        flops=8 * 10**9,
    )(par, ids, own, peer, keyrow, trans, grad)


def compose(share, keep, give):
    return call(compose_kernel, f32(RET * L, L), [VMEM] * 3, flops=10**9)(share, keep, give)


def place(par, idx, own, gauss):
    return call(
        place_kernel,
        [f32(gauss, L), f32(gauss // L * 8, L), bf16(gauss, 4 * L)],
        [SMEM, VMEM, VMEM],
        flops=10**9,
    )(par, idx, own)


def final(par, idx, own, peer, parts, width, pixels):
    gauss = parts[0].shape[0]
    return call(
        functools.partial(final_kernel, float(pixels)),
        [f32(gauss, L), f32(6, gauss), f32(L, width), f32(1, width), f32(1, L)],
        [SMEM] + [VMEM] * 6,
        flops=2 * 10**9,
    )(par, idx, own, peer, *parts)


def swap(value):
    return lax.ppermute(value, "px", SWAP)


def exchange(value, rows):
    sent = value.reshape(L, 1, rows * L)
    return lax.all_to_all(sent, "gs", split_axis=0, concat_axis=0, tiled=True).reshape(rows * L, L)


def per_device(
    features, gauss_params, send_index, tile_ids, tile_lists, teacher, decoder_weight, decoder_bias
):
    holders = lax.axis_size("gs")
    par = lax.axis_index("px").astype(jnp.int32).reshape(1)
    width = teacher.shape[2]
    sent, idx = pack(par, send_index.reshape(8, -1), features, gauss_params)
    sent, tile_lists, decoder_weight, teacher = lax.optimization_barrier(
        (sent, tile_lists, decoder_weight, teacher)
    )
    got = exchange(sent, FWD)
    prepared = keys(par, tile_lists, decoder_weight)
    got, (keyrow, whigh, wlow) = lax.optimization_barrier((got, prepared))
    peer = swap(got)
    length = tile_lists.shape[1]
    halves = ready(par, tile_ids, got, keyrow, length)
    flat_teacher = teacher.reshape(-1, width)
    bias = decoder_bias.reshape(1, -1)
    keep, give, trans, grad = front(
        par, tile_ids, got, peer, keyrow, halves, flat_teacher, whigh, wlow, bias, length
    )
    part, trans, grad = lax.optimization_barrier((keep + swap(give), trans, grad))
    share = exchange(part, GAT)
    keep, give = back(par, tile_ids, got, peer, keyrow, trans, grad, length)
    ret = exchange(compose(share, keep, swap(give)), RET)
    other = swap(ret)
    parts = place(par, idx, ret, features.shape[0])
    pixels = holders * tile_ids.shape[0] * 256
    grad_features, grad_params, grad_weight, grad_bias, loss = final(
        par, idx, ret, other, parts, width, pixels
    )
    return grad_features, grad_params, grad_weight, grad_bias.reshape(-1), loss[0, 0]


def solution(mesh):
    return jax.shard_map(
        per_device,
        mesh=mesh,
        in_specs=(
            P("gs", None),
            P(None, "gs"),
            P("gs"),
            P("gs"),
            P("gs", None),
            P("gs", "px", None),
            P(),
            P(),
        ),
        out_specs=(P("gs", None), P(None, "gs"), P(), P(), P()),
        check_vma=False,
    )
```

```python
import functools

import jax
import jax.numpy as jnp
from jax import lax
from jax.experimental import pallas as pl
from jax.experimental.pallas import tpu as pltpu
from jax.sharding import PartitionSpec as P

F32 = jnp.float32
BF16 = jnp.bfloat16
L = 128
SWAP = [(0, 1), (1, 0)]
FWD = 5
RET = 7
GAT = 3
VMEM = pl.BlockSpec(memory_space=pltpu.VMEM)
SMEM = pl.BlockSpec(memory_space=pltpu.SMEM)
HBM = pl.BlockSpec(memory_space=pltpu.HBM)


def nn(lhs, rhs):
    return lax.dot_general(lhs, rhs, (((1,), (0,)), ((), ())), preferred_element_type=F32)


def nt(lhs, rhs):
    return lax.dot_general(lhs, rhs, (((1,), (1,)), ((), ())), preferred_element_type=F32)


def split2(value):
    high = value.astype(BF16)
    return high, (value - high.astype(F32)).astype(BF16)


def split3(value):
    high = value.astype(BF16)
    rest = value - high.astype(F32)
    mid = rest.astype(BF16)
    return high, mid, (rest - mid.astype(F32)).astype(BF16)


def ones_where(mask):
    return jnp.where(mask, 1.0, 0.0).astype(F32)


def column_of(rows):
    pad = jnp.zeros((L - rows.shape[0], L), F32)
    return jnp.concatenate([rows, pad], axis=0).T


def slot_rows(raw):
    slot = lax.broadcasted_iota(jnp.int32, (8, L), 1) & 7
    mine = slot == lax.broadcasted_iota(jnp.int32, (8, L), 0)
    spread = []
    for r in range(8):
        row = raw[r : r + 1, :]
        high = jnp.where(mine, row >> 4, 0).astype(F32)
        low = jnp.where(mine, row & 15, 0).astype(F32)
        spread.append(jnp.concatenate([high, low], axis=0).astype(BF16))
    source = lax.broadcasted_iota(jnp.int32, (8 * L, L), 0) >> 3
    owner = lax.broadcasted_iota(jnp.int32, (8 * L, L), 1)
    got = nn(jnp.concatenate(spread, axis=1), ones_where(source == owner).astype(BF16))
    return (got[:8] * 16.0 + got[8:]).astype(jnp.int32)


def pack_kernel(par_ref, send_hbm, feat_hbm, prm_hbm, out_ref, idx_ref, send_ref, feat_ref, prm_ref, sems):
    copies = [
        pltpu.make_async_copy(src, dst, sems.at[n])
        for n, (src, dst) in enumerate(
            ((send_hbm, send_ref), (feat_hbm, feat_ref), (prm_hbm, prm_ref))
        )
    ]
    for copy in copies:
        copy.start()
    gauss = feat_ref.shape[0]
    copies[0].wait()
    first = par_ref[0] == 0
    idx = slot_rows(send_ref[...])
    idx_ref[...] = idx
    rows = jnp.where(first, idx[0:4, :], idx[4:8, :])
    cols = column_of(rows.astype(F32))
    lane = lax.broadcasted_iota(jnp.int32, (L, gauss), 1).astype(F32)
    hots = [ones_where(cols[:, c : c + 1] == lane).astype(BF16) for c in range(4)]
    copies[2].wait()
    copies[1].wait()
    got = nn(
        jnp.concatenate(hots, axis=0), jnp.concatenate(split2(feat_ref[...]), axis=1)
    )
    groups = gauss // L
    pieces = [prm_ref[:, g * L : (g + 1) * L] for g in range(groups)]
    pad = jnp.zeros((2, L), F32)
    stacked = jnp.concatenate([x for piece in pieces for x in (piece, pad)], axis=0)
    stack3 = jnp.concatenate(split3(stacked), axis=0)
    low_iota = lax.broadcasted_iota(jnp.int32, (L, L), 0)
    packed = []
    for c in range(4):
        part = got[c * L : c * L + L]
        out_ref[pl.ds(c, L, stride=FWD), :] = part[:, :L] + part[:, L:]
        row = rows[c : c + 1, :]
        low = ones_where((row & (L - 1)) == low_iota).astype(BF16)
        part = nn(stack3, low)
        span = groups * 8
        part = part[:span] + part[span : 2 * span] + part[2 * span :]
        total = jnp.zeros((8, L), F32)
        for g in range(groups):
            total = total + jnp.where((row >> 7) == g, part[g * 8 : g * 8 + 8], 0.0)
        packed.append(total)
    out_ref[pl.ds(4, L, stride=FWD), :] = column_of(jnp.concatenate(packed, axis=0))


def key_kernel(par_ref, lists_ref, weight_ref, row_ref, high_ref, low_ref):
    high_ref[...], low_ref[...] = split2(weight_ref[...])
    shift = par_ref[0] * 4
    tiles, length = lists_ref.shape
    slot_iota = lax.broadcasted_iota(jnp.int32, (8, length), 0)
    holder_iota = lax.broadcasted_iota(jnp.int32, (L, length), 0)
    place = lax.broadcasted_iota(jnp.int32, (8, length), 1)
    place_high = (place >> 4).astype(F32)
    place_low = (place & 15).astype(F32)
    total = jnp.zeros((32, L), F32)
    for t in range(tiles):
        entry = lists_ref[t : t + 1, :]
        holder = ones_where((entry >> 3) == holder_iota).astype(BF16)
        slot = ones_where(((entry + shift) & 7) == slot_iota)
        left = jnp.concatenate(
            [slot * (t + 1.0), slot * place_high, slot * place_low, jnp.zeros((8, length), F32)],
            axis=0,
        ).astype(BF16)
        total = total + nt(left, holder)
    tile = total[0:8]
    key = jnp.where(tile > 0.5, (tile - 1.0) * length + total[8:16] * 16.0 + total[16:24], -1.0)
    row_ref[...] = key


class Pool:
    def __init__(self, length, par_ref, ids_ref, keyrow_ref, prm_ref, sides):
        self.length, self.prm_ref = length, prm_ref
        stripe = par_ref[0]
        self.key = keyrow_ref[...]
        live = self.key >= 0.0
        self.tile = jnp.floor(self.key * (1.0 / length))
        self.ox = jnp.zeros((8, L), F32)
        self.oy = jnp.zeros((8, L), F32)
        for t in range(8):
            ident = ids_ref[t]
            here = self.tile == float(t)
            self.ox = jnp.where(here, ((ident & 127) * 16).astype(F32) + 0.5, self.ox)
            self.oy = jnp.where(
                here, ((ident >> 7) * 16 + stripe * 8).astype(F32) + 0.5, self.oy
            )
        self.base = jnp.where(live, self.tile * length, 1.0e9)
        self.live = ones_where(live)
        self.kx = lax.broadcasted_iota(jnp.int32, (16, L), 0).astype(F32)
        self.ky = lax.broadcasted_iota(jnp.int32, (8, L), 0).astype(F32)
        for side, ref in sides:
            prm_ref[side * 32 : side * 32 + 32, :] = ref[pl.ds(4, L, stride=FWD), :].T[0:32]

    def geometry(self, b):
        prm = self.prm_ref[b * 8 : b * 8 + 8, :]
        dx = (self.kx + self.ox[b : b + 1, :]) - prm[0:1]
        dy = (self.ky + self.oy[b : b + 1, :]) - prm[1:2]
        return prm, dx, dy

    def alphas(self, b):
        prm, dx, dy = self.geometry(b)
        ax = prm[2:3] * dx * dx
        cy = prm[4:5] * dy * dy
        bx = prm[3:4] * dx
        for j in range(8):
            power = -0.5 * (ax + cy[j : j + 1]) - bx * dy[j : j + 1]
            ex = self.live[b : b + 1, :] * jnp.exp(power)
            yield slice(j * 16, j * 16 + 16), ex, prm[5:6] * ex

    def fill_mask(self, mask_ref):
        cols = column_of(self.key)
        for a in range(8):
            front = jnp.broadcast_to(cols[:, a : a + 1], (L, L))
            for b in range(8):
                hit = (front < self.key[b : b + 1, :]) & (front >= self.base[b : b + 1, :])
                mask_ref[a * L : a * L + L, b * L : b * L + L] = ones_where(hit).astype(BF16)

    def spread(self, b, weights, high_ref, low_ref):
        cols = slice(b * L, b * L + L)
        high, low = split2(weights)
        for t in range(8):
            here = ones_where(self.tile[b : b + 1, :] == float(t))
            here = jnp.broadcast_to(here, (L, L)).astype(BF16)
            high_ref[t * L : t * L + L, cols] = high * here
            low_ref[t * L : t * L + L, cols] = low * here


def fill_features(own_ref, peer_ref, feat_ref):
    for side, ref in ((0, own_ref), (1, peer_ref)):
        for c in range(4):
            at = (side * 4 + c) * L
            high, low = split2(ref[pl.ds(c, L, stride=FWD), :])
            feat_ref[at : at + L, 0:L] = high
            feat_ref[at : at + L, L : 2 * L] = low


def fill_logs(pool, b, alpha_ref, lk_ref):
    cols = slice(b * L, b * L + L)
    for spot, ex, alpha in pool.alphas(b):
        high, low = split2(jnp.log1p(-alpha))
        alpha_ref[spot, cols] = alpha
        lk_ref[spot, cols] = high
        lk_ref[L + spot.start : L + spot.stop, cols] = low


def ready_kernel(
    length, par_ref, ids_ref, own_ref, keyrow_ref, mask_ref, alpha_ref, lk_ref, prm_ref
):
    pool = Pool(length, par_ref, ids_ref, keyrow_ref, prm_ref, ((0, own_ref),))
    pool.fill_mask(mask_ref)
    for b in range(4):
        fill_logs(pool, b, alpha_ref, lk_ref)


def front_kernel(
    length,
    par_ref,
    ids_ref,
    own_ref,
    peer_ref,
    keyrow_ref,
    mask_ref,
    half_alpha_ref,
    half_lk_ref,
    teacher_ref,
    whigh_ref,
    wlow_ref,
    bias_ref,
    keep_ref,
    give_ref,
    trans_ref,
    resid_hi,
    resid_lo,
    prm_ref,
    feat_ref,
    alpha_ref,
    lk_ref,
    wm_hi,
    wm_lo,
    rt_ref,
):
    pool = Pool(
        length, par_ref, ids_ref, keyrow_ref, prm_ref, ((0, own_ref), (1, peer_ref))
    )
    fill_features(own_ref, peer_ref, feat_ref)
    half = 4 * L
    alpha_ref[:, 0:half] = half_alpha_ref[...]
    lk_ref[:, 0:half] = half_lk_ref[...]
    for b in range(4, 8):
        fill_logs(pool, b, alpha_ref, lk_ref)

    for b in range(0, 8, 2):
        both = nn(lk_ref[...], mask_ref[:, b * L : b * L + 2 * L])
        trans = jnp.exp(both[:L] + both[L:])
        trans_ref[:, b * L : b * L + 2 * L] = trans
        for q in range(2):
            cols = slice((b + q) * L, (b + q) * L + L)
            weights = trans[:, q * L : q * L + L] * alpha_ref[:, cols]
            pool.spread(b + q, weights, wm_hi, wm_lo)

    w_hi, w_lo = whigh_ref[...], wlow_ref[...]
    w_pair = jnp.concatenate([w_hi, w_hi], axis=0)
    width = whigh_ref.shape[1]
    squares = jnp.zeros((1, width), F32)
    bias_sum = jnp.zeros((1, width), F32)
    step = 2 * L
    for r in range(4):
        rows = slice(r * step, r * step + step)
        both = nn(wm_hi[rows, :], feat_ref[...])
        rendered = both[:, :L] + both[:, L:] + nn(wm_lo[rows, :], feat_ref[:, 0:L])
        high, low = split2(rendered)
        rt_hi, rt_lo = split2(rendered.T)
        rt_ref[0:L, rows] = rt_hi
        rt_ref[L : 2 * L, rows] = rt_lo
        decoded = nn(jnp.concatenate([high, low], axis=1), w_pair) + nn(high, w_lo)
        resid = decoded + bias_ref[...] - teacher_ref[rows, :]
        squares = squares + jnp.sum(resid * resid, axis=0, keepdims=True)
        bias_sum = bias_sum + jnp.sum(resid, axis=0, keepdims=True)
        high, low = split2(resid)
        resid_hi[rows, :] = high
        resid_lo[rows, :] = low

    both = nn(rt_ref[...], resid_hi[...])
    grad_w = both[:L] + both[L:] + nn(rt_ref[0:L, :], resid_lo[...])
    sq_row = jnp.broadcast_to(jnp.sum(squares, axis=1, keepdims=True), (1, L))
    first = par_ref[0] == 0
    half = width // 2
    for ref, left in ((keep_ref, first), (give_ref, jnp.logical_not(first))):
        piece = jnp.where(left, grad_w[:, :half], grad_w[:, half:])
        ref[pl.ds(0, L, stride=GAT), :] = piece[:, :L]
        ref[pl.ds(1, L, stride=GAT), :] = piece[:, L:]
        piece = jnp.where(left, bias_sum[:, :half], bias_sum[:, half:])
        rows = jnp.concatenate([piece[:, :L], piece[:, L:], sq_row], axis=0)
        ref[pl.ds(2, L, stride=GAT), :] = column_of(rows)


def pixel_kernel(resid_hi, resid_lo, whigh_ref, wlow_ref, grad_ref):
    w_hi = whigh_ref[...]
    w_both = jnp.concatenate([w_hi, wlow_ref[...]], axis=0)
    step = 2 * L
    for r in range(4):
        rows = slice(r * step, r * step + step)
        both = nt(resid_hi[rows, :], w_both)
        grad_ref[rows, :] = both[:, :L] + both[:, L:] + nt(resid_lo[rows, :], w_hi)


def back_kernel(
    length,
    par_ref,
    ids_ref,
    own_ref,
    peer_ref,
    keyrow_ref,
    trans_ref,
    grad_ref,
    keep_ref,
    give_ref,
    mask_ref,
    prm_ref,
    feat_ref,
    feat2_ref,
    ex_ref,
    alpha_ref,
    lk_ref,
    wm_hi,
    wm_lo,
    drt_ref,
    dw_ref,
):
    pool = Pool(
        length, par_ref, ids_ref, keyrow_ref, prm_ref, ((0, own_ref), (1, peer_ref))
    )
    fill_features(own_ref, peer_ref, feat_ref)
    feat2_ref[:, 0:L] = feat_ref[:, 0:L]
    feat2_ref[:, L : 2 * L] = feat_ref[:, 0:L]
    pool.fill_mask(mask_ref)
    for b in range(8):
        cols = slice(b * L, b * L + L)
        for spot, ex, alpha in pool.alphas(b):
            ex_ref[spot, cols] = ex
            alpha_ref[spot, cols] = alpha
        pool.spread(b, trans_ref[:, cols] * alpha_ref[:, cols], wm_hi, wm_lo)

    dw_ref[...] = jnp.zeros(dw_ref.shape, F32)
    step = 2 * L
    for r in range(4):
        rows = slice(r * step, r * step + step)
        grad = grad_ref[rows, :]
        high, low = split2(grad)
        pair = jnp.concatenate([high, low], axis=1)
        dt_hi, dt_lo = split2(grad.T)
        drt_ref[0:L, rows] = dt_hi
        drt_ref[L : 2 * L, rows] = dt_lo
        for b in range(0, 8, 2):
            entries = slice(b * L, b * L + step)
            part = nt(pair, feat2_ref[entries, :]) + nt(high, feat_ref[entries, L : 2 * L])
            for q in range(2):
                cols = slice((b + q) * L, (b + q) * L + L)
                tile = pool.tile[b + q : b + q + 1, :]
                got = part[:, q * L : q * L + L]
                kept = jnp.where(tile == float(2 * r), got[:L], dw_ref[:, cols])
                dw_ref[:, cols] = jnp.where(tile == float(2 * r + 1), got[L:], kept)

    for b in range(8):
        cols = slice(b * L, b * L + L)
        high, low = split2(dw_ref[:, cols] * (trans_ref[:, cols] * alpha_ref[:, cols]))
        lk_ref[0:L, cols] = high
        lk_ref[L : 2 * L, cols] = low

    def total(value):
        return jnp.sum(value, axis=0, keepdims=True)

    blocks = []
    for b in range(0, 8, 2):
        wide = slice(b * L, b * L + step)
        both = nt(lk_ref[...], mask_ref[wide, :])
        alpha = alpha_ref[:, wide]
        dalpha = dw_ref[:, wide] * trans_ref[:, wide] - (both[:L] + both[L:]) / (1.0 - alpha)
        dpower = dalpha * alpha
        dopac = total(dalpha * ex_ref[:, wide])
        for q in range(2):
            prm, dx, dy = pool.geometry(b + q)
            flat = jnp.zeros((16, L), F32)
            by_y = jnp.zeros((16, L), F32)
            by_yy = jnp.zeros((16, L), F32)
            for j in range(8):
                part = dpower[j * 16 : j * 16 + 16, q * L : q * L + L]
                scaled = part * dy[j : j + 1]
                flat = flat + part
                by_y = by_y + scaled
                by_yy = by_yy + scaled * dy[j : j + 1]
            sx = total(flat * dx)
            sxx = total(flat * dx * dx)
            sy = total(by_y)
            sxy = total(by_y * dx)
            syy = total(by_yy)
            blocks += [
                prm[2:3] * sx + prm[3:4] * sy,
                prm[4:5] * sy + prm[3:4] * sx,
                -0.5 * sxx,
                -sxy,
                -0.5 * syy,
                dopac[:, q * L : q * L + L],
                jnp.zeros((2, L), F32),
            ]

    for side, ref in ((0, keep_ref), (1, give_ref)):
        for c in range(0, 4, 2):
            wide = slice((side * 4 + c) * L, (side * 4 + c) * L + step)
            both = nn(drt_ref[...], wm_hi[:, wide])
            grad = both[:L] + both[L:] + nn(drt_ref[0:L, :], wm_lo[:, wide])
            ref[pl.ds(c, L, stride=FWD), :] = grad[:, :L].T
            ref[pl.ds(c + 1, L, stride=FWD), :] = grad[:, L:].T
        rows = jnp.concatenate(blocks[side * 28 : side * 28 + 28], axis=0)
        ref[pl.ds(4, L, stride=FWD), :] = column_of(rows)


def compose_kernel(share_ref, keep_ref, give_ref, out_ref):
    for c in range(5):
        spot = pl.ds(c, L, stride=FWD)
        rows = keep_ref[spot, :] + give_ref[spot, :]
        if c == 4:
            small = jnp.sum(share_ref[pl.ds(2, L, stride=GAT), :], axis=0, keepdims=True)
            rows = rows + pltpu.roll(jnp.broadcast_to(small, (L, L)), 32, 1)
        out_ref[pl.ds(c, L, stride=RET), :] = rows
    for c in range(2):
        total = jnp.sum(share_ref[pl.ds(c, L, stride=GAT), :], axis=0, keepdims=True)
        out_ref[pl.ds(5 + c, L, stride=RET), :] = jnp.broadcast_to(total, (L, L))


def place_kernel(par_ref, idx_ref, own_ref, feat_ref, prm_ref, hot_ref):
    gauss = feat_ref.shape[0]
    first = par_ref[0] == 0
    idx = idx_ref[...]
    top, bottom = idx[0:4], idx[4:8]
    sub = lax.broadcasted_iota(jnp.int32, (gauss, L), 0)
    other = jnp.where(first, bottom, top)
    for c in range(4):
        hot_ref[:, c * L : c * L + L] = ones_where(other[c : c + 1] == sub).astype(BF16)
    mine = jnp.where(first, top, bottom)
    hots = [ones_where(mine[c : c + 1] == sub).astype(BF16) for c in range(4)]
    feat_ref[...] = place_features(own_ref, jnp.concatenate(hots, axis=1))
    prm_ref[...] = place_params(own_ref, mine, gauss // L)


def place_features(ref, onehot):
    grads = [
        jnp.concatenate(split2(ref[pl.ds(c, L, stride=RET), :]), axis=1) for c in range(4)
    ]
    both = nn(onehot, jnp.concatenate(grads, axis=0))
    return both[:, :L] + both[:, L:]


def place_params(ref, idx, groups):
    low_iota = lax.broadcasted_iota(jnp.int32, (L, L), 0)
    prm = ref[pl.ds(4, L, stride=RET), :].T
    params = jnp.zeros((2 * groups * 8, L), F32)
    for c in range(4):
        row = idx[c : c + 1]
        block = prm[c * 8 : c * 8 + 8]
        spread = jnp.concatenate(
            [jnp.where((row >> 7) == g, block, 0.0) for g in range(groups)], axis=0
        )
        both = jnp.concatenate(split2(spread), axis=0)
        hot = ones_where((row & (L - 1)) == low_iota).astype(BF16)
        params = params + nt(both, hot)
    return params[: groups * 8] + params[groups * 8 :]


def final_kernel(
    pixels,
    par_ref,
    idx_ref,
    own_ref,
    peer_ref,
    part_feat_ref,
    part_prm_ref,
    hot_ref,
    feat_ref,
    prm_ref,
    weight_ref,
    bias_ref,
    loss_ref,
):
    first = par_ref[0] == 0
    feat_ref[...] = part_feat_ref[...] + place_features(peer_ref, hot_ref[...])
    groups = feat_ref.shape[0] // L
    idx = idx_ref[...]
    other = jnp.where(first, idx[4:8], idx[0:4])
    params = part_prm_ref[...] + place_params(peer_ref, other, groups)
    for g in range(groups):
        prm_ref[:, g * L : g * L + L] = params[g * 8 : g * 8 + 6]

    width = weight_ref.shape[1]
    half = width // 2
    scale = 1.0 / pixels
    for ref, left in ((own_ref, first), (peer_ref, jnp.logical_not(first))):
        small = ref[pl.ds(4, L, stride=RET), :].T
        wide = [ref[pl.ds(5 + c, L, stride=RET), :] * scale for c in range(2)]
        row = jnp.concatenate([small[32:33], small[33:34]], axis=1) * scale
        wide = jnp.concatenate(wide, axis=1)

        def store(at):
            weight_ref[:, at : at + half] = wide
            bias_ref[:, at : at + half] = row

        pl.when(left)(functools.partial(store, 0))
        pl.when(jnp.logical_not(left))(functools.partial(store, half))
    loss_ref[...] = small[34:35, :] * (scale / width)


def call(kernel, shapes, specs, scratch=(), flops=0, limit=40):
    single = not isinstance(shapes, (list, tuple))
    count = 1 if single else len(shapes)
    cost = pl.CostEstimate(flops=flops, bytes_accessed=flops // 300, transcendentals=0)
    return pl.pallas_call(
        kernel,
        out_shape=shapes,
        in_specs=specs,
        out_specs=VMEM if single else [VMEM] * count,
        scratch_shapes=list(scratch),
        compiler_params=pltpu.CompilerParams(vmem_limit_bytes=limit * 1024 * 1024),
        cost_estimate=cost,
    )


def f32(*shape):
    return jax.ShapeDtypeStruct(shape, F32)


def bf16(*shape):
    return jax.ShapeDtypeStruct(shape, BF16)


def pack(par, send, features, gauss_params):
    shapes = [f32(FWD * L, L), jax.ShapeDtypeStruct((8, L), jnp.int32)]
    inputs = (send, features, gauss_params)
    scratch = [pltpu.VMEM(x.shape, x.dtype) for x in inputs]
    scratch.append(pltpu.SemaphoreType.DMA((3,)))
    return call(pack_kernel, shapes, [SMEM, HBM, HBM, HBM], scratch, flops=2 * 10**9, limit=62)(par, *inputs)


def keys(par, tile_lists, weight):
    shapes = [f32(8, L), bf16(*weight.shape), bf16(*weight.shape)]
    return call(key_kernel, shapes, [SMEM, VMEM, VMEM], flops=2 * 10**9)(par, tile_lists, weight)


def ready(par, ids, own, keyrow, length):
    pool = 8 * L
    return call(
        functools.partial(ready_kernel, float(length)),
        [bf16(pool, pool), f32(L, pool // 2), bf16(2 * L, pool // 2)],
        [SMEM, SMEM, VMEM, VMEM],
        [pltpu.VMEM((64, L), F32)],
        flops=10**9,
    )(par, ids, own, keyrow)


def front(par, ids, own, peer, keyrow, halves, teacher, whigh, wlow, bias, length):
    pixels, width = teacher.shape
    pool = 8 * L
    scratch = [
        pltpu.VMEM((64, L), F32),
        pltpu.VMEM((pool, 2 * L), BF16),
        pltpu.VMEM((L, pool), F32),
        pltpu.VMEM((2 * L, pool), BF16),
        pltpu.VMEM((pixels, pool), BF16),
        pltpu.VMEM((pixels, pool), BF16),
        pltpu.VMEM((2 * L, pixels), BF16),
    ]
    return call(
        functools.partial(front_kernel, float(length)),
        [f32(GAT * L, L), f32(GAT * L, L), f32(L, pool), bf16(pixels, width), bf16(pixels, width)],
        [SMEM, SMEM] + [VMEM] * 10,
        scratch,
        flops=10**10,
    )(par, ids, own, peer, keyrow, *halves, teacher, whigh, wlow, bias)


def pixel(resid_hi, resid_lo, whigh, wlow):
    shape = f32(resid_hi.shape[0], whigh.shape[0])
    return call(pixel_kernel, shape, [VMEM] * 4, flops=10**9)(resid_hi, resid_lo, whigh, wlow)


def back(par, ids, own, peer, keyrow, trans, grad, length):
    pool = 8 * L
    pixels = grad.shape[0]
    scratch = [
        pltpu.VMEM((pool, pool), BF16),
        pltpu.VMEM((64, L), F32),
        pltpu.VMEM((pool, 2 * L), BF16),
        pltpu.VMEM((pool, 2 * L), BF16),
        pltpu.VMEM((L, pool), F32),
        pltpu.VMEM((L, pool), F32),
        pltpu.VMEM((2 * L, pool), BF16),
        pltpu.VMEM((pixels, pool), BF16),
        pltpu.VMEM((pixels, pool), BF16),
        pltpu.VMEM((2 * L, pixels), BF16),
        pltpu.VMEM((L, pool), F32),
    ]
    return call(
        functools.partial(back_kernel, float(length)),
        [f32(FWD * L, L), f32(FWD * L, L)],
        [SMEM, SMEM] + [VMEM] * 5,
        scratch,
        flops=8 * 10**9,
    )(par, ids, own, peer, keyrow, trans, grad)


def compose(share, keep, give):
    return call(compose_kernel, f32(RET * L, L), [VMEM] * 3, flops=10**9)(share, keep, give)


def place(par, idx, own, gauss):
    return call(
        place_kernel,
        [f32(gauss, L), f32(gauss // L * 8, L), bf16(gauss, 4 * L)],
        [SMEM, VMEM, VMEM],
        flops=10**9,
    )(par, idx, own)


def final(par, idx, own, peer, parts, width, pixels):
    gauss = parts[0].shape[0]
    return call(
        functools.partial(final_kernel, float(pixels)),
        [f32(gauss, L), f32(6, gauss), f32(L, width), f32(1, width), f32(1, L)],
        [SMEM] + [VMEM] * 6,
        flops=2 * 10**9,
    )(par, idx, own, peer, *parts)


def swap(value):
    return lax.ppermute(value, "px", SWAP)


def exchange(value, rows):
    sent = value.reshape(L, 1, rows * L)
    return lax.all_to_all(sent, "gs", split_axis=0, concat_axis=0, tiled=True).reshape(rows * L, L)


def per_device(
    features, gauss_params, send_index, tile_ids, tile_lists, teacher, decoder_weight, decoder_bias
):
    holders = lax.axis_size("gs")
    par = lax.axis_index("px").astype(jnp.int32).reshape(1)
    width = teacher.shape[2]
    sent, idx = pack(par, send_index.reshape(8, -1), features, gauss_params)
    sent, tile_lists, decoder_weight, teacher = lax.optimization_barrier(
        (sent, tile_lists, decoder_weight, teacher)
    )
    got = exchange(sent, FWD)
    prepared = keys(par, tile_lists, decoder_weight)
    got, (keyrow, whigh, wlow) = lax.optimization_barrier((got, prepared))
    peer = swap(got)
    length = tile_lists.shape[1]
    halves = ready(par, tile_ids, got, keyrow, length)
    flat_teacher = teacher.reshape(-1, width)
    bias = decoder_bias.reshape(1, -1)
    keep, give, trans, resid_hi, resid_lo = front(
        par, tile_ids, got, peer, keyrow, halves, flat_teacher, whigh, wlow, bias, length
    )
    given = swap(give)
    grad = pixel(resid_hi, resid_lo, whigh, wlow)
    part, trans, grad = lax.optimization_barrier((keep + given, trans, grad))
    share = exchange(part, GAT)
    keep, give = back(par, tile_ids, got, peer, keyrow, trans, grad, length)
    ret = exchange(compose(share, keep, swap(give)), RET)
    other = swap(ret)
    parts = place(par, idx, ret, features.shape[0])
    pixels = holders * tile_ids.shape[0] * 256
    grad_features, grad_params, grad_weight, grad_bias, loss = final(
        par, idx, ret, other, parts, width, pixels
    )
    return grad_features, grad_params, grad_weight, grad_bias.reshape(-1), loss[0, 0]


def solution(mesh):
    return jax.shard_map(
        per_device,
        mesh=mesh,
        in_specs=(
            P("gs", None),
            P(None, "gs"),
            P("gs"),
            P("gs"),
            P("gs", None),
            P("gs", "px", None),
            P(),
            P(),
        ),
        out_specs=(P("gs", None), P(None, "gs"), P(), P(), P()),
        check_vma=False,
    )
```

```python
import functools

import jax
import jax.numpy as jnp
from jax import lax
from jax.experimental import pallas as pl
from jax.experimental.pallas import tpu as pltpu
from jax.sharding import PartitionSpec as P

F32 = jnp.float32
BF16 = jnp.bfloat16
L = 128
SWAP = [(0, 1), (1, 0)]
FWD = 5
RET = 7
GAT = 3
VMEM = pl.BlockSpec(memory_space=pltpu.VMEM)
SMEM = pl.BlockSpec(memory_space=pltpu.SMEM)
HBM = pl.BlockSpec(memory_space=pltpu.HBM)


def nn(lhs, rhs):
    return lax.dot_general(lhs, rhs, (((1,), (0,)), ((), ())), preferred_element_type=F32)


def nt(lhs, rhs):
    return lax.dot_general(lhs, rhs, (((1,), (1,)), ((), ())), preferred_element_type=F32)


def split2(value):
    high = value.astype(BF16)
    return high, (value - high.astype(F32)).astype(BF16)


def split3(value):
    high = value.astype(BF16)
    rest = value - high.astype(F32)
    mid = rest.astype(BF16)
    return high, mid, (rest - mid.astype(F32)).astype(BF16)


def ones_where(mask):
    return jnp.where(mask, 1.0, 0.0).astype(F32)


def column_of(rows):
    pad = jnp.zeros((L - rows.shape[0], L), F32)
    return jnp.concatenate([rows, pad], axis=0).T


def slot_rows(raw):
    slot = lax.broadcasted_iota(jnp.int32, (8, L), 1) & 7
    mine = slot == lax.broadcasted_iota(jnp.int32, (8, L), 0)
    spread = []
    for r in range(8):
        row = raw[r : r + 1, :]
        high = jnp.where(mine, row >> 4, 0).astype(F32)
        low = jnp.where(mine, row & 15, 0).astype(F32)
        spread.append(jnp.concatenate([high, low], axis=0).astype(BF16))
    source = lax.broadcasted_iota(jnp.int32, (8 * L, L), 0) >> 3
    owner = lax.broadcasted_iota(jnp.int32, (8 * L, L), 1)
    got = nn(jnp.concatenate(spread, axis=1), ones_where(source == owner).astype(BF16))
    return (got[:8] * 16.0 + got[8:]).astype(jnp.int32)


def pack_kernel(par_ref, send_hbm, feat_hbm, prm_hbm, out_ref, idx_ref, send_ref, feat_ref, prm_ref, sems):
    copies = [
        pltpu.make_async_copy(src, dst, sems.at[n])
        for n, (src, dst) in enumerate(
            ((send_hbm, send_ref), (feat_hbm, feat_ref), (prm_hbm, prm_ref))
        )
    ]
    for copy in copies:
        copy.start()
    gauss = feat_ref.shape[0]
    copies[0].wait()
    first = par_ref[0] == 0
    idx = slot_rows(send_ref[...])
    idx_ref[...] = idx
    rows = jnp.where(first, idx[0:4, :], idx[4:8, :])
    cols = column_of(rows.astype(F32))
    lane = lax.broadcasted_iota(jnp.int32, (L, gauss), 1).astype(F32)
    hots = [ones_where(cols[:, c : c + 1] == lane).astype(BF16) for c in range(4)]
    copies[2].wait()
    copies[1].wait()
    got = nn(
        jnp.concatenate(hots, axis=0), jnp.concatenate(split2(feat_ref[...]), axis=1)
    )
    groups = gauss // L
    pieces = [prm_ref[:, g * L : (g + 1) * L] for g in range(groups)]
    pad = jnp.zeros((2, L), F32)
    stacked = jnp.concatenate([x for piece in pieces for x in (piece, pad)], axis=0)
    stack3 = jnp.concatenate(split3(stacked), axis=0)
    low_iota = lax.broadcasted_iota(jnp.int32, (L, L), 0)
    packed = []
    for c in range(4):
        part = got[c * L : c * L + L]
        out_ref[pl.ds(c, L, stride=FWD), :] = part[:, :L] + part[:, L:]
        row = rows[c : c + 1, :]
        low = ones_where((row & (L - 1)) == low_iota).astype(BF16)
        part = nn(stack3, low)
        span = groups * 8
        part = part[:span] + part[span : 2 * span] + part[2 * span :]
        total = jnp.zeros((8, L), F32)
        for g in range(groups):
            total = total + jnp.where((row >> 7) == g, part[g * 8 : g * 8 + 8], 0.0)
        packed.append(total)
    out_ref[pl.ds(4, L, stride=FWD), :] = column_of(jnp.concatenate(packed, axis=0))


def key_kernel(par_ref, lists_ref, weight_ref, row_ref, high_ref, low_ref):
    high_ref[...], low_ref[...] = split2(weight_ref[...])
    shift = par_ref[0] * 4
    tiles, length = lists_ref.shape
    slot_iota = lax.broadcasted_iota(jnp.int32, (8, length), 0)
    holder_iota = lax.broadcasted_iota(jnp.int32, (L, length), 0)
    place = lax.broadcasted_iota(jnp.int32, (8, length), 1)
    place_high = (place >> 4).astype(F32)
    place_low = (place & 15).astype(F32)
    total = jnp.zeros((32, L), F32)
    for t in range(tiles):
        entry = lists_ref[t : t + 1, :]
        holder = ones_where((entry >> 3) == holder_iota).astype(BF16)
        slot = ones_where(((entry + shift) & 7) == slot_iota)
        left = jnp.concatenate(
            [slot * (t + 1.0), slot * place_high, slot * place_low, jnp.zeros((8, length), F32)],
            axis=0,
        ).astype(BF16)
        total = total + nt(left, holder)
    tile = total[0:8]
    key = jnp.where(tile > 0.5, (tile - 1.0) * length + total[8:16] * 16.0 + total[16:24], -1.0)
    row_ref[...] = key


class Pool:
    def __init__(self, length, par_ref, ids_ref, keyrow_ref, prm_ref, sides):
        self.length, self.prm_ref = length, prm_ref
        stripe = par_ref[0]
        self.key = keyrow_ref[...]
        live = self.key >= 0.0
        self.tile = jnp.floor(self.key * (1.0 / length))
        self.ox = jnp.zeros((8, L), F32)
        self.oy = jnp.zeros((8, L), F32)
        for t in range(8):
            ident = ids_ref[t]
            here = self.tile == float(t)
            self.ox = jnp.where(here, ((ident & 127) * 16).astype(F32) + 0.5, self.ox)
            self.oy = jnp.where(
                here, ((ident >> 7) * 16 + stripe * 8).astype(F32) + 0.5, self.oy
            )
        self.base = jnp.where(live, self.tile * length, 1.0e9)
        self.live = ones_where(live)
        self.kx = lax.broadcasted_iota(jnp.int32, (16, L), 0).astype(F32)
        self.ky = lax.broadcasted_iota(jnp.int32, (8, L), 0).astype(F32)
        for side, ref in sides:
            prm_ref[side * 32 : side * 32 + 32, :] = ref[pl.ds(4, L, stride=FWD), :].T[0:32]

    def geometry(self, b):
        prm = self.prm_ref[b * 8 : b * 8 + 8, :]
        dx = (self.kx + self.ox[b : b + 1, :]) - prm[0:1]
        dy = (self.ky + self.oy[b : b + 1, :]) - prm[1:2]
        return prm, dx, dy

    def alphas(self, b):
        prm, dx, dy = self.geometry(b)
        ax = prm[2:3] * dx * dx
        cy = prm[4:5] * dy * dy
        bx = prm[3:4] * dx
        for j in range(8):
            power = -0.5 * (ax + cy[j : j + 1]) - bx * dy[j : j + 1]
            ex = self.live[b : b + 1, :] * jnp.exp(power)
            yield slice(j * 16, j * 16 + 16), ex, prm[5:6] * ex

    def fill_mask(self, mask_ref):
        cols = column_of(self.key)
        one, zero = jnp.ones((8, 16, L), BF16), jnp.zeros((8, 16, L), BF16)

        def short(rows, shape):
            return jnp.broadcast_to(rows, shape).astype(jnp.int32).astype(jnp.int16)

        base = jnp.minimum(self.base, 30000.0)
        ends = [short(self.key[b : b + 1, :], (16, L))[None] for b in range(8)]
        starts = [short(base[b : b + 1, :], (16, L))[None] for b in range(8)]
        for a in range(8):
            front = short(cols[:, a : a + 1], (L, L)).reshape(8, 16, L)
            for b in range(8):
                hit = (front < ends[b]) & (front >= starts[b])
                got = jnp.where(hit, one, zero).reshape(L, L)
                mask_ref[a * L : a * L + L, b * L : b * L + L] = got

    def spread(self, b, weights, high_ref, low_ref):
        cols = slice(b * L, b * L + L)
        high, low = (x.reshape(8, 16, L) for x in split2(weights))
        for t in range(8):
            here = ones_where(self.tile[b : b + 1, :] == float(t))
            here = jnp.broadcast_to(here, (16, L)).astype(BF16)[None]
            high_ref[t * L : t * L + L, cols] = (high * here).reshape(L, L)
            low_ref[t * L : t * L + L, cols] = (low * here).reshape(L, L)


def fill_features(own_ref, peer_ref, feat_ref):
    for side, ref in ((0, own_ref), (1, peer_ref)):
        for c in range(4):
            at = (side * 4 + c) * L
            high, low = split2(ref[pl.ds(c, L, stride=FWD), :])
            feat_ref[at : at + L, 0:L] = high
            feat_ref[at : at + L, L : 2 * L] = low


def fill_logs(pool, b, alpha_ref, lk_ref):
    cols = slice(b * L, b * L + L)
    for spot, ex, alpha in pool.alphas(b):
        high, low = split2(jnp.log1p(-alpha))
        alpha_ref[spot, cols] = alpha
        lk_ref[spot, cols] = high
        lk_ref[L + spot.start : L + spot.stop, cols] = low


def ready_kernel(
    length, par_ref, ids_ref, own_ref, keyrow_ref, mask_ref, alpha_ref, lk_ref, prm_ref
):
    pool = Pool(length, par_ref, ids_ref, keyrow_ref, prm_ref, ((0, own_ref),))
    pool.fill_mask(mask_ref)
    for b in range(4):
        fill_logs(pool, b, alpha_ref, lk_ref)


def front_kernel(
    length,
    par_ref,
    ids_ref,
    own_ref,
    peer_ref,
    keyrow_ref,
    mask_ref,
    half_alpha_ref,
    half_lk_ref,
    teacher_ref,
    whigh_ref,
    wlow_ref,
    bias_ref,
    keep_ref,
    give_ref,
    trans_ref,
    resid_hi,
    resid_lo,
    prm_ref,
    feat_ref,
    alpha_ref,
    lk_ref,
    wm_hi,
    wm_lo,
    rt_ref,
):
    pool = Pool(
        length, par_ref, ids_ref, keyrow_ref, prm_ref, ((0, own_ref), (1, peer_ref))
    )
    fill_features(own_ref, peer_ref, feat_ref)
    half = 4 * L
    alpha_ref[:, 0:half] = half_alpha_ref[...]
    lk_ref[:, 0:half] = half_lk_ref[...]
    for b in range(4, 8):
        fill_logs(pool, b, alpha_ref, lk_ref)

    for b in range(0, 8, 2):
        both = nn(lk_ref[...], mask_ref[:, b * L : b * L + 2 * L])
        trans = jnp.exp(both[:L] + both[L:])
        trans_ref[:, b * L : b * L + 2 * L] = trans
        for q in range(2):
            cols = slice((b + q) * L, (b + q) * L + L)
            weights = trans[:, q * L : q * L + L] * alpha_ref[:, cols]
            pool.spread(b + q, weights, wm_hi, wm_lo)

    w_hi, w_lo = whigh_ref[...], wlow_ref[...]
    w_pair = jnp.concatenate([w_hi, w_hi], axis=0)
    width = whigh_ref.shape[1]
    squares = jnp.zeros((1, width), F32)
    bias_sum = jnp.zeros((1, width), F32)
    step = 8 * L
    for r in range(1):
        rows = slice(r * step, r * step + step)
        both = nn(wm_hi[rows, :], feat_ref[...])
        rendered = both[:, :L] + both[:, L:] + nn(wm_lo[rows, :], feat_ref[:, 0:L])
        high, low = split2(rendered)
        rt_hi, rt_lo = split2(rendered.T)
        rt_ref[0:L, rows] = rt_hi
        rt_ref[L : 2 * L, rows] = rt_lo
        decoded = nn(jnp.concatenate([high, low], axis=1), w_pair) + nn(high, w_lo)
        resid = decoded + bias_ref[...] - teacher_ref[rows, :]
        squares = squares + jnp.sum(resid * resid, axis=0, keepdims=True)
        bias_sum = bias_sum + jnp.sum(resid, axis=0, keepdims=True)
        high, low = split2(resid)
        resid_hi[rows, :] = high
        resid_lo[rows, :] = low

    both = nn(rt_ref[...], resid_hi[...])
    grad_w = both[:L] + both[L:] + nn(rt_ref[0:L, :], resid_lo[...])
    sq_row = jnp.broadcast_to(jnp.sum(squares, axis=1, keepdims=True), (1, L))
    first = par_ref[0] == 0
    half = width // 2
    for ref, left in ((keep_ref, first), (give_ref, jnp.logical_not(first))):
        piece = jnp.where(left, grad_w[:, :half], grad_w[:, half:])
        ref[pl.ds(0, L, stride=GAT), :] = piece[:, :L]
        ref[pl.ds(1, L, stride=GAT), :] = piece[:, L:]
        piece = jnp.where(left, bias_sum[:, :half], bias_sum[:, half:])
        rows = jnp.concatenate([piece[:, :L], piece[:, L:], sq_row], axis=0)
        ref[pl.ds(2, L, stride=GAT), :] = column_of(rows)


def pixel_kernel(resid_hi, resid_lo, whigh_ref, wlow_ref, grad_ref):
    w_hi = whigh_ref[...]
    w_both = jnp.concatenate([w_hi, wlow_ref[...]], axis=0)
    step = 2 * L
    for r in range(4):
        rows = slice(r * step, r * step + step)
        both = nt(resid_hi[rows, :], w_both)
        grad_ref[rows, :] = both[:, :L] + both[:, L:] + nt(resid_lo[rows, :], w_hi)


def back_kernel(
    length,
    par_ref,
    ids_ref,
    own_ref,
    peer_ref,
    keyrow_ref,
    trans_ref,
    grad_ref,
    keep_ref,
    give_ref,
    mask_ref,
    prm_ref,
    feat_ref,
    feat2_ref,
    ex_ref,
    alpha_ref,
    lk_ref,
    wm_hi,
    wm_lo,
    drt_ref,
    dw_ref,
):
    pool = Pool(
        length, par_ref, ids_ref, keyrow_ref, prm_ref, ((0, own_ref), (1, peer_ref))
    )
    fill_features(own_ref, peer_ref, feat_ref)
    feat2_ref[:, 0:L] = feat_ref[:, 0:L]
    feat2_ref[:, L : 2 * L] = feat_ref[:, 0:L]
    pool.fill_mask(mask_ref)
    for b in range(8):
        cols = slice(b * L, b * L + L)
        for spot, ex, alpha in pool.alphas(b):
            ex_ref[spot, cols] = ex
            alpha_ref[spot, cols] = alpha
        pool.spread(b, trans_ref[:, cols] * alpha_ref[:, cols], wm_hi, wm_lo)

    dw_ref[...] = jnp.zeros(dw_ref.shape, F32)
    step = 2 * L
    span = 4
    for r in range(8 // span):
        rows = slice(r * span * L, (r + 1) * span * L)
        grad = grad_ref[rows, :]
        high, low = split2(grad)
        pair = jnp.concatenate([high, low], axis=1)
        dt_hi, dt_lo = split2(grad.T)
        drt_ref[0:L, rows] = dt_hi
        drt_ref[L : 2 * L, rows] = dt_lo
        for b in range(0, 8, 2):
            entries = slice(b * L, b * L + step)
            part = nt(pair, feat2_ref[entries, :]) + nt(high, feat_ref[entries, L : 2 * L])
            for q in range(2):
                cols = slice((b + q) * L, (b + q) * L + L)
                tile = pool.tile[b + q : b + q + 1, :]
                kept = dw_ref[:, cols]
                for t in range(span):
                    got = part[t * L : t * L + L, q * L : q * L + L]
                    kept = jnp.where(tile == float(r * span + t), got, kept)
                dw_ref[:, cols] = kept

    for b in range(8):
        cols = slice(b * L, b * L + L)
        high, low = split2(dw_ref[:, cols] * (trans_ref[:, cols] * alpha_ref[:, cols]))
        lk_ref[0:L, cols] = high
        lk_ref[L : 2 * L, cols] = low

    def total(value):
        return jnp.sum(value, axis=0, keepdims=True)

    blocks = []
    for b in range(0, 8, 2):
        wide = slice(b * L, b * L + step)
        both = nt(lk_ref[...], mask_ref[wide, :])
        alpha = alpha_ref[:, wide]
        dalpha = dw_ref[:, wide] * trans_ref[:, wide] - (both[:L] + both[L:]) / (1.0 - alpha)
        dpower = dalpha * alpha
        dopac = total(dalpha * ex_ref[:, wide])
        for q in range(2):
            prm, dx, dy = pool.geometry(b + q)
            flat = jnp.zeros((16, L), F32)
            by_y = jnp.zeros((16, L), F32)
            by_yy = jnp.zeros((16, L), F32)
            for j in range(8):
                part = dpower[j * 16 : j * 16 + 16, q * L : q * L + L]
                scaled = part * dy[j : j + 1]
                flat = flat + part
                by_y = by_y + scaled
                by_yy = by_yy + scaled * dy[j : j + 1]
            sx = total(flat * dx)
            sxx = total(flat * dx * dx)
            sy = total(by_y)
            sxy = total(by_y * dx)
            syy = total(by_yy)
            blocks += [
                prm[2:3] * sx + prm[3:4] * sy,
                prm[4:5] * sy + prm[3:4] * sx,
                -0.5 * sxx,
                -sxy,
                -0.5 * syy,
                dopac[:, q * L : q * L + L],
                jnp.zeros((2, L), F32),
            ]

    for side, ref in ((0, keep_ref), (1, give_ref)):
        for c in range(0, 4, 2):
            wide = slice((side * 4 + c) * L, (side * 4 + c) * L + step)
            both = nn(drt_ref[...], wm_hi[:, wide])
            grad = both[:L] + both[L:] + nn(drt_ref[0:L, :], wm_lo[:, wide])
            ref[pl.ds(c, L, stride=FWD), :] = grad[:, :L].T
            ref[pl.ds(c + 1, L, stride=FWD), :] = grad[:, L:].T
        rows = jnp.concatenate(blocks[side * 28 : side * 28 + 28], axis=0)
        ref[pl.ds(4, L, stride=FWD), :] = column_of(rows)


def compose_kernel(share_ref, keep_ref, give_ref, out_ref):
    for c in range(5):
        spot = pl.ds(c, L, stride=FWD)
        rows = keep_ref[spot, :] + give_ref[spot, :]
        if c == 4:
            small = jnp.sum(share_ref[pl.ds(2, L, stride=GAT), :], axis=0, keepdims=True)
            rows = rows + pltpu.roll(jnp.broadcast_to(small, (L, L)), 32, 1)
        out_ref[pl.ds(c, L, stride=RET), :] = rows
    for c in range(2):
        total = jnp.sum(share_ref[pl.ds(c, L, stride=GAT), :], axis=0, keepdims=True)
        out_ref[pl.ds(5 + c, L, stride=RET), :] = jnp.broadcast_to(total, (L, L))


def place_kernel(par_ref, idx_ref, own_ref, feat_ref, prm_ref, hot_ref):
    gauss = feat_ref.shape[0]
    first = par_ref[0] == 0
    idx = idx_ref[...]
    top, bottom = idx[0:4], idx[4:8]
    sub = lax.broadcasted_iota(jnp.int32, (gauss, L), 0)
    other = jnp.where(first, bottom, top)
    for c in range(4):
        hot_ref[:, c * L : c * L + L] = ones_where(other[c : c + 1] == sub).astype(BF16)
    mine = jnp.where(first, top, bottom)
    hots = [ones_where(mine[c : c + 1] == sub).astype(BF16) for c in range(4)]
    feat_ref[...] = place_features(own_ref, jnp.concatenate(hots, axis=1))
    prm_ref[...] = place_params(own_ref, mine, gauss // L)


def place_features(ref, onehot):
    grads = [
        jnp.concatenate(split2(ref[pl.ds(c, L, stride=RET), :]), axis=1) for c in range(4)
    ]
    both = nn(onehot, jnp.concatenate(grads, axis=0))
    return both[:, :L] + both[:, L:]


def place_params(ref, idx, groups):
    low_iota = lax.broadcasted_iota(jnp.int32, (L, L), 0)
    prm = ref[pl.ds(4, L, stride=RET), :].T
    params = jnp.zeros((2 * groups * 8, L), F32)
    for c in range(4):
        row = idx[c : c + 1]
        block = prm[c * 8 : c * 8 + 8]
        spread = jnp.concatenate(
            [jnp.where((row >> 7) == g, block, 0.0) for g in range(groups)], axis=0
        )
        both = jnp.concatenate(split2(spread), axis=0)
        hot = ones_where((row & (L - 1)) == low_iota).astype(BF16)
        params = params + nt(both, hot)
    return params[: groups * 8] + params[groups * 8 :]


def final_kernel(
    pixels,
    par_ref,
    idx_ref,
    own_ref,
    peer_ref,
    part_feat_ref,
    part_prm_ref,
    hot_ref,
    feat_ref,
    prm_ref,
    weight_ref,
    bias_ref,
    loss_ref,
):
    first = par_ref[0] == 0
    feat_ref[...] = part_feat_ref[...] + place_features(peer_ref, hot_ref[...])
    groups = feat_ref.shape[0] // L
    idx = idx_ref[...]
    other = jnp.where(first, idx[4:8], idx[0:4])
    params = part_prm_ref[...] + place_params(peer_ref, other, groups)
    for g in range(groups):
        prm_ref[:, g * L : g * L + L] = params[g * 8 : g * 8 + 6]

    width = weight_ref.shape[1]
    half = width // 2
    scale = 1.0 / pixels
    for ref, left in ((own_ref, first), (peer_ref, jnp.logical_not(first))):
        small = ref[pl.ds(4, L, stride=RET), :].T
        wide = [ref[pl.ds(5 + c, L, stride=RET), :] * scale for c in range(2)]
        row = jnp.concatenate([small[32:33], small[33:34]], axis=1) * scale
        wide = jnp.concatenate(wide, axis=1)

        def store(at):
            weight_ref[:, at : at + half] = wide
            bias_ref[:, at : at + half] = row

        pl.when(left)(functools.partial(store, 0))
        pl.when(jnp.logical_not(left))(functools.partial(store, half))
    loss_ref[...] = small[34:35, :] * (scale / width)


def call(kernel, shapes, specs, scratch=(), flops=0, limit=40):
    single = not isinstance(shapes, (list, tuple))
    count = 1 if single else len(shapes)
    cost = pl.CostEstimate(flops=flops, bytes_accessed=flops // 300, transcendentals=0)
    return pl.pallas_call(
        kernel,
        out_shape=shapes,
        in_specs=specs,
        out_specs=VMEM if single else [VMEM] * count,
        scratch_shapes=list(scratch),
        compiler_params=pltpu.CompilerParams(vmem_limit_bytes=limit * 1024 * 1024),
        cost_estimate=cost,
    )


def f32(*shape):
    return jax.ShapeDtypeStruct(shape, F32)


def bf16(*shape):
    return jax.ShapeDtypeStruct(shape, BF16)


def pack(par, send, features, gauss_params):
    shapes = [f32(FWD * L, L), jax.ShapeDtypeStruct((8, L), jnp.int32)]
    inputs = (send, features, gauss_params)
    scratch = [pltpu.VMEM(x.shape, x.dtype) for x in inputs]
    scratch.append(pltpu.SemaphoreType.DMA((3,)))
    return call(pack_kernel, shapes, [SMEM, HBM, HBM, HBM], scratch, flops=2 * 10**9, limit=62)(par, *inputs)


def keys(par, tile_lists, weight):
    shapes = [f32(8, L), bf16(*weight.shape), bf16(*weight.shape)]
    return call(key_kernel, shapes, [SMEM, VMEM, VMEM], flops=2 * 10**9)(par, tile_lists, weight)


def ready(par, ids, own, keyrow, length):
    pool = 8 * L
    return call(
        functools.partial(ready_kernel, float(length)),
        [bf16(pool, pool), f32(L, pool // 2), bf16(2 * L, pool // 2)],
        [SMEM, SMEM, VMEM, VMEM],
        [pltpu.VMEM((64, L), F32)],
        flops=10**9,
    )(par, ids, own, keyrow)


def front(par, ids, own, peer, keyrow, halves, teacher, whigh, wlow, bias, length):
    pixels, width = teacher.shape
    pool = 8 * L
    scratch = [
        pltpu.VMEM((64, L), F32),
        pltpu.VMEM((pool, 2 * L), BF16),
        pltpu.VMEM((L, pool), F32),
        pltpu.VMEM((2 * L, pool), BF16),
        pltpu.VMEM((pixels, pool), BF16),
        pltpu.VMEM((pixels, pool), BF16),
        pltpu.VMEM((2 * L, pixels), BF16),
    ]
    return call(
        functools.partial(front_kernel, float(length)),
        [f32(GAT * L, L), f32(GAT * L, L), f32(L, pool), bf16(pixels, width), bf16(pixels, width)],
        [SMEM, SMEM] + [VMEM] * 10,
        scratch,
        flops=10**10,
    )(par, ids, own, peer, keyrow, *halves, teacher, whigh, wlow, bias)


def pixel(resid_hi, resid_lo, whigh, wlow):
    shape = f32(resid_hi.shape[0], whigh.shape[0])
    return call(pixel_kernel, shape, [VMEM] * 4, flops=10**9)(resid_hi, resid_lo, whigh, wlow)


def back(par, ids, own, peer, keyrow, trans, grad, length):
    pool = 8 * L
    pixels = grad.shape[0]
    scratch = [
        pltpu.VMEM((pool, pool), BF16),
        pltpu.VMEM((64, L), F32),
        pltpu.VMEM((pool, 2 * L), BF16),
        pltpu.VMEM((pool, 2 * L), BF16),
        pltpu.VMEM((L, pool), F32),
        pltpu.VMEM((L, pool), F32),
        pltpu.VMEM((2 * L, pool), BF16),
        pltpu.VMEM((pixels, pool), BF16),
        pltpu.VMEM((pixels, pool), BF16),
        pltpu.VMEM((2 * L, pixels), BF16),
        pltpu.VMEM((L, pool), F32),
    ]
    return call(
        functools.partial(back_kernel, float(length)),
        [f32(FWD * L, L), f32(FWD * L, L)],
        [SMEM, SMEM] + [VMEM] * 5,
        scratch,
        flops=8 * 10**9,
    )(par, ids, own, peer, keyrow, trans, grad)


def compose(share, keep, give):
    return call(compose_kernel, f32(RET * L, L), [VMEM] * 3, flops=10**9)(share, keep, give)


def place(par, idx, own, gauss):
    return call(
        place_kernel,
        [f32(gauss, L), f32(gauss // L * 8, L), bf16(gauss, 4 * L)],
        [SMEM, VMEM, VMEM],
        flops=10**9,
    )(par, idx, own)


def final(par, idx, own, peer, parts, width, pixels):
    gauss = parts[0].shape[0]
    return call(
        functools.partial(final_kernel, float(pixels)),
        [f32(gauss, L), f32(6, gauss), f32(L, width), f32(1, width), f32(1, L)],
        [SMEM] + [VMEM] * 6,
        flops=2 * 10**9,
    )(par, idx, own, peer, *parts)


def swap(value):
    return lax.ppermute(value, "px", SWAP)


def exchange(value, rows):
    sent = value.reshape(L, 1, rows * L)
    return lax.all_to_all(sent, "gs", split_axis=0, concat_axis=0, tiled=True).reshape(rows * L, L)


def per_device(
    features, gauss_params, send_index, tile_ids, tile_lists, teacher, decoder_weight, decoder_bias
):
    holders = lax.axis_size("gs")
    par = lax.axis_index("px").astype(jnp.int32).reshape(1)
    width = teacher.shape[2]
    sent, idx = pack(par, send_index.reshape(8, -1), features, gauss_params)
    sent, tile_lists, decoder_weight, teacher = lax.optimization_barrier(
        (sent, tile_lists, decoder_weight, teacher)
    )
    got = exchange(sent, FWD)
    prepared = keys(par, tile_lists, decoder_weight)
    got, (keyrow, whigh, wlow) = lax.optimization_barrier((got, prepared))
    peer = swap(got)
    length = tile_lists.shape[1]
    halves = ready(par, tile_ids, got, keyrow, length)
    flat_teacher = teacher.reshape(-1, width)
    bias = decoder_bias.reshape(1, -1)
    keep, give, trans, resid_hi, resid_lo = front(
        par, tile_ids, got, peer, keyrow, halves, flat_teacher, whigh, wlow, bias, length
    )
    given = swap(give)
    grad = pixel(resid_hi, resid_lo, whigh, wlow)
    part, trans, grad = lax.optimization_barrier((keep + given, trans, grad))
    share = exchange(part, GAT)
    keep, give = back(par, tile_ids, got, peer, keyrow, trans, grad, length)
    ret = exchange(compose(share, keep, swap(give)), RET)
    other = swap(ret)
    parts = place(par, idx, ret, features.shape[0])
    pixels = holders * tile_ids.shape[0] * 256
    grad_features, grad_params, grad_weight, grad_bias, loss = final(
        par, idx, ret, other, parts, width, pixels
    )
    return grad_features, grad_params, grad_weight, grad_bias.reshape(-1), loss[0, 0]


def solution(mesh):
    return jax.shard_map(
        per_device,
        mesh=mesh,
        in_specs=(
            P("gs", None),
            P(None, "gs"),
            P("gs"),
            P("gs"),
            P("gs", None),
            P("gs", "px", None),
            P(),
            P(),
        ),
        out_specs=(P("gs", None), P(None, "gs"), P(), P(), P()),
        check_vma=False,
    )
```

```python
import functools

import jax
import jax.numpy as jnp
from jax import lax
from jax.experimental import pallas as pl
from jax.experimental.pallas import tpu as pltpu
from jax.sharding import PartitionSpec as P

F32 = jnp.float32
BF16 = jnp.bfloat16
L = 128
SWAP = [(0, 1), (1, 0)]
FWD = 5
RET = 7
GAT = 3
VMEM = pl.BlockSpec(memory_space=pltpu.VMEM)
SMEM = pl.BlockSpec(memory_space=pltpu.SMEM)
HBM = pl.BlockSpec(memory_space=pltpu.HBM)


def nn(lhs, rhs):
    return lax.dot_general(lhs, rhs, (((1,), (0,)), ((), ())), preferred_element_type=F32)


def nt(lhs, rhs):
    return lax.dot_general(lhs, rhs, (((1,), (1,)), ((), ())), preferred_element_type=F32)


def split2(value):
    high = value.astype(BF16)
    return high, (value - high.astype(F32)).astype(BF16)


def split3(value):
    high = value.astype(BF16)
    rest = value - high.astype(F32)
    mid = rest.astype(BF16)
    return high, mid, (rest - mid.astype(F32)).astype(BF16)


def ones_where(mask):
    return jnp.where(mask, 1.0, 0.0).astype(F32)


def column_of(rows):
    pad = jnp.zeros((L - rows.shape[0], L), F32)
    return jnp.concatenate([rows, pad], axis=0).T


def slot_rows(raw):
    slot = lax.broadcasted_iota(jnp.int32, (8, L), 1) & 7
    mine = slot == lax.broadcasted_iota(jnp.int32, (8, L), 0)
    spread = []
    for r in range(8):
        row = raw[r : r + 1, :]
        high = jnp.where(mine, row >> 4, 0).astype(F32)
        low = jnp.where(mine, row & 15, 0).astype(F32)
        spread.append(jnp.concatenate([high, low], axis=0).astype(BF16))
    source = lax.broadcasted_iota(jnp.int32, (8 * L, L), 0) >> 3
    owner = lax.broadcasted_iota(jnp.int32, (8 * L, L), 1)
    got = nn(jnp.concatenate(spread, axis=1), ones_where(source == owner).astype(BF16))
    return (got[:8] * 16.0 + got[8:]).astype(jnp.int32)


def pack_kernel(par_ref, send_hbm, feat_hbm, prm_hbm, out_ref, idx_ref, send_ref, feat_ref, prm_ref, sems):
    copies = [
        pltpu.make_async_copy(src, dst, sems.at[n])
        for n, (src, dst) in enumerate(
            ((send_hbm, send_ref), (feat_hbm, feat_ref), (prm_hbm, prm_ref))
        )
    ]
    for copy in copies:
        copy.start()
    gauss = feat_ref.shape[0]
    copies[0].wait()
    first = par_ref[0] == 0
    idx = slot_rows(send_ref[...])
    idx_ref[...] = idx
    rows = jnp.where(first, idx[0:4, :], idx[4:8, :])
    cols = column_of(rows.astype(F32))
    lane = lax.broadcasted_iota(jnp.int32, (L, gauss), 1).astype(F32)
    hots = [ones_where(cols[:, c : c + 1] == lane).astype(BF16) for c in range(4)]
    copies[2].wait()
    copies[1].wait()
    got = nn(
        jnp.concatenate(hots, axis=0), jnp.concatenate(split2(feat_ref[...]), axis=1)
    )
    groups = gauss // L
    pieces = [prm_ref[:, g * L : (g + 1) * L] for g in range(groups)]
    pad = jnp.zeros((2, L), F32)
    stacked = jnp.concatenate([x for piece in pieces for x in (piece, pad)], axis=0)
    stack3 = jnp.concatenate(split3(stacked), axis=0)
    low_iota = lax.broadcasted_iota(jnp.int32, (L, L), 0)
    packed = []
    for c in range(4):
        part = got[c * L : c * L + L]
        out_ref[pl.ds(c, L, stride=FWD), :] = part[:, :L] + part[:, L:]
        row = rows[c : c + 1, :]
        low = ones_where((row & (L - 1)) == low_iota).astype(BF16)
        part = nn(stack3, low)
        span = groups * 8
        part = part[:span] + part[span : 2 * span] + part[2 * span :]
        total = jnp.zeros((8, L), F32)
        for g in range(groups):
            total = total + jnp.where((row >> 7) == g, part[g * 8 : g * 8 + 8], 0.0)
        packed.append(total)
    out_ref[pl.ds(4, L, stride=FWD), :] = column_of(jnp.concatenate(packed, axis=0))


def key_kernel(par_ref, lists_ref, weight_ref, row_ref, high_ref, low_ref):
    high_ref[...], low_ref[...] = split2(weight_ref[...])
    shift = par_ref[0] * 4
    tiles, length = lists_ref.shape
    slot_iota = lax.broadcasted_iota(jnp.int32, (8, length), 0)
    holder_iota = lax.broadcasted_iota(jnp.int32, (L, length), 0)
    place = lax.broadcasted_iota(jnp.int32, (8, length), 1)
    place_high = (place >> 4).astype(F32)
    place_low = (place & 15).astype(F32)
    total = jnp.zeros((32, L), F32)
    for t in range(tiles):
        entry = lists_ref[t : t + 1, :]
        holder = ones_where((entry >> 3) == holder_iota).astype(BF16)
        slot = ones_where(((entry + shift) & 7) == slot_iota)
        left = jnp.concatenate(
            [slot * (t + 1.0), slot * place_high, slot * place_low, jnp.zeros((8, length), F32)],
            axis=0,
        ).astype(BF16)
        total = total + nt(left, holder)
    tile = total[0:8]
    key = jnp.where(tile > 0.5, (tile - 1.0) * length + total[8:16] * 16.0 + total[16:24], -1.0)
    row_ref[...] = key


class Pool:

    def __init__(self, length, par_ref, ids_ref, keyrow_ref, prm_ref, sides):
        self.length, self.prm_ref = length, prm_ref
        stripe = par_ref[0]
        self.key = keyrow_ref[...]
        live = self.key >= 0.0
        self.tile = jnp.floor(self.key * (1.0 / length))
        self.ox = jnp.zeros((8, L), F32)
        self.oy = jnp.zeros((8, L), F32)
        for t in range(8):
            ident = ids_ref[t]
            here = self.tile == float(t)
            self.ox = jnp.where(here, ((ident & 127) * 16).astype(F32) + 0.5, self.ox)
            self.oy = jnp.where(
                here, ((ident >> 7) * 16 + stripe * 8).astype(F32) + 0.5, self.oy
            )
        self.base = jnp.where(live, self.tile * length, 1.0e9)
        self.kx = lax.broadcasted_iota(jnp.int32, (16, L), 0).astype(F32)
        self.ky = lax.broadcasted_iota(jnp.int32, (8, L), 0).astype(F32)
        for side, ref in sides:
            prm_ref[side * 32 : side * 32 + 32, :] = ref[pl.ds(4, L, stride=FWD), :].T[0:32]

    def geometry(self, b):
        prm = self.prm_ref[b * 8 : b * 8 + 8, :]
        dx = (self.kx + self.ox[b : b + 1, :]) - prm[0:1]
        dy = (self.ky + self.oy[b : b + 1, :]) - prm[1:2]
        return prm, dx, dy

    def alphas(self, b):
        prm, dx, dy = self.geometry(b)
        ax = prm[2:3] * dx * dx
        cy = prm[4:5] * dy * dy
        bx = prm[3:4] * dx
        live = self.key[b : b + 1, :] >= 0.0
        for j in range(8):
            power = -0.5 * (ax + cy[j : j + 1]) - bx * dy[j : j + 1]
            ex = jnp.where(live, jnp.exp(power), 0.0)
            yield slice(j * 16, j * 16 + 16), ex, prm[5:6] * ex

    def fill_mask(self, mask_ref):
        cols = column_of(self.key)
        one, zero = jnp.ones((8, 16, L), BF16), jnp.zeros((8, 16, L), BF16)

        def short(rows, shape):
            return jnp.broadcast_to(rows, shape).astype(jnp.int32).astype(jnp.int16)

        base = jnp.minimum(self.base, 30000.0)
        ends = [short(self.key[b : b + 1, :], (16, L))[None] for b in range(8)]
        starts = [short(base[b : b + 1, :], (16, L))[None] for b in range(8)]
        for a in range(8):
            front = short(cols[:, a : a + 1], (L, L)).reshape(8, 16, L)
            for b in range(8):
                hit = (front < ends[b]) & (front >= starts[b])
                got = jnp.where(hit, one, zero).reshape(L, L)
                mask_ref[a * L : a * L + L, b * L : b * L + L] = got

    def spread(self, b, weights, high_ref, low_ref):
        cols = slice(b * L, b * L + L)
        high, low = (x.reshape(8, 16, L) for x in split2(weights))
        for t in range(8):
            here = ones_where(self.tile[b : b + 1, :] == float(t))
            here = jnp.broadcast_to(here, (16, L)).astype(BF16)[None]
            high_ref[t * L : t * L + L, cols] = (high * here).reshape(L, L)
            low_ref[t * L : t * L + L, cols] = (low * here).reshape(L, L)


def fill_features(own_ref, peer_ref, feat_ref):
    for side, ref in ((0, own_ref), (1, peer_ref)):
        for c in range(4):
            at = (side * 4 + c) * L
            high, low = split2(ref[pl.ds(c, L, stride=FWD), :])
            feat_ref[at : at + L, 0:L] = high
            feat_ref[at : at + L, L : 2 * L] = low


def fill_logs(pool, b, alpha_ref, lk_ref):
    cols = slice(b * L, b * L + L)
    for spot, ex, alpha in pool.alphas(b):
        high, low = split2(jnp.log1p(-alpha))
        alpha_ref[spot, cols] = alpha
        lk_ref[spot, cols] = high
        lk_ref[L + spot.start : L + spot.stop, cols] = low


def ready_kernel(
    length, par_ref, ids_ref, own_ref, keyrow_ref, mask_ref, alpha_ref, lk_ref, prm_ref
):
    pool = Pool(length, par_ref, ids_ref, keyrow_ref, prm_ref, ((0, own_ref),))
    pool.fill_mask(mask_ref)
    for b in range(4):
        fill_logs(pool, b, alpha_ref, lk_ref)


def front_kernel(
    length,
    par_ref,
    ids_ref,
    own_ref,
    peer_ref,
    keyrow_ref,
    mask_ref,
    half_alpha_ref,
    half_lk_ref,
    teacher_ref,
    whigh_ref,
    wlow_ref,
    bias_ref,
    keep_ref,
    give_ref,
    trans_ref,
    resid_hi,
    resid_lo,
    prm_ref,
    feat_ref,
    alpha_ref,
    lk_ref,
    wm_hi,
    wm_lo,
    rt_ref,
):
    pool = Pool(
        length, par_ref, ids_ref, keyrow_ref, prm_ref, ((0, own_ref), (1, peer_ref))
    )
    fill_features(own_ref, peer_ref, feat_ref)
    half = 4 * L
    alpha_ref[:, 0:half] = half_alpha_ref[...]
    lk_ref[:, 0:half] = half_lk_ref[...]
    for b in range(4, 8):
        fill_logs(pool, b, alpha_ref, lk_ref)

    for b in range(0, 8, 2):
        both = nn(lk_ref[...], mask_ref[:, b * L : b * L + 2 * L])
        trans = jnp.exp(both[:L] + both[L:])
        trans_ref[:, b * L : b * L + 2 * L] = trans
        for q in range(2):
            cols = slice((b + q) * L, (b + q) * L + L)
            weights = trans[:, q * L : q * L + L] * alpha_ref[:, cols]
            pool.spread(b + q, weights, wm_hi, wm_lo)

    w_hi, w_lo = whigh_ref[...], wlow_ref[...]
    w_pair = jnp.concatenate([w_hi, w_hi], axis=0)
    width = whigh_ref.shape[1]
    squares = jnp.zeros((1, width), F32)
    bias_sum = jnp.zeros((1, width), F32)
    step = 8 * L
    for r in range(1):
        rows = slice(r * step, r * step + step)
        both = nn(wm_hi[rows, :], feat_ref[...])
        rendered = both[:, :L] + both[:, L:] + nn(wm_lo[rows, :], feat_ref[:, 0:L])
        high, low = split2(rendered)
        rt_hi, rt_lo = split2(rendered.T)
        rt_ref[0:L, rows] = rt_hi
        rt_ref[L : 2 * L, rows] = rt_lo
        decoded = nn(jnp.concatenate([high, low], axis=1), w_pair) + nn(high, w_lo)
        resid = decoded + bias_ref[...] - teacher_ref[rows, :]
        squares = squares + jnp.sum(resid * resid, axis=0, keepdims=True)
        bias_sum = bias_sum + jnp.sum(resid, axis=0, keepdims=True)
        high, low = split2(resid)
        resid_hi[rows, :] = high
        resid_lo[rows, :] = low

    both = nn(rt_ref[...], resid_hi[...])
    grad_w = both[:L] + both[L:] + nn(rt_ref[0:L, :], resid_lo[...])
    sq_row = jnp.broadcast_to(jnp.sum(squares, axis=1, keepdims=True), (1, L))
    first = par_ref[0] == 0
    half = width // 2
    for ref, left in ((keep_ref, first), (give_ref, jnp.logical_not(first))):
        piece = jnp.where(left, grad_w[:, :half], grad_w[:, half:])
        ref[pl.ds(0, L, stride=GAT), :] = piece[:, :L]
        ref[pl.ds(1, L, stride=GAT), :] = piece[:, L:]
        piece = jnp.where(left, bias_sum[:, :half], bias_sum[:, half:])
        rows = jnp.concatenate([piece[:, :L], piece[:, L:], sq_row], axis=0)
        ref[pl.ds(2, L, stride=GAT), :] = column_of(rows)


def pixel_kernel(resid_hi, resid_lo, whigh_ref, wlow_ref, grad_ref):
    w_hi = whigh_ref[...]
    w_both = jnp.concatenate([w_hi, wlow_ref[...]], axis=0)
    step = 2 * L
    for r in range(4):
        rows = slice(r * step, r * step + step)
        both = nt(resid_hi[rows, :], w_both)
        grad_ref[rows, :] = both[:, :L] + both[:, L:] + nt(resid_lo[rows, :], w_hi)


def back_kernel(
    length,
    par_ref,
    ids_ref,
    own_ref,
    peer_ref,
    keyrow_ref,
    trans_ref,
    grad_ref,
    keep_ref,
    give_ref,
    mask_ref,
    prm_ref,
    feat_ref,
    feat2_ref,
    ex_ref,
    alpha_ref,
    lk_ref,
    wm_hi,
    wm_lo,
    drt_ref,
    dw_ref,
):
    pool = Pool(
        length, par_ref, ids_ref, keyrow_ref, prm_ref, ((0, own_ref), (1, peer_ref))
    )
    fill_features(own_ref, peer_ref, feat_ref)
    feat2_ref[:, 0:L] = feat_ref[:, 0:L]
    feat2_ref[:, L : 2 * L] = feat_ref[:, 0:L]
    pool.fill_mask(mask_ref)
    for b in range(8):
        cols = slice(b * L, b * L + L)
        for spot, ex, alpha in pool.alphas(b):
            ex_ref[spot, cols] = ex
            alpha_ref[spot, cols] = alpha
        pool.spread(b, trans_ref[:, cols] * alpha_ref[:, cols], wm_hi, wm_lo)

    dw_ref[...] = jnp.zeros(dw_ref.shape, F32)
    step = 2 * L
    span = 4
    for r in range(8 // span):
        rows = slice(r * span * L, (r + 1) * span * L)
        grad = grad_ref[rows, :]
        high, low = split2(grad)
        pair = jnp.concatenate([high, low], axis=1)
        dt_hi, dt_lo = split2(grad.T)
        drt_ref[0:L, rows] = dt_hi
        drt_ref[L : 2 * L, rows] = dt_lo
        for b in range(0, 8, 2):
            entries = slice(b * L, b * L + step)
            part = nt(pair, feat2_ref[entries, :]) + nt(high, feat_ref[entries, L : 2 * L])
            for q in range(2):
                cols = slice((b + q) * L, (b + q) * L + L)
                tile = pool.tile[b + q : b + q + 1, :]
                kept = dw_ref[:, cols]
                for t in range(span):
                    got = part[t * L : t * L + L, q * L : q * L + L]
                    kept = jnp.where(tile == float(r * span + t), got, kept)
                dw_ref[:, cols] = kept

    for b in range(8):
        cols = slice(b * L, b * L + L)
        high, low = split2(dw_ref[:, cols] * (trans_ref[:, cols] * alpha_ref[:, cols]))
        lk_ref[0:L, cols] = high
        lk_ref[L : 2 * L, cols] = low

    def total(value):
        return jnp.sum(value, axis=0, keepdims=True)

    blocks = []
    for b in range(0, 8, 2):
        wide = slice(b * L, b * L + step)
        both = nt(lk_ref[...], mask_ref[wide, :])
        alpha = alpha_ref[:, wide]
        dalpha = dw_ref[:, wide] * trans_ref[:, wide] - (both[:L] + both[L:]) / (1.0 - alpha)
        dpower = dalpha * alpha
        dopac = total(dalpha * ex_ref[:, wide])
        for q in range(2):
            prm, dx, dy = pool.geometry(b + q)
            flat = jnp.zeros((16, L), F32)
            by_y = jnp.zeros((16, L), F32)
            by_yy = jnp.zeros((16, L), F32)
            for j in range(8):
                part = dpower[j * 16 : j * 16 + 16, q * L : q * L + L]
                scaled = part * dy[j : j + 1]
                flat = flat + part
                by_y = by_y + scaled
                by_yy = by_yy + scaled * dy[j : j + 1]
            sx = total(flat * dx)
            sxx = total(flat * dx * dx)
            sy = total(by_y)
            sxy = total(by_y * dx)
            syy = total(by_yy)
            blocks += [
                prm[2:3] * sx + prm[3:4] * sy,
                prm[4:5] * sy + prm[3:4] * sx,
                -0.5 * sxx,
                -sxy,
                -0.5 * syy,
                dopac[:, q * L : q * L + L],
                jnp.zeros((2, L), F32),
            ]

    for side, ref in ((0, keep_ref), (1, give_ref)):
        for c in range(0, 4, 2):
            wide = slice((side * 4 + c) * L, (side * 4 + c) * L + step)
            both = nn(drt_ref[...], wm_hi[:, wide])
            grad = both[:L] + both[L:] + nn(drt_ref[0:L, :], wm_lo[:, wide])
            ref[pl.ds(c, L, stride=FWD), :] = grad[:, :L].T
            ref[pl.ds(c + 1, L, stride=FWD), :] = grad[:, L:].T
        rows = jnp.concatenate(blocks[side * 28 : side * 28 + 28], axis=0)
        ref[pl.ds(4, L, stride=FWD), :] = column_of(rows)


def compose_kernel(share_ref, keep_ref, give_ref, out_ref):
    for c in range(5):
        spot = pl.ds(c, L, stride=FWD)
        rows = keep_ref[spot, :] + give_ref[spot, :]
        if c == 4:
            small = jnp.sum(share_ref[pl.ds(2, L, stride=GAT), :], axis=0, keepdims=True)
            rows = rows + pltpu.roll(jnp.broadcast_to(small, (L, L)), 32, 1)
        out_ref[pl.ds(c, L, stride=RET), :] = rows
    for c in range(2):
        total = jnp.sum(share_ref[pl.ds(c, L, stride=GAT), :], axis=0, keepdims=True)
        out_ref[pl.ds(5 + c, L, stride=RET), :] = jnp.broadcast_to(total, (L, L))


def place_kernel(par_ref, idx_ref, own_ref, feat_ref, prm_ref, hot_ref):
    gauss = feat_ref.shape[0]
    first = par_ref[0] == 0
    idx = idx_ref[...]
    top, bottom = idx[0:4], idx[4:8]
    sub = lax.broadcasted_iota(jnp.int32, (gauss, L), 0)
    other = jnp.where(first, bottom, top)
    for c in range(4):
        hot_ref[:, c * L : c * L + L] = ones_where(other[c : c + 1] == sub).astype(BF16)
    mine = jnp.where(first, top, bottom)
    hots = [ones_where(mine[c : c + 1] == sub).astype(BF16) for c in range(4)]
    feat_ref[...] = place_features(own_ref, jnp.concatenate(hots, axis=1))
    prm_ref[...] = place_params(own_ref, mine, gauss // L)


def place_features(ref, onehot):
    grads = [
        jnp.concatenate(split2(ref[pl.ds(c, L, stride=RET), :]), axis=1) for c in range(4)
    ]
    both = nn(onehot, jnp.concatenate(grads, axis=0))
    return both[:, :L] + both[:, L:]


def place_params(ref, idx, groups):
    low_iota = lax.broadcasted_iota(jnp.int32, (L, L), 0)
    prm = ref[pl.ds(4, L, stride=RET), :].T
    params = jnp.zeros((2 * groups * 8, L), F32)
    for c in range(4):
        row = idx[c : c + 1]
        block = prm[c * 8 : c * 8 + 8]
        spread = jnp.concatenate(
            [jnp.where((row >> 7) == g, block, 0.0) for g in range(groups)], axis=0
        )
        both = jnp.concatenate(split2(spread), axis=0)
        hot = ones_where((row & (L - 1)) == low_iota).astype(BF16)
        params = params + nt(both, hot)
    return params[: groups * 8] + params[groups * 8 :]


def final_kernel(
    pixels,
    par_ref,
    idx_ref,
    own_ref,
    peer_ref,
    part_feat_ref,
    part_prm_ref,
    hot_ref,
    feat_ref,
    prm_ref,
    weight_ref,
    bias_ref,
    loss_ref,
):
    first = par_ref[0] == 0
    feat_ref[...] = part_feat_ref[...] + place_features(peer_ref, hot_ref[...])
    groups = feat_ref.shape[0] // L
    idx = idx_ref[...]
    other = jnp.where(first, idx[4:8], idx[0:4])
    params = part_prm_ref[...] + place_params(peer_ref, other, groups)
    for g in range(groups):
        prm_ref[:, g * L : g * L + L] = params[g * 8 : g * 8 + 6]

    width = weight_ref.shape[1]
    half = width // 2
    scale = 1.0 / pixels
    for ref, left in ((own_ref, first), (peer_ref, jnp.logical_not(first))):
        small = ref[pl.ds(4, L, stride=RET), :].T
        wide = [ref[pl.ds(5 + c, L, stride=RET), :] * scale for c in range(2)]
        row = jnp.concatenate([small[32:33], small[33:34]], axis=1) * scale
        wide = jnp.concatenate(wide, axis=1)

        def store(at):
            weight_ref[:, at : at + half] = wide
            bias_ref[:, at : at + half] = row

        pl.when(left)(functools.partial(store, 0))
        pl.when(jnp.logical_not(left))(functools.partial(store, half))
    loss_ref[...] = small[34:35, :] * (scale / width)


def call(kernel, shapes, specs, scratch=(), flops=0, limit=40):
    single = not isinstance(shapes, (list, tuple))
    count = 1 if single else len(shapes)
    cost = pl.CostEstimate(flops=flops, bytes_accessed=flops // 300, transcendentals=0)
    return pl.pallas_call(
        kernel,
        out_shape=shapes,
        in_specs=specs,
        out_specs=VMEM if single else [VMEM] * count,
        scratch_shapes=list(scratch),
        compiler_params=pltpu.CompilerParams(vmem_limit_bytes=limit * 1024 * 1024),
        cost_estimate=cost,
    )


def f32(*shape):
    return jax.ShapeDtypeStruct(shape, F32)


def bf16(*shape):
    return jax.ShapeDtypeStruct(shape, BF16)


def pack(par, send, features, gauss_params):
    shapes = [f32(FWD * L, L), jax.ShapeDtypeStruct((8, L), jnp.int32)]
    inputs = (send, features, gauss_params)
    scratch = [pltpu.VMEM(x.shape, x.dtype) for x in inputs]
    scratch.append(pltpu.SemaphoreType.DMA((3,)))
    return call(pack_kernel, shapes, [SMEM, HBM, HBM, HBM], scratch, flops=2 * 10**9, limit=62)(par, *inputs)


def keys(par, tile_lists, weight):
    shapes = [f32(8, L), bf16(*weight.shape), bf16(*weight.shape)]
    return call(key_kernel, shapes, [SMEM, VMEM, VMEM], flops=2 * 10**9)(par, tile_lists, weight)


def ready(par, ids, own, keyrow, length):
    pool = 8 * L
    return call(
        functools.partial(ready_kernel, float(length)),
        [bf16(pool, pool), f32(L, pool // 2), bf16(2 * L, pool // 2)],
        [SMEM, SMEM, VMEM, VMEM],
        [pltpu.VMEM((64, L), F32)],
        flops=10**9,
    )(par, ids, own, keyrow)


def front(par, ids, own, peer, keyrow, halves, teacher, whigh, wlow, bias, length):
    pixels, width = teacher.shape
    pool = 8 * L
    scratch = [
        pltpu.VMEM((64, L), F32),
        pltpu.VMEM((pool, 2 * L), BF16),
        pltpu.VMEM((L, pool), F32),
        pltpu.VMEM((2 * L, pool), BF16),
        pltpu.VMEM((pixels, pool), BF16),
        pltpu.VMEM((pixels, pool), BF16),
        pltpu.VMEM((2 * L, pixels), BF16),
    ]
    return call(
        functools.partial(front_kernel, float(length)),
        [f32(GAT * L, L), f32(GAT * L, L), f32(L, pool), bf16(pixels, width), bf16(pixels, width)],
        [SMEM, SMEM] + [VMEM] * 10,
        scratch,
        flops=10**10,
    )(par, ids, own, peer, keyrow, *halves, teacher, whigh, wlow, bias)


def pixel(resid_hi, resid_lo, whigh, wlow):
    shape = f32(resid_hi.shape[0], whigh.shape[0])
    return call(pixel_kernel, shape, [VMEM] * 4, flops=10**9)(resid_hi, resid_lo, whigh, wlow)


def back(par, ids, own, peer, keyrow, trans, grad, length):
    pool = 8 * L
    pixels = grad.shape[0]
    scratch = [
        pltpu.VMEM((pool, pool), BF16),
        pltpu.VMEM((64, L), F32),
        pltpu.VMEM((pool, 2 * L), BF16),
        pltpu.VMEM((pool, 2 * L), BF16),
        pltpu.VMEM((L, pool), F32),
        pltpu.VMEM((L, pool), F32),
        pltpu.VMEM((2 * L, pool), BF16),
        pltpu.VMEM((pixels, pool), BF16),
        pltpu.VMEM((pixels, pool), BF16),
        pltpu.VMEM((2 * L, pixels), BF16),
        pltpu.VMEM((L, pool), F32),
    ]
    return call(
        functools.partial(back_kernel, float(length)),
        [f32(FWD * L, L), f32(FWD * L, L)],
        [SMEM, SMEM] + [VMEM] * 5,
        scratch,
        flops=8 * 10**9,
    )(par, ids, own, peer, keyrow, trans, grad)


def compose(share, keep, give):
    return call(compose_kernel, f32(RET * L, L), [VMEM] * 3, flops=10**9)(share, keep, give)


def place(par, idx, own, gauss):
    return call(
        place_kernel,
        [f32(gauss, L), f32(gauss // L * 8, L), bf16(gauss, 4 * L)],
        [SMEM, VMEM, VMEM],
        flops=10**9,
    )(par, idx, own)


def final(par, idx, own, peer, parts, width, pixels):
    gauss = parts[0].shape[0]
    return call(
        functools.partial(final_kernel, float(pixels)),
        [f32(gauss, L), f32(6, gauss), f32(L, width), f32(1, width), f32(1, L)],
        [SMEM] + [VMEM] * 6,
        flops=2 * 10**9,
    )(par, idx, own, peer, *parts)


def swap(value):
    return lax.ppermute(value, "px", SWAP)


def exchange(value, rows):
    sent = value.reshape(L, 1, rows * L)
    return lax.all_to_all(sent, "gs", split_axis=0, concat_axis=0, tiled=True).reshape(rows * L, L)


def per_device(
    features, gauss_params, send_index, tile_ids, tile_lists, teacher, decoder_weight, decoder_bias
):
    holders = lax.axis_size("gs")
    par = lax.axis_index("px").astype(jnp.int32).reshape(1)
    width = teacher.shape[2]
    sent, idx = pack(par, send_index.reshape(8, -1), features, gauss_params)
    sent, tile_lists, decoder_weight, teacher = lax.optimization_barrier(
        (sent, tile_lists, decoder_weight, teacher)
    )
    got = exchange(sent, FWD)
    prepared = keys(par, tile_lists, decoder_weight)
    got, (keyrow, whigh, wlow) = lax.optimization_barrier((got, prepared))
    peer = swap(got)
    length = tile_lists.shape[1]
    halves = ready(par, tile_ids, got, keyrow, length)
    flat_teacher = teacher.reshape(-1, width)
    bias = decoder_bias.reshape(1, -1)
    keep, give, trans, resid_hi, resid_lo = front(
        par, tile_ids, got, peer, keyrow, halves, flat_teacher, whigh, wlow, bias, length
    )
    given = swap(give)
    grad = pixel(resid_hi, resid_lo, whigh, wlow)
    part, trans, grad = lax.optimization_barrier((keep + given, trans, grad))
    share = exchange(part, GAT)
    keep, give = back(par, tile_ids, got, peer, keyrow, trans, grad, length)
    ret = exchange(compose(share, keep, swap(give)), RET)
    other = swap(ret)
    parts = place(par, idx, ret, features.shape[0])
    pixels = holders * tile_ids.shape[0] * 256
    grad_features, grad_params, grad_weight, grad_bias, loss = final(
        par, idx, ret, other, parts, width, pixels
    )
    return grad_features, grad_params, grad_weight, grad_bias.reshape(-1), loss[0, 0]


def solution(mesh):
    return jax.shard_map(
        per_device,
        mesh=mesh,
        in_specs=(
            P("gs", None),
            P(None, "gs"),
            P("gs"),
            P("gs"),
            P("gs", None),
            P("gs", "px", None),
            P(),
            P(),
        ),
        out_specs=(P("gs", None), P(None, "gs"), P(), P(), P()),
        check_vma=False,
    )
```
